32 devices in a mesh: replica: 16 (over z, y, core), tensor: 2 (over x).
Axes of the slice: x: 2, y: 2, z: 4, core: 2. Of those that a mesh axis runs over, the one named last changes fastest.
Arguments:
- prompt_rows: bfloat16 [2048, 2048], P('replica', 'tensor'), may hold values from -6 to 6
- request_rows: bfloat16 [2048, 2048], P('replica', 'tensor'), may hold values from -6 to 6
- request_keyval_cache: bfloat16 [2048, 64, 512], P('replica', None, 'tensor'), may hold values from -9 to 9
- cache_len: int32 [2048], P('replica'), may hold values from 1 to 64, as said below
- destination: int32 [2048, 1], P('replica'), may hold values from 0 to 15; in each aligned block of 128 rows (0 to 127, 128 to 255, ...) at most 16 rows name the same one
- prefix_cache: bfloat16 [32768, 512], P('replica', 'tensor'), as said below
- attn_gain: float32 [2048], replicated, may hold values from 0.1 to 1.9
- w_query: bfloat16 [2048, 1024], P(None, 'tensor'), may hold values from -0.125 to 0.125
- keyval_weight: bfloat16 [2048, 512], P(None, 'tensor'), may hold values from -0.125 to 0.125
- w_out: bfloat16 [1024, 2048], P('tensor'), may hold values from -0.75 to 0.75
- mlp_gain: float32 [2048], replicated, may hold values from 0.1 to 1.9
- w_gate: bfloat16 [2048, 2560], P(None, 'tensor'), may hold values from -0.125 to 0.125
- w_up: bfloat16 [2048, 2560], P(None, 'tensor'), may hold values from -0.125 to 0.125
- w_down: bfloat16 [2560, 2048], P('tensor'), may hold values from -0.125 to 0.125
Outputs:
- prompt_out: bfloat16 [2048, 2048], P('replica', 'tensor')
- request_out: bfloat16 [2048, 2048], P('replica', 'tensor')
The draws below stay inside these ranges and needn't reach their ends.
Inputs may be any that keep to these rules, and one draw needn't show every extreme that they name: `cache_len`: the first of each replica's 128 requests has exactly 64 cached tokens. `destination`: among the 128 requests of one replica no replica is named more than 16 times, and in every draw some replica is named exactly 16 times by some replica. `prefix_cache`: keys and values of each replica's shared prefix.
All inputs are finite; a program needn't handle non-finite values.
Results may differ from the reference program's by a relative error of at most 0.019.
The reference program's roundings to bfloat16 on the way count: a program that leaves them out, or rounds other values in their place, can miss the bound.
Values may be sent and summed in bfloat16 or wider, within the bound.
No kernel may reach another device: no remote copies, remote signals or barrier semaphores. Data moves between devices by JAX's collectives and lax.ppermute only.
A program may use at most 128 MiB of HBM per device.

```python
import math
import jax
import jax.numpy as jnp
import numpy as np
from jax import lax

MODEL_WIDTH = 2048
HQ = 16
KEY_VALUE_HEADS = 4
HEAD_SIZE = 64
FF = 2560
PT = 128
MIG = 128
MAX_CACHED = 64
PFX = 2048
CAP = 16
PROMPTS = 2048
DECODE_REQUESTS = 2048
PREFIX_ROWS = 32768
N_REPLICA = 16
N_TENSOR = 2


def draw_cache_len(key, part):
    lengths = jax.random.randint(key, (DECODE_REQUESTS,), 1, MAX_CACHED + 1)
    leading = jnp.arange(DECODE_REQUESTS) % MIG == 0
    return jnp.where(leading, MAX_CACHED, lengths).astype(jnp.int32)


def draw_prefix_cache(key, part):
    column_list = KEY_VALUE_HEADS * 2 * HEAD_SIZE
    base = jax.random.normal(key, (PREFIX_ROWS, column_list), jnp.float32)
    return base.astype(jnp.bfloat16)


def level_of(key, dims, pieces, least, high):
    factor_of = 1.0
    for dim, blocks in pieces:
        steps = jax.random.uniform(jax.random.fold_in(jax.random.fold_in(key, 6), dim), (blocks,), jnp.float32, least / len(pieces), high / len(pieces))
        factor_of = factor_of * jnp.repeat(jnp.exp(steps), dims[dim] // blocks).reshape((-1,) + (1,) * (len(dims) - 1 - dim))
    return factor_of


def deal_out(rng, own, number, rows, number_of, top, reach, skew):
    sequence = jax.random.permutation(rng, number_of)
    heavy_load, ordinary = portions_of(number_of, rows * top, reach, skew, True), portions_of(number_of, rows * top, reach, skew, False)
    places = jnp.arange(number_of)

    def named(tallies, rotation):
        used = int((tallies > 0).sum())
        fixed = max(1, used // 4)
        shifted = fixed + (places - fixed + rotation * (used - fixed)) % max(1, number_of - fixed)
        return jnp.zeros((number_of,), jnp.int32).at[sequence[jnp.where(places < fixed, places, shifted)]].set(jnp.asarray(tallies, jnp.int32))

    tallies = jnp.where(number % 4 == 0, named(heavy_load, number // 4), named(ordinary, number - number // 4 - 1))
    mixed = jax.random.permutation(jax.random.fold_in(own, 3), number_of)
    giver, taker = mixed[0:number_of // 2 * 2:2], mixed[1:number_of // 2 * 2:2]
    room = jnp.minimum(tallies[giver] - 1, reach - tallies[taker]) // 2
    room = jnp.where((giver == sequence[0]) | (taker == sequence[0]) | (tallies[taker] == 0), 0, jnp.maximum(room, 0))
    shifted = jax.random.randint(jax.random.fold_in(own, 4), (number_of // 2,), 0, 1 << 20) % (room + 1)
    tallies = tallies.at[giver].add(-shifted).at[taker].add(shifted)
    members = jnp.searchsorted(jnp.cumsum(tallies), jnp.arange(rows * top), side="right").astype(jnp.int32)
    listing = members.reshape(top, rows).T
    listing = listing[jax.random.permutation(jax.random.fold_in(own, 1), rows)]
    rotation = jax.random.randint(jax.random.fold_in(own, 2), (rows, 1), 0, top)
    return jnp.take_along_axis(listing, (jnp.arange(top)[None, :] + rotation) % top, axis=1)


def portions_of(amount, total, limit, lean, full):
    portions = [(1 << 20) // math.isqrt(grade ** lean) + 1 for grade in range(1, amount + 1)]
    largest = limit if full else min(limit, max(-(-total // amount), total * portions[0] // sum(portions)))
    least = 1 if total - largest >= amount - 1 else 0
    counts, surplus = [largest] + [least] * (amount - 1), total - largest - least * (amount - 1)
    while surplus > 0:
        candidates = [i for i in range(1, amount) if counts[i] < largest] or [i for i in range(1, amount) if counts[i] < limit]
        pool, remaining = sum([portions[i] for i in candidates]), surplus
        for i in candidates:
            addition = min(limit - counts[i], max(1, remaining * portions[i] // pool), surplus)
            counts[i] = counts[i] + addition
            surplus = surplus - addition
    return np.array(counts)


def centred(own_key, extent, scale, limit, split=(), held_as=jnp.bfloat16):
    entries = scale * jax.random.normal(own_key, extent, jnp.float32)
    if split:
        entries = entries * level_of(own_key, extent, split, -0.22, 0.18)
    return jnp.clip(entries, -limit, limit).astype(held_as)


def setup_inputs(seed: int = 0) -> dict:
    splits = jax.random.split(jax.random.key(seed), 15)
    prompt_rows = centred(splits[0], (PROMPTS, MODEL_WIDTH), 1.0, 6.0, ((0, 16), (1, 2)))
    request_rows = centred(splits[1], (DECODE_REQUESTS, MODEL_WIDTH), 1.0, 6.0, ((0, 16), (1, 2)))
    request_keyval_cache = centred(splits[2], (DECODE_REQUESTS, MAX_CACHED, KEY_VALUE_HEADS * 2 * HEAD_SIZE), 1.5, 9.0, ((0, 16), (2, 2)))
    cache_len = draw_cache_len(jax.random.fold_in(splits[14], 71), 0)
    destination_keys = jax.random.split(jax.random.fold_in(splits[4], 1), DECODE_REQUESTS // MIG)
    destination_turns = jax.random.permutation(jax.random.fold_in(splits[4], 3), DECODE_REQUESTS // MIG)
    destination = jax.vmap(lambda own, number: deal_out(jax.random.fold_in(splits[4], 2), own, number, MIG, N_REPLICA, 1, CAP, 2))(destination_keys, destination_turns).reshape((DECODE_REQUESTS, 1))
    prefix_cache = draw_prefix_cache(jax.random.fold_in(splits[14], 71), 0)
    attn_gain = jnp.clip(1.0 + 0.18 * jax.random.normal(splits[6], (MODEL_WIDTH,), jnp.float32), 0.1, 1.9)
    w_query = centred(splits[7], (MODEL_WIDTH, HQ * HEAD_SIZE), MODEL_WIDTH ** -0.5, 0.125, ((1, 2),))
    keyval_weight = centred(splits[8], (MODEL_WIDTH, KEY_VALUE_HEADS * 2 * HEAD_SIZE), MODEL_WIDTH ** -0.5, 0.125, ((1, 2),))
    w_out = centred(splits[9], (HQ * HEAD_SIZE, MODEL_WIDTH), HEAD_SIZE ** -0.5, 0.75, ((0, 2),))
    mlp_gain = jnp.clip(1.0 + 0.18 * jax.random.normal(splits[10], (MODEL_WIDTH,), jnp.float32), 0.1, 1.9)
    w_gate = centred(splits[11], (MODEL_WIDTH, FF), MODEL_WIDTH ** -0.5, 0.125, ((1, 2),))
    w_up = centred(splits[12], (MODEL_WIDTH, FF), MODEL_WIDTH ** -0.5, 0.125, ((1, 2),))
    w_down = centred(splits[13], (FF, MODEL_WIDTH), FF ** -0.5, 0.125, ((0, 2),))
    return dict(prompt_rows=prompt_rows, request_rows=request_rows, request_keyval_cache=request_keyval_cache, cache_len=cache_len, destination=destination, prefix_cache=prefix_cache, attn_gain=attn_gain, w_query=w_query, keyval_weight=keyval_weight, w_out=w_out, mlp_gain=mlp_gain, w_gate=w_gate, w_up=w_up, w_down=w_down)


EPS = 1e-05

def rms_norm(row_vals, gain_vec):
    values = row_vals.astype(jnp.float32)
    inv_scale = lax.rsqrt(lax.optimization_barrier(jnp.mean(values * values, axis=-1, keepdims=True)) + EPS)
    return (values * inv_scale * gain_vec.astype(jnp.float32)).astype(jnp.bfloat16)

def split_sum(left_rows, right_rows, groups):
    width = left_rows.shape[1] // groups
    summed = jnp.zeros((left_rows.shape[0], right_rows.shape[1]), jnp.float32)
    for group in range(groups):
        product = jnp.dot(left_rows[:, group * width:(group + 1) * width], right_rows[group * width:(group + 1) * width], preferred_element_type=jnp.float32).astype(jnp.bfloat16)
        summed = summed + lax.optimization_barrier(product).astype(jnp.float32)
    return summed

def attend(queries, keyval, visible):
    queries = lax.optimization_barrier(queries)
    keyval = lax.optimization_barrier(keyval)
    row_count = queries.shape[0]
    kv_heads = keyval.shape[1] // (2 * HEAD_SIZE)
    grouped = queries.astype(jnp.float32).reshape(row_count, kv_heads, -1, HEAD_SIZE)
    key_rows = keyval.astype(jnp.float32).reshape(-1, kv_heads, 2, HEAD_SIZE)
    scores = jnp.einsum('rkgd,skd->rkgs', grouped, key_rows[:, :, 0]) * HEAD_SIZE ** (-0.5)
    scores = jnp.where(visible[:, None, None, :], scores, -jnp.inf)
    row_max = lax.optimization_barrier(jnp.max(scores, axis=3, keepdims=True))
    exp_vals = jnp.exp(scores - row_max)
    weights = (exp_vals / lax.optimization_barrier(jnp.sum(exp_vals, axis=3, keepdims=True))).astype(jnp.bfloat16)
    weights = lax.optimization_barrier(weights).astype(jnp.float32)
    mixed_out = jnp.einsum('rkgs,skd->rkgd', weights, key_rows[:, :, 1])
    return mixed_out.reshape(row_count, -1).astype(jnp.bfloat16)

def reference(prompt_rows, request_rows, request_keyval_cache, cache_len, destination, prefix_cache, attn_gain, w_query, keyval_weight, w_out, mlp_gain, w_gate, w_up, w_down):

    def project(row_block):
        normed = rms_norm(row_block, attn_gain)
        queries = jnp.dot(normed, w_query, preferred_element_type=jnp.float32).astype(jnp.bfloat16)
        keyval = jnp.dot(normed, keyval_weight, preferred_element_type=jnp.float32).astype(jnp.bfloat16)
        return (queries, keyval)

    def finish(row_block, attended):
        residual = (row_block.astype(jnp.float32) + split_sum(attended, w_out, N_TENSOR)).astype(jnp.bfloat16)
        normed = rms_norm(residual, mlp_gain)
        gate_act = jnp.dot(normed, w_gate, preferred_element_type=jnp.float32)
        up_act = jnp.dot(normed, w_up, preferred_element_type=jnp.float32)
        hidden = (jax.nn.silu(gate_act) * up_act).astype(jnp.bfloat16)
        return (residual.astype(jnp.float32) + split_sum(hidden, w_down, N_TENSOR)).astype(jnp.bfloat16)
    prefixes = prefix_cache.reshape(N_REPLICA, PFX, -1)
    prompt_q, prompt_kv = project(prompt_rows)
    row_ids = jnp.arange(PT, dtype=jnp.int32)[:, None]
    col_ids = jnp.arange(PFX + PT, dtype=jnp.int32)[None, :]
    prompt_visible = (col_ids < PFX) | (col_ids - PFX <= row_ids)

    def one_prompt(operands):
        query_block, kv_block, prefix_block = operands
        return attend(query_block, jnp.concatenate((prefix_block, kv_block), axis=0), prompt_visible)
    prompt_att = lax.map(one_prompt, (prompt_q.reshape(N_REPLICA, PT, -1), prompt_kv.reshape(N_REPLICA, PT, -1), prefixes))
    prompt_out = finish(prompt_rows, prompt_att.reshape(PROMPTS, -1))
    request_q, request_kv = project(request_rows)
    targets = destination[:, 0].astype(jnp.int32)

    def one_request(operands):
        query_row, kv_row, cache_rows, length, target = operands
        prefix_block = lax.dynamic_index_in_dim(prefixes, target, 0, keepdims=False)
        key_rows = jnp.concatenate((prefix_block, cache_rows, kv_row[None, :]), axis=0)
        visible = jnp.concatenate((jnp.ones((PFX,), bool), jnp.arange(MAX_CACHED, dtype=jnp.int32) < length, jnp.ones((1,), bool)))
        return attend(query_row[None, :], key_rows, visible[None, :])[0]
    request_att = lax.map(one_request, (request_q, request_kv, request_keyval_cache, cache_len.astype(jnp.int32), targets))
    request_out = finish(request_rows, request_att)
    return (prompt_out, request_out)
```

```python
import functools
import math

import jax
import jax.numpy as jnp
from jax import lax
from jax.experimental import pallas as pl
from jax.experimental.pallas import tpu as pltpu
from jax.sharding import PartitionSpec as P

HEAD_SIZE = 64
QUERIES_PER_KEY = 4
PAIR = 2 * HEAD_SIZE
GROUP = 16
EPS = 1e-05
FACTOR = HEAD_SIZE ** (-0.5) * math.log2(math.e)
F32 = jnp.float32
BF16 = jnp.bfloat16
VMEM_BYTES = 48 * 1024 * 1024
WHOLE = pl.BlockSpec(memory_space=pltpu.VMEM)
SCALAR = pl.BlockSpec(memory_space=pltpu.SMEM)


def params():
    return pltpu.CompilerParams(vmem_limit_bytes=VMEM_BYTES)


def cost(flops, read, exps=0):
    return pl.CostEstimate(flops=int(flops), bytes_accessed=int(read), transcendentals=int(exps))


def lane_ids(shape):
    return lax.broadcasted_iota(jnp.int32, shape, len(shape) - 1)


def rms_norm(values, gain_row):
    inv_scale = lax.rsqrt(jnp.mean(values * values, axis=1, keepdims=True) + EPS)
    return (values * inv_scale * gain_row).astype(BF16)


def in_order(place_ref, parts):
    if len(parts) == 2:
        first = place_ref[0] == 0
        own, other = parts
        parts = (jnp.where(first, own, other), jnp.where(first, other, own))
    return jnp.concatenate(parts, axis=1)


def head_query(queries, head):
    pair = head // 2
    block = queries[:, pair * PAIR : (pair + 1) * PAIR].astype(F32)
    if head % 2:
        block = pltpu.roll(block, HEAD_SIZE, 1)
    return jnp.where(lane_ids(block.shape) < HEAD_SIZE, block, 0.0).astype(BF16)


def ones_for_keys(keyval):
    key_half = lane_ids(keyval.shape) % PAIR < HEAD_SIZE
    return jnp.where(key_half, 1.0, keyval.astype(F32)).astype(BF16)


def scores_of(query_rows, key_rows):
    return lax.dot_general(
        query_rows, key_rows, (((1,), (1,)), ((), ())), preferred_element_type=F32
    )


def pack_pair(even, odd):
    even = even / pltpu.roll(even, HEAD_SIZE, 1)
    odd = odd / pltpu.roll(odd, HEAD_SIZE, 1)
    return jnp.where(
        lane_ids(even.shape) < HEAD_SIZE, pltpu.roll(even, HEAD_SIZE, 1), odd
    )


def project(rows, gain_ref, w_query_ref, keyval_weight_ref):
    normed = rms_norm(rows.astype(F32), gain_ref[...])
    queries = jnp.dot(normed, w_query_ref[...], preferred_element_type=F32).astype(BF16)
    keyval = jnp.dot(normed, keyval_weight_ref[...], preferred_element_type=F32).astype(BF16)
    return queries, keyval


def request_project_kernel(count, place_ref, *refs):
    parts, refs = refs[:count], refs[count:]
    gain_ref, w_query_ref, keyval_weight_ref, spread_ref, q_ref, kv_ref, send_ref = refs
    rows = in_order(place_ref, [ref[...] for ref in parts])
    queries, keyval = project(rows, gain_ref, w_query_ref, keyval_weight_ref)
    q_ref[...] = queries
    kv_ref[...] = keyval
    send_ref[...] = jnp.dot(spread_ref[...], queries, preferred_element_type=F32).astype(BF16)


def prompt_kernel(count, place_ref, *refs):
    parts, refs = refs[:count], refs[count:]
    gain_ref, w_query_ref, keyval_weight_ref, prefix_ref, w_out_ref, mixed_ref, q_scr, kvx_scr, att_scr = refs
    rows = in_order(place_ref, [ref[...] for ref in parts])
    queries, keyval = project(rows, gain_ref, w_query_ref, keyval_weight_ref)
    heads = queries.shape[1] // HEAD_SIZE
    row_count = queries.shape[0]
    for head in range(heads):
        q_scr[head] = head_query(queries, head)
    kvx_scr[...] = ones_for_keys(prefix_ref[...])
    own_ones = ones_for_keys(keyval)
    row_ids = lax.broadcasted_iota(jnp.int32, (2 * row_count, row_count), 0) % row_count
    visible = lax.broadcasted_iota(jnp.int32, (2 * row_count, row_count), 1) <= row_ids
    for kv in range(heads // QUERIES_PER_KEY):
        columns = slice(kv * PAIR, (kv + 1) * PAIR)
        own_keys = keyval[:, columns]
        own_values = own_ones[:, columns]
        for half in range(QUERIES_PER_KEY // 2):
            pair = kv * (QUERIES_PER_KEY // 2) + half
            query_rows = q_scr[pl.ds(2 * pair, 2)].reshape(2 * row_count, PAIR)
            past = scores_of(query_rows, prefix_ref[:, columns])
            own = jnp.where(visible, scores_of(query_rows, own_keys), -jnp.inf)
            row_max = jnp.maximum(
                jnp.max(past, axis=1, keepdims=True), jnp.max(own, axis=1, keepdims=True)
            )
            past_exp = jnp.exp2((past - row_max) * FACTOR).astype(BF16)
            own_exp = jnp.exp2((own - row_max) * FACTOR).astype(BF16)
            total = jnp.dot(past_exp, kvx_scr[:, columns], preferred_element_type=F32)
            total = total + jnp.dot(own_exp, own_values, preferred_element_type=F32)
            att_scr[:, pair * PAIR : (pair + 1) * PAIR] = pack_pair(
                total[:row_count], total[row_count:]
            ).astype(BF16)
    mixed_ref[...] = jnp.dot(
        att_scr[...], w_out_ref[...], preferred_element_type=F32
    ).astype(BF16)


def slot_kernel(q_ref, prefix_ref, out_ref, q_scr, kvx_scr):
    slots, width = q_ref.shape
    heads = width // HEAD_SIZE
    queries = q_ref[...]
    for head in range(heads):
        q_scr[head] = head_query(queries, head)
    kvx_scr[...] = ones_for_keys(prefix_ref[...])
    lanes = lane_ids((slots, PAIR))
    sums = jnp.zeros((slots, PAIR), F32)
    for kv in range(heads // QUERIES_PER_KEY):
        columns = slice(kv * PAIR, (kv + 1) * PAIR)
        for half in range(QUERIES_PER_KEY // 2):
            pair = kv * (QUERIES_PER_KEY // 2) + half
            totals = []
            for head in (2 * pair, 2 * pair + 1):
                scores = scores_of(q_scr[head], prefix_ref[:, columns])
                row_max = jnp.max(scores, axis=1, keepdims=True)
                exp_vals = jnp.exp2((scores - row_max) * FACTOR).astype(BF16)
                total = jnp.dot(exp_vals, kvx_scr[:, columns], preferred_element_type=F32)
                totals.append(total)
                log_sum = row_max * FACTOR + jnp.log2(total)
                high = log_sum.astype(BF16).astype(F32)
                middle = (log_sum - high).astype(BF16).astype(F32)
                low = log_sum - high - middle
                for place, part in enumerate((high, middle, low)):
                    sums = jnp.where(lanes == 3 * head + place, part, sums)
            out_ref[:, pair * PAIR : (pair + 1) * PAIR] = pack_pair(*totals).astype(BF16)
    out_ref[:, width:] = sums.astype(BF16)


def past_kernel(q_ref, kv_ref, len_ref, cache_ref, out_ref, sum_ref):
    group, width = q_ref.shape
    heads = width // HEAD_SIZE
    cached = cache_ref.shape[1]
    kv_width = kv_ref.shape[1]
    queries = q_ref[...]
    own = kv_ref[...].astype(F32)
    own_ones = jnp.where(lane_ids(own.shape) % PAIR < HEAD_SIZE, 1.0, own)
    keys = cache_ref[...].reshape(group * cached, kv_width)
    padded, own_scores = [], []
    for head in range(heads):
        kv = head // QUERIES_PER_KEY
        query = head_query(queries, head)
        blocks = [jnp.zeros_like(query)] * (kv_width // PAIR)
        blocks[kv] = query
        padded.append(jnp.concatenate(blocks, axis=1) if len(blocks) > 1 else query)
        own_scores.append(
            jnp.sum(query.astype(F32) * own[:, kv * PAIR : (kv + 1) * PAIR], axis=1, keepdims=True)
        )
    query_rows = jnp.concatenate(padded, axis=0)
    own_scores = jnp.concatenate(own_scores, axis=0)
    lengths = jnp.concatenate([len_ref[...]] * heads, axis=0)
    shape = (heads * group, group * cached)
    columns = lane_ids(shape)
    owner = lax.broadcasted_iota(jnp.int32, shape, 0) % group
    visible = (columns // cached == owner) & (columns % cached < lengths)
    scores = jnp.where(visible, scores_of(query_rows, keys), -jnp.inf)
    row_max = jnp.maximum(jnp.max(scores, axis=1, keepdims=True), own_scores)
    exp_vals = jnp.exp2((scores - row_max) * FACTOR).astype(BF16)
    own_exp = jnp.exp2((own_scores - row_max) * FACTOR).astype(BF16).astype(F32)
    totals = jnp.dot(exp_vals, ones_for_keys(keys), preferred_element_type=F32)
    lanes = lane_ids((group, PAIR))
    sums = jnp.zeros((group, PAIR), F32)
    done = []
    for head in range(heads):
        kv = head // QUERIES_PER_KEY
        at = slice(head * group, (head + 1) * group)
        block = slice(kv * PAIR, (kv + 1) * PAIR)
        total = totals[at, block] + own_exp[at] * own_ones[:, block]
        log_sum = row_max[at] * FACTOR + jnp.log2(total)
        sums = jnp.where(lanes == head, log_sum, sums)
        done.append(total)
    for pair in range(heads // 2):
        out_ref[:, pair * PAIR : (pair + 1) * PAIR] = pack_pair(done[2 * pair], done[2 * pair + 1])
    sum_ref[...] = sums


def merge_kernel(gather_ref, back_ref, past_ref, sum_ref, w_out_ref, mixed_ref):
    width = past_ref.shape[1]
    heads = width // HEAD_SIZE
    prefix = jnp.dot(gather_ref[...], back_ref[...], preferred_element_type=F32)
    prefix_sums = prefix[:, width:]
    past_sums = sum_ref[...]
    lanes = lane_ids(past_sums.shape)
    shares = []
    for head in range(heads):
        prefix_log = jnp.sum(
            jnp.where(lanes // 3 == head, prefix_sums, 0.0), axis=1, keepdims=True
        )
        past_log = jnp.sum(jnp.where(lanes == head, past_sums, 0.0), axis=1, keepdims=True)
        top = jnp.maximum(prefix_log, past_log)
        prefix_part = jnp.exp2(prefix_log - top)
        past_part = jnp.exp2(past_log - top)
        both = prefix_part + past_part
        shares.append((prefix_part / both, past_part / both))
    attended = []
    for pair in range(heads // 2):
        at = slice(pair * PAIR, (pair + 1) * PAIR)
        key_half = lanes < HEAD_SIZE
        prefix_share = jnp.where(key_half, shares[2 * pair][0], shares[2 * pair + 1][0])
        past_share = jnp.where(key_half, shares[2 * pair][1], shares[2 * pair + 1][1])
        attended.append((prefix_share * prefix[:, at] + past_share * past_ref[:, at]).astype(BF16))
    mixed_ref[...] = jnp.dot(
        jnp.concatenate(attended, axis=1), w_out_ref[...], preferred_element_type=F32
    ).astype(BF16)


def mlp_kernel(count, steps, place_ref, *refs):
    parts, refs = refs[:count], refs[count:]
    mixed, refs = refs[:count], refs[count:]
    gain_ref, w_gate_ref, w_up_ref, w_down_ref, *refs = refs
    *out_refs, normed_scr, total_scr = refs
    step = pl.program_id(0)
    total_width = total_scr.shape[1]
    width = total_width // count

    @pl.when(step == 0)
    def _():
        rows = in_order(place_ref, [ref[...] for ref in parts]).astype(F32)
        summed = mixed[0][...].astype(F32)
        for ref in mixed[1:]:
            summed = summed + ref[...].astype(F32)
        residual = (rows + summed).astype(BF16)
        normed_scr[...] = rms_norm(residual.astype(F32), gain_ref[...])
        if count == 2:
            first = place_ref[0] == 0
            out_refs[2][...] = jnp.where(first, residual[:, :width], residual[:, width:])
        else:
            out_refs[1][...] = residual

    normed = normed_scr[...]
    gate_act = jnp.dot(normed, w_gate_ref[...], preferred_element_type=F32)
    up_act = jnp.dot(normed, w_up_ref[...], preferred_element_type=F32)
    hidden = (gate_act / (1.0 + jnp.exp(-gate_act)) * up_act).astype(BF16)
    product = jnp.dot(hidden, w_down_ref[...], preferred_element_type=F32)

    @pl.when(step == 0)
    def _():
        total_scr[...] = product

    @pl.when(step > 0)
    def _():
        total_scr[...] += product

    @pl.when(step == steps - 1)
    def _():
        terms = total_scr[...].astype(BF16)
        if count == 2:
            first = place_ref[0] == 0
            out_refs[0][...] = jnp.where(first, terms[:, :width], terms[:, width:])
            out_refs[1][...] = jnp.where(first, terms[:, width:], terms[:, :width])
        else:
            out_refs[0][...] = terms


def swap(block, count):
    if count == 2:
        return [block, lax.ppermute(block, "tensor", [(0, 1), (1, 0)])]
    if count == 1:
        return [block]
    gathered = lax.all_gather(block, "tensor", axis=0, tiled=False)
    return [gathered[i] for i in range(count)]


def mlp(place, parts, mixed, gain, w_gate, w_up, w_down):
    count = len(parts)
    rows = parts[0].shape[0]
    model = sum(part.shape[1] for part in parts)
    hidden = w_gate.shape[1]
    steps = 5 if hidden % (5 * 128) == 0 else 1
    chunk = hidden // steps
    width = model // count
    if count == 2:
        outs = [jax.ShapeDtypeStruct((rows, width), BF16)] * 3
    else:
        outs = [jax.ShapeDtypeStruct((rows, model), BF16)] * 2
    return pl.pallas_call(
        functools.partial(mlp_kernel, count, steps),
        grid=(steps,),
        in_specs=[SCALAR]
        + [pl.BlockSpec((rows, width), lambda i: (0, 0))] * count
        + [pl.BlockSpec((rows, model), lambda i: (0, 0))] * count
        + [
            pl.BlockSpec((1, model), lambda i: (0, 0)),
            pl.BlockSpec((model, chunk), lambda i: (0, i)),
            pl.BlockSpec((model, chunk), lambda i: (0, i)),
            pl.BlockSpec((chunk, model), lambda i: (i, 0)),
        ],
        out_specs=[pl.BlockSpec(out.shape, lambda i: (0, 0)) for out in outs],
        out_shape=outs,
        scratch_shapes=[pltpu.VMEM((rows, model), BF16), pltpu.VMEM((rows, model), F32)],
        compiler_params=params(),
        cost_estimate=cost(6 * rows * model * hidden, 6 * model * hidden, rows * hidden),
        name="mlp",
    )(place, *parts, *mixed, gain, w_gate, w_up, w_down)


def finish(place, parts, mixed, layer_params):
    count = len(parts)
    mlp_gain, w_gate, w_up, w_down = layer_params
    outs = mlp(place, parts, mixed, mlp_gain, w_gate, w_up, w_down)
    if count == 2:
        keep, send, residual = outs
        other = lax.ppermute(send, "tensor", [(0, 1), (1, 0)])
        summed = keep.astype(F32) + other.astype(F32)
        return (residual.astype(F32) + summed).astype(BF16)
    terms, residual = outs
    width = terms.shape[1] // count
    summed = lax.psum_scatter(terms.astype(F32), "tensor", scatter_dimension=1, tiled=True)
    own = lax.dynamic_slice_in_dim(residual, lax.axis_index("tensor") * width, width, axis=1)
    return (own.astype(F32) + summed).astype(BF16)


def body(
    prompt_rows,
    request_rows,
    request_keyval_cache,
    cache_len,
    destination,
    prefix_cache,
    attn_gain,
    w_query,
    keyval_weight,
    w_out,
    mlp_gain,
    w_gate,
    w_up,
    w_down,
):
    count = lax.axis_size("tensor")
    replicas = lax.axis_size("replica")
    place = lax.axis_index("tensor").astype(jnp.int32).reshape(1)
    requests = request_rows.shape[0]
    prompts = prompt_rows.shape[0]
    model = w_query.shape[0]
    width = w_query.shape[1]
    kv_width = keyval_weight.shape[1]
    heads = width // HEAD_SIZE
    prefix_len = prefix_cache.shape[0]
    attn_gain = attn_gain.reshape(1, model)
    mlp_gain = mlp_gain.reshape(1, model)
    mlp_params = (mlp_gain, w_gate, w_up, w_down)

    request_parts = swap(request_rows, count)
    prompt_parts = swap(prompt_rows, count)

    per_peer = 2 * requests // replicas
    slots = replicas * per_peer
    target = destination[:, 0]
    earlier = lax.broadcasted_iota(jnp.int32, (requests, requests), 1) < lax.broadcasted_iota(
        jnp.int32, (requests, requests), 0
    )
    peer_rank = jnp.sum(((target[:, None] == target[None, :]) & earlier).astype(jnp.int32), axis=1)
    slot_place = target * per_peer + peer_rank
    gather = (
        lax.broadcasted_iota(jnp.int32, (requests, slots), 1) == slot_place[:, None]
    ).astype(BF16)
    spread = (
        lax.broadcasted_iota(jnp.int32, (slots, requests), 0) == slot_place[None, :]
    ).astype(BF16)

    queries, keyval, send = pl.pallas_call(
        functools.partial(request_project_kernel, count),
        in_specs=[SCALAR] + [WHOLE] * (count + 4),
        out_specs=[WHOLE] * 3,
        out_shape=[
            jax.ShapeDtypeStruct((requests, width), BF16),
            jax.ShapeDtypeStruct((requests, kv_width), BF16),
            jax.ShapeDtypeStruct((slots, width), BF16),
        ],
        compiler_params=params(),
        cost_estimate=cost(
            2 * requests * model * (width + kv_width), 2 * model * (width + kv_width)
        ),
        name="request_project",
    )(place, *request_parts, attn_gain, w_query, keyval_weight, spread)

    slot_queries = lax.all_to_all(send, "replica", split_axis=0, concat_axis=0, tiled=True)

    prompt_mixed = pl.pallas_call(
        functools.partial(prompt_kernel, count),
        in_specs=[SCALAR] + [WHOLE] * (count + 5),
        out_specs=WHOLE,
        out_shape=jax.ShapeDtypeStruct((prompts, model), BF16),
        scratch_shapes=[
            pltpu.VMEM((heads, prompts, PAIR), BF16),
            pltpu.VMEM((prefix_len, kv_width), BF16),
            pltpu.VMEM((prompts, width), BF16),
        ],
        compiler_params=params(),
        cost_estimate=cost(
            2 * prompts * model * (2 * width + kv_width) + 4 * prompts * heads * prefix_len * PAIR,
            2 * model * (2 * width + kv_width) + 2 * prefix_len * kv_width,
            prompts * heads * prefix_len,
        ),
        name="prompt_attention",
    )(place, *prompt_parts, attn_gain, w_query, keyval_weight, prefix_cache, w_out)

    cached = request_keyval_cache.shape[1]
    past, past_sums = pl.pallas_call(
        past_kernel,
        grid=(requests // GROUP,),
        in_specs=[
            pl.BlockSpec((GROUP, width), lambda i: (i, 0)),
            pl.BlockSpec((GROUP, kv_width), lambda i: (i, 0)),
            pl.BlockSpec((GROUP, 1), lambda i: (i, 0)),
            pl.BlockSpec((GROUP, cached, kv_width), lambda i: (i, 0, 0)),
        ],
        out_specs=[
            pl.BlockSpec((GROUP, width), lambda i: (i, 0)),
            pl.BlockSpec((GROUP, PAIR), lambda i: (i, 0)),
        ],
        out_shape=[
            jax.ShapeDtypeStruct((requests, width), F32),
            jax.ShapeDtypeStruct((requests, PAIR), F32),
        ],
        compiler_params=params(),
        cost_estimate=cost(
            4 * requests * heads * GROUP * cached * kv_width,
            2 * requests * cached * kv_width,
            requests * heads * GROUP * cached,
        ),
        name="past_attention",
    )(queries, keyval, cache_len.reshape(requests, 1), request_keyval_cache)

    slot_out = pl.pallas_call(
        slot_kernel,
        in_specs=[WHOLE] * 2,
        out_specs=WHOLE,
        out_shape=jax.ShapeDtypeStruct((slots, width + PAIR), BF16),
        scratch_shapes=[
            pltpu.VMEM((heads, slots, PAIR), BF16),
            pltpu.VMEM((prefix_len, kv_width), BF16),
        ],
        compiler_params=params(),
        cost_estimate=cost(
            4 * slots * heads * prefix_len * PAIR,
            2 * prefix_len * kv_width,
            slots * heads * prefix_len,
        ),
        name="slot_attention",
    )(slot_queries, prefix_cache)

    back = lax.all_to_all(slot_out, "replica", split_axis=0, concat_axis=0, tiled=True)

    prompt_out = finish(place, prompt_parts, swap(prompt_mixed, count), mlp_params)

    request_mixed = pl.pallas_call(
        merge_kernel,
        in_specs=[WHOLE] * 5,
        out_specs=WHOLE,
        out_shape=jax.ShapeDtypeStruct((requests, model), BF16),
        compiler_params=params(),
        cost_estimate=cost(2 * requests * width * model, 2 * width * model),
        name="merge",
    )(gather, back, past, past_sums, w_out)

    request_out = finish(place, request_parts, swap(request_mixed, count), mlp_params)
    return (prompt_out, request_out)


def solution(mesh):
    return jax.shard_map(
        body,
        mesh=mesh,
        in_specs=(
            P("replica", "tensor"),
            P("replica", "tensor"),
            P("replica", None, "tensor"),
            P("replica"),
            P("replica", None),
            P("replica", "tensor"),
            P(),
            P(None, "tensor"),
            P(None, "tensor"),
            P("tensor", None),
            P(),
            P(None, "tensor"),
            P(None, "tensor"),
            P("tensor", None),
        ),
        out_specs=(P("replica", "tensor"), P("replica", "tensor")),
        check_vma=False,
    )
```

```python
import functools
import math

import jax
import jax.numpy as jnp
from jax import lax
from jax.experimental import pallas as pl
from jax.experimental.pallas import tpu as pltpu
from jax.sharding import PartitionSpec as P

HEAD_SIZE = 64
QUERIES_PER_KEY = 4
PAIR = 2 * HEAD_SIZE
GROUP = 8
CHUNK = 256
EPS = 1e-05
FACTOR = HEAD_SIZE ** (-0.5) * math.log2(math.e)
F32 = jnp.float32
BF16 = jnp.bfloat16
MIB = 1024 * 1024
MOST_VMEM = 62 * MIB
ANY = pl.BlockSpec(memory_space=pl.ANY)
HBM = pl.BlockSpec(memory_space=pltpu.HBM)
SCALAR = pl.BlockSpec(memory_space=pltpu.SMEM)


def params(limit=MOST_VMEM):
    return pltpu.CompilerParams(vmem_limit_bytes=limit)


def cost(flops, read, exps=0):
    return pl.CostEstimate(flops=int(flops), bytes_accessed=int(read), transcendentals=int(exps))


def lane_ids(shape):
    return lax.broadcasted_iota(jnp.int32, shape, len(shape) - 1)


def rms_norm(values, gain_row):
    inv_scale = lax.rsqrt(jnp.mean(values * values, axis=1, keepdims=True) + EPS)
    return (values * inv_scale * gain_row).astype(BF16)


def in_order(place_ref, parts):
    if len(parts) == 2:
        first = place_ref[0] == 0
        own, other = parts
        parts = (jnp.where(first, own, other), jnp.where(first, other, own))
    return jnp.concatenate(parts, axis=1)


def column_of(row):
    shape = (row.shape[1], row.shape[1])
    rows = lax.broadcasted_iota(jnp.int32, shape, 0)
    return jnp.sum(
        jnp.where(rows == lane_ids(shape), jnp.broadcast_to(row, shape), 0), axis=1, keepdims=True
    )


def slot_places(target_row, per_peer):
    count = target_row.shape[1]
    target_column = column_of(target_row)
    shape = (count, count)
    rows, columns = lax.broadcasted_iota(jnp.int32, shape, 0), lane_ids(shape)
    same = (target_column == target_row).astype(jnp.int32)
    column = target_column * per_peer + jnp.sum(
        jnp.where(columns < rows, same, 0), axis=1, keepdims=True
    )
    row = target_row * per_peer + jnp.sum(
        jnp.where(rows < columns, same, 0), axis=0, keepdims=True
    )
    return column, row


def head_query(queries, head):
    pair = head // 2
    block = queries[:, pair * PAIR : (pair + 1) * PAIR].astype(F32)
    if head % 2:
        block = pltpu.roll(block, HEAD_SIZE, 1)
    return jnp.where(lane_ids(block.shape) < HEAD_SIZE, block, 0.0).astype(BF16)


def ones_for_keys(keyval):
    key_half = lane_ids(keyval.shape) % PAIR < HEAD_SIZE
    return jnp.where(key_half, 1.0, keyval.astype(F32)).astype(BF16)


def scores_of(query_rows, key_rows):
    return lax.dot_general(
        query_rows, key_rows, (((1,), (1,)), ((), ())), preferred_element_type=F32
    )


def pack_pair(even, odd):
    even = even / pltpu.roll(even, HEAD_SIZE, 1)
    odd = odd / pltpu.roll(odd, HEAD_SIZE, 1)
    return jnp.where(
        lane_ids(even.shape) < HEAD_SIZE, pltpu.roll(even, HEAD_SIZE, 1), odd
    )


class Copies:
    def __init__(self, sems):
        self.sems = sems
        self.used = 0
        self.flying = []

    def start(self, source, target):
        copy = pltpu.make_async_copy(source, target, self.sems.at[self.used])
        copy.start()
        self.used += 1
        self.flying.append(copy)
        return copy

    def wait(self):
        for copy in self.flying:
            copy.wait()
        self.flying = []


def fetch(refs, targets, sems):
    copies = Copies(sems)
    for ref, target in zip(refs, targets):
        copies.start(ref, target)
    started, copies.flying = copies.flying, []
    return copies, started


def scratch_like(*arrays):
    return [pltpu.VMEM(x.shape, x.dtype) for x in arrays]


def request_kernel(count, per_peer, place_ref, *refs):
    inputs = count + 6
    sources, (send_ref, past_ref, sum_ref), refs = refs[:inputs], refs[inputs : inputs + 3], refs[inputs + 3 :]
    held, (send_scr, past_scr, sum_scr), refs = refs[:inputs], refs[inputs : inputs + 3], refs[inputs + 3 :]
    q_scr, score_scr, weight_scr, mixed_scr, sems = refs
    copies, started = fetch(sources, held, sems)
    gain_ref, target_ref, w_query_ref, len_ref, keyval_weight_ref, cache_ref = held[count:]
    requests, cached, kv_width = cache_ref.shape
    groups = requests // GROUP
    keys = GROUP * cached
    for copy in started[: count + 2]:
        copy.wait()
    _, slot_row = slot_places(target_ref[...], per_peer)
    spread = lax.broadcasted_iota(jnp.int32, (send_scr.shape[0], requests), 0) == slot_row
    rows = in_order(place_ref, [ref[...] for ref in held[:count]])
    normed = rms_norm(rows.astype(F32), gain_ref[...])
    started[count + 2].wait()
    queries = jnp.dot(normed, w_query_ref[...], preferred_element_type=F32).astype(BF16)
    send_scr[...] = jnp.dot(
        spread.astype(BF16), queries, preferred_element_type=F32
    ).astype(BF16)
    copies.start(send_scr, send_ref)
    started[count + 3].wait()
    started[count + 4].wait()
    keyval = jnp.dot(normed, keyval_weight_ref[...], preferred_element_type=F32).astype(BF16)
    heads = queries.shape[1] // HEAD_SIZE
    block_rows = heads * GROUP
    q_scr[...] = jnp.zeros_like(q_scr)
    for head in range(heads):
        at = head // QUERIES_PER_KEY * PAIR
        q_scr[:, head * GROUP : (head + 1) * GROUP, at : at + PAIR] = (
            head_query(queries, head).astype(F32).reshape(groups, GROUP, PAIR)
        )
    own = jnp.broadcast_to(
        keyval.astype(F32).reshape(groups, 1, GROUP, kv_width), (groups, heads, GROUP, kv_width)
    ).reshape(groups * block_rows, kv_width)
    own_scores = jnp.sum(
        q_scr[...].reshape(groups * block_rows, kv_width) * own, axis=1, keepdims=True
    )
    owner = lax.broadcasted_iota(jnp.int32, (block_rows, keys), 0) % GROUP
    columns = lane_ids((block_rows, keys))
    position = jnp.where(columns // cached == owner, columns % cached, cached)
    lengths = column_of(len_ref[...])
    started[count + 5].wait()
    for group in range(groups):
        block = cache_ref[group * GROUP : (group + 1) * GROUP].reshape(keys, kv_width)
        live = position < jnp.concatenate(
            [lengths[group * GROUP : (group + 1) * GROUP]] * heads, axis=0
        )
        score_scr[group] = jnp.where(
            live, scores_of(q_scr[group].astype(BF16), block), -jnp.inf
        )
    scores = score_scr[...].reshape(groups * block_rows, keys)
    row_max = jnp.maximum(jnp.max(scores, axis=1, keepdims=True), own_scores)
    exp_vals = jnp.exp2((scores - row_max) * FACTOR)
    own_exp = jnp.exp2((own_scores - row_max) * FACTOR)
    weight_scr[...] = exp_vals.astype(BF16).reshape(groups, block_rows, keys)
    total = jnp.sum(exp_vals, axis=1, keepdims=True) + own_exp
    log_sum = (row_max * FACTOR + jnp.log2(total)).reshape(groups, block_rows, 1)
    for group in range(groups):
        block = cache_ref[group * GROUP : (group + 1) * GROUP].reshape(keys, kv_width)
        mixed_scr[group] = jnp.dot(weight_scr[group], block, preferred_element_type=F32)
    mixed = mixed_scr[...].reshape(groups * block_rows, kv_width)
    mixed = (mixed + own_exp.astype(BF16).astype(F32) * own) * (1.0 / total)
    mixed = mixed.reshape(groups, block_rows, kv_width)
    lanes = lane_ids((requests, PAIR))
    sums = jnp.zeros((requests, PAIR), F32)
    done = []
    for head in range(heads):
        at = head // QUERIES_PER_KEY * PAIR
        rows_of = slice(head * GROUP, (head + 1) * GROUP)
        done.append(mixed[:, rows_of, at : at + PAIR].reshape(requests, PAIR))
        sums = jnp.where(lanes == head, log_sum[:, rows_of].reshape(requests, 1), sums)
    for pair in range(heads // 2):
        past_scr[:, pair * PAIR : (pair + 1) * PAIR] = jnp.where(
            lanes < HEAD_SIZE, pltpu.roll(done[2 * pair], HEAD_SIZE, 1), done[2 * pair + 1]
        )
    sum_scr[...] = sums
    copies.start(past_scr, past_ref)
    copies.start(sum_scr, sum_ref)
    copies.wait()


def prompt_kernel(count, place_ref, *refs):
    inputs = count + 4
    sources, att_ref, refs = refs[:inputs], refs[inputs], refs[inputs + 1 :]
    held, (q_scr, kvx_scr, att_scr, sems) = refs[:inputs], refs[inputs:]
    copies, started = fetch(sources, held, sems)
    for copy in started[: count + 1]:
        copy.wait()
    gain_ref, w_query_ref, keyval_weight_ref, prefix_ref = held[count:]
    rows = in_order(place_ref, [ref[...] for ref in held[:count]])
    normed = rms_norm(rows.astype(F32), gain_ref[...])
    started[count + 1].wait()
    queries = jnp.dot(normed, w_query_ref[...], preferred_element_type=F32).astype(BF16)
    started[count + 2].wait()
    keyval = jnp.dot(normed, keyval_weight_ref[...], preferred_element_type=F32).astype(BF16)
    started[count + 3].wait()
    heads = queries.shape[1] // HEAD_SIZE
    row_count = queries.shape[0]
    for head in range(heads):
        q_scr[head] = head_query(queries, head)
    kvx_scr[...] = ones_for_keys(prefix_ref[...])
    own_ones = ones_for_keys(keyval)
    row_ids = lax.broadcasted_iota(jnp.int32, (2 * row_count, row_count), 0) % row_count
    visible = lax.broadcasted_iota(jnp.int32, (2 * row_count, row_count), 1) <= row_ids
    for kv in range(heads // QUERIES_PER_KEY):
        columns = slice(kv * PAIR, (kv + 1) * PAIR)
        own_keys = keyval[:, columns]
        own_values = own_ones[:, columns]
        for half in range(QUERIES_PER_KEY // 2):
            pair = kv * (QUERIES_PER_KEY // 2) + half
            query_rows = q_scr[pl.ds(2 * pair, 2)].reshape(2 * row_count, PAIR)
            past = scores_of(query_rows, prefix_ref[:, columns])
            own = jnp.where(visible, scores_of(query_rows, own_keys), -jnp.inf)
            row_max = jnp.maximum(
                jnp.max(past, axis=1, keepdims=True), jnp.max(own, axis=1, keepdims=True)
            )
            past_exp = jnp.exp2((past - row_max) * FACTOR).astype(BF16)
            own_exp = jnp.exp2((own - row_max) * FACTOR).astype(BF16)
            total = jnp.dot(past_exp, kvx_scr[:, columns], preferred_element_type=F32)
            total = total + jnp.dot(own_exp, own_values, preferred_element_type=F32)
            att_scr[:, pair * PAIR : (pair + 1) * PAIR] = pack_pair(
                total[:row_count], total[row_count:]
            ).astype(BF16)
    copies.start(att_scr, att_ref)
    copies.wait()


def slot_kernel(q_hbm, prefix_hbm, out_hbm, q_ref, prefix_ref, out_ref, q_scr, kvx_scr, sems):
    copies, started = fetch((q_hbm, prefix_hbm), (q_ref, prefix_ref), sems)
    started[0].wait()
    slots, width = q_ref.shape
    heads = width // HEAD_SIZE
    queries = q_ref[...]
    for head in range(heads):
        q_scr[head] = head_query(queries, head)
    started[1].wait()
    kvx_scr[...] = ones_for_keys(prefix_ref[...])
    lanes = lane_ids((slots, PAIR))
    sums = jnp.zeros((slots, PAIR), F32)
    for kv in range(heads // QUERIES_PER_KEY):
        columns = slice(kv * PAIR, (kv + 1) * PAIR)
        for half in range(QUERIES_PER_KEY // 2):
            pair = kv * (QUERIES_PER_KEY // 2) + half
            totals = []
            for head in (2 * pair, 2 * pair + 1):
                scores = scores_of(q_scr[head], prefix_ref[:, columns])
                row_max = jnp.max(scores, axis=1, keepdims=True)
                exp_vals = jnp.exp2((scores - row_max) * FACTOR).astype(BF16)
                total = jnp.dot(exp_vals, kvx_scr[:, columns], preferred_element_type=F32)
                totals.append(total)
                log_sum = row_max * FACTOR + jnp.log2(total)
                high = log_sum.astype(BF16).astype(F32)
                middle = (log_sum - high).astype(BF16).astype(F32)
                low = log_sum - high - middle
                for place, part in enumerate((high, middle, low)):
                    sums = jnp.where(lanes == 3 * head + place, part, sums)
            out_ref[:, pair * PAIR : (pair + 1) * PAIR] = pack_pair(*totals).astype(BF16)
    out_ref[:, width:] = sums.astype(BF16)
    copies.start(out_ref, out_hbm)
    copies.wait()


def merge_kernel(per_peer, *refs):
    sources, att_ref, held, (att_scr, sems) = refs[:4], refs[4], refs[5:9], refs[9:]
    copies, started = fetch(sources, held, sems)
    target_ref, back_ref, past_ref, sum_ref = held
    for copy in started:
        copy.wait()
    slot_column, _ = slot_places(target_ref[...], per_peer)
    gather = lane_ids((slot_column.shape[0], back_ref.shape[0])) == slot_column
    width = past_ref.shape[1]
    heads = width // HEAD_SIZE
    prefix = jnp.dot(gather.astype(BF16), back_ref[...], preferred_element_type=F32)
    prefix_sums = prefix[:, width:]
    past_sums = sum_ref[...]
    lanes = lane_ids(past_sums.shape)
    shares = []
    for head in range(heads):
        prefix_log = jnp.sum(
            jnp.where(lanes // 3 == head, prefix_sums, 0.0), axis=1, keepdims=True
        )
        past_log = jnp.sum(jnp.where(lanes == head, past_sums, 0.0), axis=1, keepdims=True)
        top = jnp.maximum(prefix_log, past_log)
        prefix_part = jnp.exp2(prefix_log - top)
        past_part = jnp.exp2(past_log - top)
        both = prefix_part + past_part
        shares.append((prefix_part / both, past_part / both))
    for pair in range(heads // 2):
        at = slice(pair * PAIR, (pair + 1) * PAIR)
        key_half = lanes < HEAD_SIZE
        prefix_share = jnp.where(key_half, shares[2 * pair][0], shares[2 * pair + 1][0])
        past_share = jnp.where(key_half, shares[2 * pair][1], shares[2 * pair + 1][1])
        att_scr[:, at] = (prefix_share * prefix[:, at] + past_share * past_ref[:, at]).astype(BF16)
    copies.start(att_scr, att_ref)
    copies.wait()


def mlp_kernel(count, blocks, place_ref, *refs):
    inputs = 2 * count + 1
    groups = count
    weight_count = groups + 3
    sources, refs = refs[:inputs], refs[inputs:]
    weight_refs, refs = refs[: blocks + 3], refs[blocks + 3 :]
    outs = 3 if count == 2 else 2
    out_refs, held_refs, refs = refs[:outs], refs[outs : outs + weight_count], refs[outs + weight_count :]
    held, out_scr, sems = refs[:inputs], refs[inputs : inputs + outs], refs[inputs + outs]
    copies, started = fetch(sources, held, sems)
    w_outs, (w_gate, w_up, w_down) = held_refs[:groups], held_refs[groups:]
    hidden_width = w_gate.shape[1]
    chunks = [
        pl.ds(start, min(CHUNK, hidden_width - start)) for start in range(0, hidden_width, CHUNK)
    ]
    if blocks == groups:
        outs_in = [[copies.start(weight_refs[i], w_outs[i])] for i in range(groups)]
    else:
        half = weight_refs[1].shape[0]
        odd = place_ref[1]
        outs_in = [
            [copies.start(weight_refs[0], w_outs[0])],
            [
                copies.start(weight_refs[1 + i], w_outs[1].at[pl.ds(start, half)])
                for i, start in enumerate(
                    (
                        2 * odd * half,
                        (2 * odd + 1) * half,
                        2 * (1 - odd) * half,
                        (2 * (1 - odd) + 1) * half,
                    )
                )
            ],
        ]
    weight_refs = weight_refs[blocks:]
    columns = [
        [
            copies.start(weight_refs[i].at[:, at], (w_gate, w_up)[i].at[:, at])
            for i in range(2)
        ]
        for at in chunks
    ]
    downs = [copies.start(weight_refs[2].at[at], w_down.at[at]) for at in chunks]
    copies.flying = []
    for copy in started:
        copy.wait()
    rows = in_order(place_ref, [ref[...] for ref in held[:count]]).astype(F32)
    width = rows.shape[1] // count
    mixed = None
    for i in range(groups):
        for copy in outs_in[i]:
            copy.wait()
        term = jnp.dot(held[count + i][...], w_outs[i][...], preferred_element_type=F32)
        term = term.astype(BF16).astype(F32)
        mixed = term if mixed is None else mixed + term
    residual = (rows + mixed).astype(BF16)
    normed = rms_norm(residual.astype(F32), held[2 * count][...])
    if count == 2:
        first = place_ref[0] == 0
        out_scr[2][...] = jnp.where(first, residual[:, :width], residual[:, width:])
        copies.start(out_scr[2], out_refs[2])
    else:
        out_scr[1][...] = residual
        copies.start(out_scr[1], out_refs[1])
    hidden = []
    for i, at in enumerate(chunks):
        columns[i][0].wait()
        columns[i][1].wait()
        gate_act = jnp.dot(normed, w_gate[:, at], preferred_element_type=F32)
        up_act = jnp.dot(normed, w_up[:, at], preferred_element_type=F32)
        hidden.append((gate_act / (1.0 + jnp.exp(-gate_act)) * up_act).astype(BF16))
    for copy in downs:
        copy.wait()
    hidden = jnp.concatenate(hidden, axis=1)
    terms = jnp.dot(hidden, w_down[...], preferred_element_type=F32).astype(BF16)
    if count == 2:
        out_scr[0][...] = jnp.where(first, terms[:, :width], terms[:, width:])
        out_scr[1][...] = jnp.where(first, terms[:, width:], terms[:, :width])
        copies.start(out_scr[0], out_refs[0])
        copies.start(out_scr[1], out_refs[1])
    else:
        out_scr[0][...] = terms
        copies.start(out_scr[0], out_refs[0])
    copies.wait()


def swap(block, count):
    if count == 2:
        return [block, lax.ppermute(block, "tensor", [(0, 1), (1, 0)])]
    if count == 1:
        return [block]
    gathered = lax.all_gather(block, "tensor", axis=0, tiled=False)
    return [gathered[i] for i in range(count)]


def share_rows(block, count, replicas, after):
    if count != 2 or replicas % 2:
        return swap(block, count), after
    half = block.shape[0] // 2
    odd = lax.axis_index("replica") % 2
    mine = lax.dynamic_slice_in_dim(block, odd * half, half, axis=0)
    pieces = (mine[: half // 2], mine[half // 2 :])
    pieces, after = lax.optimization_barrier((pieces, after))
    return [lax.ppermute(piece, "tensor", [(0, 1), (1, 0)]) for piece in pieces], after


def pass_rows(fetched, replicas):
    return lax.ppermute(fetched, "replica", [(i, i ^ 1) for i in range(replicas)])


def finish(place, parts, attended, gain, w_outs, *weights):
    count = len(parts)
    rows = parts[0].shape[0]
    model = sum(part.shape[1] for part in parts)
    hidden = weights[-1].shape[0]
    width = model // count
    if count == 2:
        outs = [jax.ShapeDtypeStruct((rows, width), BF16)] * 3
    else:
        outs = [jax.ShapeDtypeStruct((rows, model), BF16)] * 2
    operands = (*parts, *attended, gain)
    copies = len(operands) + len(w_outs) + 3 * (-(-hidden // CHUNK)) + len(outs)
    held = [pltpu.VMEM(w.shape, w.dtype) for w in [w_outs[0]] * count + list(weights)]
    return pl.pallas_call(
        functools.partial(mlp_kernel, count, len(w_outs)),
        in_specs=[SCALAR] + [ANY] * (len(operands) + len(w_outs) + len(weights)),
        out_specs=[HBM] * len(outs),
        out_shape=outs,
        scratch_shapes=held
        + scratch_like(*operands, *outs)
        + [pltpu.SemaphoreType.DMA((copies,))],
        compiler_params=params(),
        cost_estimate=cost(6 * rows * model * hidden, 6 * model * hidden, rows * hidden),
        name="mlp",
    )(place, *operands, *w_outs, *weights)


def exchange(terms, count):
    if count == 2:
        keep, send, residual = terms
        other = lax.ppermute(send, "tensor", [(0, 1), (1, 0)])
        summed = keep.astype(F32) + other.astype(F32)
        return (residual.astype(F32) + summed).astype(BF16)
    terms, residual = terms
    width = terms.shape[1] // count
    summed = lax.psum_scatter(terms.astype(F32), "tensor", scatter_dimension=1, tiled=True)
    own = lax.dynamic_slice_in_dim(residual, lax.axis_index("tensor") * width, width, axis=1)
    return (own.astype(F32) + summed).astype(BF16)


def body(
    prompt_rows,
    request_rows,
    request_keyval_cache,
    cache_len,
    destination,
    prefix_cache,
    attn_gain,
    w_query,
    keyval_weight,
    w_out,
    mlp_gain,
    w_gate,
    w_up,
    w_down,
):
    count = lax.axis_size("tensor")
    replicas = lax.axis_size("replica")
    place = jnp.stack((lax.axis_index("tensor"), lax.axis_index("replica") % 2)).astype(jnp.int32)
    requests = request_rows.shape[0]
    prompts = prompt_rows.shape[0]
    model = w_query.shape[0]
    width = w_query.shape[1]
    kv_width = keyval_weight.shape[1]
    heads = width // HEAD_SIZE
    prefix_len = prefix_cache.shape[0]
    attn_gain = attn_gain.reshape(1, model)
    mlp_gain = mlp_gain.reshape(1, model)

    request_parts = swap(request_rows, count)

    per_peer = 2 * requests // replicas
    slots = replicas * per_peer
    target = destination.reshape(1, requests)
    cached = request_keyval_cache.shape[1]
    w_outs, prompt_rows = share_rows(w_out, count, replicas, prompt_rows)
    prompt_parts = swap(prompt_rows, count)
    outs = [
        jax.ShapeDtypeStruct((slots, width), BF16),
        jax.ShapeDtypeStruct((requests, width), F32),
        jax.ShapeDtypeStruct((requests, PAIR), F32),
    ]
    operands = (
        *request_parts,
        attn_gain,
        target,
        w_query,
        cache_len.reshape(1, requests),
        keyval_weight,
        request_keyval_cache,
    )
    blocks = (requests // GROUP, heads * GROUP)
    send, past, past_sums = pl.pallas_call(
        functools.partial(request_kernel, count, per_peer),
        in_specs=[SCALAR] + [ANY] * len(operands),
        out_specs=[HBM] * 3,
        out_shape=outs,
        scratch_shapes=scratch_like(*operands, *outs)
        + [
            pltpu.VMEM((*blocks, kv_width), F32),
            pltpu.VMEM((*blocks, GROUP * cached), F32),
            pltpu.VMEM((*blocks, GROUP * cached), BF16),
            pltpu.VMEM((*blocks, kv_width), F32),
            pltpu.SemaphoreType.DMA((len(operands) + 3,)),
        ],
        compiler_params=params(),
        cost_estimate=cost(
            2 * requests * model * (width + kv_width), 2 * model * (width + kv_width)
        ),
        name="request_project",
    )(place, *operands)

    send, prompt_parts[-1], past, past_sums = lax.optimization_barrier(
        (send, prompt_parts[-1], past, past_sums)
    )
    slot_queries = lax.all_to_all(send, "replica", split_axis=0, concat_axis=0, tiled=True)

    operands = (*prompt_parts, attn_gain, w_query, keyval_weight, prefix_cache)
    prompt_attended = pl.pallas_call(
        functools.partial(prompt_kernel, count),
        in_specs=[SCALAR] + [ANY] * count + [HBM] * 4,
        out_specs=HBM,
        out_shape=jax.ShapeDtypeStruct((prompts, width), BF16),
        scratch_shapes=scratch_like(*operands)
        + [
            pltpu.VMEM((heads, prompts, PAIR), BF16),
            pltpu.VMEM((prefix_len, kv_width), BF16),
            pltpu.VMEM((prompts, width), BF16),
            pltpu.SemaphoreType.DMA((len(operands) + 1,)),
        ],
        compiler_params=params(),
        cost_estimate=cost(
            2 * prompts * model * (width + kv_width) + 4 * prompts * heads * prefix_len * PAIR,
            2 * model * (width + kv_width) + 2 * prefix_len * kv_width,
            prompts * heads * prefix_len,
        ),
        name="prompt_attention",
    )(place, *operands)

    prompt_attended = swap(prompt_attended, count)
    slot_queries, prompt_attended[0], w_outs[0] = lax.optimization_barrier(
        (slot_queries, prompt_attended[0], w_outs[0])
    )
    passed = [pass_rows(w_outs[0], replicas)] if count == 2 else []
    slot_out = pl.pallas_call(
        slot_kernel,
        in_specs=[ANY, HBM],
        out_specs=HBM,
        out_shape=jax.ShapeDtypeStruct((slots, width + PAIR), BF16),
        scratch_shapes=scratch_like(slot_queries, prefix_cache)
        + [
            pltpu.VMEM((slots, width + PAIR), BF16),
            pltpu.VMEM((heads, slots, PAIR), BF16),
            pltpu.VMEM((prefix_len, kv_width), BF16),
            pltpu.SemaphoreType.DMA((3,)),
        ],
        compiler_params=params(),
        cost_estimate=cost(
            4 * slots * heads * prefix_len * PAIR,
            2 * prefix_len * kv_width,
            slots * heads * prefix_len,
        ),
        name="slot_attention",
    )(slot_queries, prefix_cache)

    slot_out, w_outs, prompt_attended = lax.optimization_barrier(
        (slot_out, w_outs, prompt_attended)
    )
    if count == 2:
        w_outs = [w_out, *w_outs, *passed, pass_rows(w_outs[1], replicas)]
    back = lax.all_to_all(slot_out, "replica", split_axis=0, concat_axis=0, tiled=True)

    weights = (mlp_gain, w_outs, w_gate, w_up, w_down)
    prompt_terms = finish(place, prompt_parts, prompt_attended, *weights)
    back, prompt_terms = lax.optimization_barrier((back, prompt_terms))
    operands = (target, back, past, past_sums)
    request_attended = pl.pallas_call(
        functools.partial(merge_kernel, per_peer),
        in_specs=[ANY] * len(operands),
        out_specs=HBM,
        out_shape=jax.ShapeDtypeStruct((requests, width), BF16),
        scratch_shapes=scratch_like(*operands)
        + [pltpu.VMEM((requests, width), BF16), pltpu.SemaphoreType.DMA((5,))],
        compiler_params=params(),
        cost_estimate=cost(4 * requests * slots * width, 4 * slots * width),
        name="merge",
    )(*operands)

    request_terms = finish(place, request_parts, swap(request_attended, count), *weights)
    return (exchange(prompt_terms, count), exchange(request_terms, count))


def solution(mesh):
    return jax.shard_map(
        body,
        mesh=mesh,
        in_specs=(
            P("replica", "tensor"),
            P("replica", "tensor"),
            P("replica", None, "tensor"),
            P("replica"),
            P("replica", None),
            P("replica", "tensor"),
            P(),
            P(None, "tensor"),
            P(None, "tensor"),
            P("tensor", None),
            P(),
            P(None, "tensor"),
            P(None, "tensor"),
            P("tensor", None),
        ),
        out_specs=(P("replica", "tensor"), P("replica", "tensor")),
        check_vma=False,
    )
```

```python
import functools
import math

import jax
import jax.numpy as jnp
from jax import lax
from jax.experimental import pallas as pl
from jax.experimental.pallas import tpu as pltpu
from jax.sharding import PartitionSpec as P

HEAD_SIZE = 64
QUERIES_PER_KEY = 4
PAIR = 2 * HEAD_SIZE
GROUP = 8
CHUNK = 256
EPS = 1e-05
FACTOR = HEAD_SIZE ** (-0.5) * math.log2(math.e)
F32 = jnp.float32
BF16 = jnp.bfloat16
MIB = 1024 * 1024
MOST_VMEM = 62 * MIB
TAIL_VMEM = 36 * MIB
ANY = pl.BlockSpec(memory_space=pl.ANY)
HBM = pl.BlockSpec(memory_space=pltpu.HBM)
HELD = pl.BlockSpec(memory_space=pltpu.VMEM)
SCALAR = pl.BlockSpec(memory_space=pltpu.SMEM)


def params(limit=MOST_VMEM):
    return pltpu.CompilerParams(vmem_limit_bytes=limit)


def cost(flops, read, exps=0):
    return pl.CostEstimate(flops=int(flops), bytes_accessed=int(read), transcendentals=int(exps))


def lane_ids(shape):
    return lax.broadcasted_iota(jnp.int32, shape, len(shape) - 1)


def rms_norm(values, gain_row):
    inv_scale = lax.rsqrt(jnp.mean(values * values, axis=1, keepdims=True) + EPS)
    return (values * inv_scale * gain_row).astype(BF16)


def in_order(place_ref, parts):
    if len(parts) == 2:
        first = place_ref[0] == 0
        own, other = parts
        parts = (jnp.where(first, own, other), jnp.where(first, other, own))
    return jnp.concatenate(parts, axis=1)


def column_of(row):
    shape = (row.shape[1], row.shape[1])
    rows = lax.broadcasted_iota(jnp.int32, shape, 0)
    return jnp.sum(
        jnp.where(rows == lane_ids(shape), jnp.broadcast_to(row, shape), 0), axis=1, keepdims=True
    )


def slot_places(target_row, per_peer):
    count = target_row.shape[1]
    target_column = column_of(target_row)
    shape = (count, count)
    rows, columns = lax.broadcasted_iota(jnp.int32, shape, 0), lane_ids(shape)
    same = (target_column == target_row).astype(jnp.int32)
    column = target_column * per_peer + jnp.sum(
        jnp.where(columns < rows, same, 0), axis=1, keepdims=True
    )
    row = target_row * per_peer + jnp.sum(
        jnp.where(rows < columns, same, 0), axis=0, keepdims=True
    )
    return column, row


def head_query(queries, head):
    pair = head // 2
    block = queries[:, pair * PAIR : (pair + 1) * PAIR].astype(F32)
    if head % 2:
        block = pltpu.roll(block, HEAD_SIZE, 1)
    return jnp.where(lane_ids(block.shape) < HEAD_SIZE, block, 0.0).astype(BF16)


def ones_for_keys(keyval):
    key_half = lane_ids(keyval.shape) % PAIR < HEAD_SIZE
    return jnp.where(key_half, 1.0, keyval.astype(F32)).astype(BF16)


def scores_of(query_rows, key_rows):
    return lax.dot_general(
        query_rows, key_rows, (((1,), (1,)), ((), ())), preferred_element_type=F32
    )


def pack_pair(even, odd):
    even = even / pltpu.roll(even, HEAD_SIZE, 1)
    odd = odd / pltpu.roll(odd, HEAD_SIZE, 1)
    return jnp.where(
        lane_ids(even.shape) < HEAD_SIZE, pltpu.roll(even, HEAD_SIZE, 1), odd
    )


class Copies:
    def __init__(self, sems):
        self.sems = sems
        self.used = 0
        self.flying = []

    def start(self, source, target):
        copy = pltpu.make_async_copy(source, target, self.sems.at[self.used])
        copy.start()
        self.used += 1
        self.flying.append(copy)
        return copy

    def wait(self):
        for copy in self.flying:
            copy.wait()
        self.flying = []


def fetch(refs, targets, sems):
    copies = Copies(sems)
    for ref, target in zip(refs, targets):
        copies.start(ref, target)
    started, copies.flying = copies.flying, []
    return copies, started


def scratch_like(*arrays):
    return [pltpu.VMEM(x.shape, x.dtype) for x in arrays]


def request_kernel(count, per_peer, place_ref, *refs):
    inputs = count + 4
    sources, (send_ref, q_ref, kv_ref), refs = refs[:inputs], refs[inputs : inputs + 3], refs[inputs + 3 :]
    held, (send_scr, q_scr, kv_scr, sems) = refs[:inputs], refs[inputs:]
    copies, started = fetch(sources, held, sems)
    gain_ref, target_ref, w_query_ref, keyval_weight_ref = held[count:]
    for copy in started[: count + 2]:
        copy.wait()
    _, slot_row = slot_places(target_ref[...], per_peer)
    spread = lax.broadcasted_iota(jnp.int32, (send_scr.shape[0], slot_row.shape[1]), 0) == slot_row
    rows = in_order(place_ref, [ref[...] for ref in held[:count]])
    normed = rms_norm(rows.astype(F32), gain_ref[...])
    started[count + 2].wait()
    queries = jnp.dot(normed, w_query_ref[...], preferred_element_type=F32).astype(BF16)
    send_scr[...] = jnp.dot(
        spread.astype(BF16), queries, preferred_element_type=F32
    ).astype(BF16)
    copies.start(send_scr, send_ref)
    q_scr[...] = queries
    copies.start(q_scr, q_ref)
    started[count + 3].wait()
    kv_scr[...] = jnp.dot(normed, keyval_weight_ref[...], preferred_element_type=F32).astype(BF16)
    copies.start(kv_scr, kv_ref)
    copies.wait()


def past_attention(queries, keyval, lengths, cache_ref, past_scr, q_scr, score_scr, weight_scr, mixed_scr):
    requests, cached, kv_width = cache_ref.shape
    groups = requests // GROUP
    keys = GROUP * cached
    heads = queries.shape[1] // HEAD_SIZE
    block_rows = heads * GROUP
    q_scr[...] = jnp.zeros_like(q_scr)
    for head in range(heads):
        at = head // QUERIES_PER_KEY * PAIR
        q_scr[:, head * GROUP : (head + 1) * GROUP, at : at + PAIR] = (
            head_query(queries, head).astype(F32).reshape(groups, GROUP, PAIR)
        )
    own = jnp.broadcast_to(
        keyval.astype(F32).reshape(groups, 1, GROUP, kv_width), (groups, heads, GROUP, kv_width)
    ).reshape(groups * block_rows, kv_width)
    own_scores = jnp.sum(
        q_scr[...].reshape(groups * block_rows, kv_width) * own, axis=1, keepdims=True
    )
    owner = lax.broadcasted_iota(jnp.int32, (block_rows, keys), 0) % GROUP
    columns = lane_ids((block_rows, keys))
    position = jnp.where(columns // cached == owner, columns % cached, cached)
    for group in range(groups):
        block = cache_ref[group * GROUP : (group + 1) * GROUP].reshape(keys, kv_width)
        live = position < jnp.concatenate(
            [lengths[group * GROUP : (group + 1) * GROUP]] * heads, axis=0
        )
        score_scr[group] = jnp.where(
            live, scores_of(q_scr[group].astype(BF16), block), -jnp.inf
        )
    scores = score_scr[...].reshape(groups * block_rows, keys)
    row_max = jnp.maximum(jnp.max(scores, axis=1, keepdims=True), own_scores)
    exp_vals = jnp.exp2((scores - row_max) * FACTOR)
    own_exp = jnp.exp2((own_scores - row_max) * FACTOR)
    weight_scr[...] = exp_vals.astype(BF16).reshape(groups, block_rows, keys)
    total = jnp.sum(exp_vals, axis=1, keepdims=True) + own_exp
    log_sum = (row_max * FACTOR + jnp.log2(total)).reshape(groups, block_rows, 1)
    for group in range(groups):
        block = cache_ref[group * GROUP : (group + 1) * GROUP].reshape(keys, kv_width)
        mixed_scr[group] = jnp.dot(weight_scr[group], block, preferred_element_type=F32)
    mixed = mixed_scr[...].reshape(groups * block_rows, kv_width)
    mixed = (mixed + own_exp.astype(BF16).astype(F32) * own) * (1.0 / total)
    mixed = mixed.reshape(groups, block_rows, kv_width)
    lanes = lane_ids((requests, PAIR))
    sums = jnp.zeros((requests, PAIR), F32)
    done = []
    for head in range(heads):
        at = head // QUERIES_PER_KEY * PAIR
        rows_of = slice(head * GROUP, (head + 1) * GROUP)
        done.append(mixed[:, rows_of, at : at + PAIR].reshape(requests, PAIR))
        sums = jnp.where(lanes == head, log_sum[:, rows_of].reshape(requests, 1), sums)
    for pair in range(heads // 2):
        past_scr[:, pair * PAIR : (pair + 1) * PAIR] = jnp.where(
            lanes < HEAD_SIZE, pltpu.roll(done[2 * pair], HEAD_SIZE, 1), done[2 * pair + 1]
        )
    past_scr[:, heads * HEAD_SIZE :] = sums


def pipelined(count, score, soften, settle):
    scores, pending = score(0), None
    for i in range(count):
        following = score(i + 1) if i + 1 < count else None
        weights = soften(i, scores)
        if pending is not None:
            settle(i - 1, pending)
        scores, pending = following, weights
    settle(count - 1, pending)


def prompt_kernel(count, place_ref, *refs):
    inputs = count + 8
    sources, (att_ref, past_ref), refs = refs[:inputs], refs[inputs : inputs + 2], refs[inputs + 2 :]
    held, (q_scr, kvx_scr, att_scr, past_scr, *past_scrs, sems) = refs[:inputs], refs[inputs:]
    copies, started = fetch(sources, held, sems)
    for copy in started[: count + 1]:
        copy.wait()
    gain_ref, w_query_ref, keyval_weight_ref, prefix_ref = held[count : count + 4]
    request_q_ref, request_kv_ref, len_ref, cache_ref = held[count + 4 :]
    rows = in_order(place_ref, [ref[...] for ref in held[:count]])
    normed = rms_norm(rows.astype(F32), gain_ref[...])
    started[count + 1].wait()
    queries = jnp.dot(normed, w_query_ref[...], preferred_element_type=F32).astype(BF16)
    started[count + 2].wait()
    keyval = jnp.dot(normed, keyval_weight_ref[...], preferred_element_type=F32).astype(BF16)
    started[count + 3].wait()
    heads = queries.shape[1] // HEAD_SIZE
    row_count = queries.shape[0]
    for head in range(heads):
        q_scr[head] = head_query(queries, head)
    kvx_scr[...] = ones_for_keys(prefix_ref[...])
    own_ones = ones_for_keys(keyval)
    row_ids = lax.broadcasted_iota(jnp.int32, (2 * row_count, row_count), 0) % row_count
    visible = lax.broadcasted_iota(jnp.int32, (2 * row_count, row_count), 1) <= row_ids

    def columns_of(pair):
        kv = 2 * pair // QUERIES_PER_KEY
        return slice(kv * PAIR, (kv + 1) * PAIR)

    def score(pair):
        query_rows = q_scr[pl.ds(2 * pair, 2)].reshape(2 * row_count, PAIR)
        past = scores_of(query_rows, prefix_ref[:, columns_of(pair)])
        own = scores_of(query_rows, keyval[:, columns_of(pair)])
        return past, jnp.where(visible, own, -jnp.inf)

    def soften(pair, scores):
        past, own = scores
        row_max = jnp.maximum(
            jnp.max(past, axis=1, keepdims=True), jnp.max(own, axis=1, keepdims=True)
        )
        return [jnp.exp2((part - row_max) * FACTOR).astype(BF16) for part in (past, own)]

    def settle(pair, weights):
        total = jnp.dot(weights[0], kvx_scr[:, columns_of(pair)], preferred_element_type=F32)
        total = total + jnp.dot(
            weights[1], own_ones[:, columns_of(pair)], preferred_element_type=F32
        )
        att_scr[:, pair * PAIR : (pair + 1) * PAIR] = pack_pair(
            total[:row_count], total[row_count:]
        ).astype(BF16)

    pipelined(heads // 2, score, soften, settle)
    copies.start(att_scr, att_ref)
    for copy in started[count + 4 :]:
        copy.wait()
    past_attention(
        request_q_ref[...],
        request_kv_ref[...],
        column_of(len_ref[...]),
        cache_ref,
        past_scr,
        *past_scrs,
    )
    copies.start(past_scr, past_ref)
    copies.wait()


def slot_kernel(q_hbm, prefix_hbm, out_hbm, q_ref, prefix_ref, out_ref, q_scr, kvx_scr, sems):
    copies, started = fetch((q_hbm, prefix_hbm), (q_ref, prefix_ref), sems)
    started[0].wait()
    slots, width = q_ref.shape
    heads = width // HEAD_SIZE
    queries = q_ref[...]
    for head in range(heads):
        q_scr[head] = head_query(queries, head)
    started[1].wait()
    kvx_scr[...] = ones_for_keys(prefix_ref[...])
    lanes = lane_ids((slots, PAIR))
    sums = [jnp.zeros((slots, PAIR), F32)]
    even = []

    def columns_of(head):
        kv = head // QUERIES_PER_KEY
        return slice(kv * PAIR, (kv + 1) * PAIR)

    def score(head):
        return scores_of(q_scr[head], prefix_ref[:, columns_of(head)])

    def soften(head, scores):
        row_max = jnp.max(scores, axis=1, keepdims=True)
        return row_max, jnp.exp2((scores - row_max) * FACTOR).astype(BF16)

    def settle(head, pending):
        row_max, weights = pending
        total = jnp.dot(weights, kvx_scr[:, columns_of(head)], preferred_element_type=F32)
        log_sum = row_max * FACTOR + jnp.log2(total)
        high = log_sum.astype(BF16).astype(F32)
        middle = (log_sum - high).astype(BF16).astype(F32)
        low = log_sum - high - middle
        for place, part in enumerate((high, middle, low)):
            sums[0] = jnp.where(lanes == 3 * head + place, part, sums[0])
        if head % 2 == 0:
            even.append(total)
            return
        at = slice((head - 1) * HEAD_SIZE, (head + 1) * HEAD_SIZE)
        out_ref[:, at] = pack_pair(even[-1], total).astype(BF16)
        copies.start(out_ref.at[:, at], out_hbm.at[:, at])

    pipelined(heads, score, soften, settle)
    out_ref[:, width:] = sums[0].astype(BF16)
    copies.start(out_ref.at[:, width:], out_hbm.at[:, width:])
    copies.wait()


def merge_kernel(per_peer, *refs):
    sources, att_ref, held, (att_scr, sems) = refs[:3], refs[3], refs[4:7], refs[7:]
    copies, started = fetch(sources, held, sems)
    target_ref, back_ref, past_ref = held
    for copy in started:
        copy.wait()
    slot_column, _ = slot_places(target_ref[...], per_peer)
    gather = lane_ids((slot_column.shape[0], back_ref.shape[0])) == slot_column
    width = past_ref.shape[1] - PAIR
    heads = width // HEAD_SIZE
    prefix = jnp.dot(gather.astype(BF16), back_ref[...], preferred_element_type=F32)
    prefix_sums = prefix[:, width:]
    past_sums = past_ref[:, width:]
    lanes = lane_ids(past_sums.shape)
    shares = []
    for head in range(heads):
        prefix_log = jnp.sum(
            jnp.where(lanes // 3 == head, prefix_sums, 0.0), axis=1, keepdims=True
        )
        past_log = jnp.sum(jnp.where(lanes == head, past_sums, 0.0), axis=1, keepdims=True)
        top = jnp.maximum(prefix_log, past_log)
        prefix_part = jnp.exp2(prefix_log - top)
        past_part = jnp.exp2(past_log - top)
        both = prefix_part + past_part
        shares.append((prefix_part / both, past_part / both))
    for pair in range(heads // 2):
        at = slice(pair * PAIR, (pair + 1) * PAIR)
        key_half = lanes < HEAD_SIZE
        prefix_share = jnp.where(key_half, shares[2 * pair][0], shares[2 * pair + 1][0])
        past_share = jnp.where(key_half, shares[2 * pair][1], shares[2 * pair + 1][1])
        att_scr[:, at] = (prefix_share * prefix[:, at] + past_share * past_ref[:, at]).astype(BF16)
    copies.start(att_scr, att_ref)
    copies.wait()


def mlp_kernel(count, blocks, place_ref, *refs):
    inputs = 2 * count + 1
    groups = count
    weight_count = groups + 3
    sources, refs = refs[:inputs], refs[inputs:]
    weight_refs, refs = refs[: blocks + 3], refs[blocks + 3 :]
    outs = 3 if count == 2 else 2
    out_refs, held_refs, refs = refs[:outs], refs[outs : outs + weight_count], refs[outs + weight_count :]
    held, out_scr, sems = refs[:inputs], refs[inputs : inputs + outs], refs[inputs + outs]
    copies, started = fetch(sources, held, sems)
    w_outs, (w_gate, w_up, w_down) = held_refs[:groups], held_refs[groups:]
    hidden_width = w_gate.shape[1]
    chunks = [
        pl.ds(start, min(CHUNK, hidden_width - start)) for start in range(0, hidden_width, CHUNK)
    ]
    if blocks == groups:
        outs_in = [[copies.start(weight_refs[i], w_outs[i])] for i in range(groups)]
    else:
        outs_in = [
            [copies.start(weight_refs[0], w_outs[0])],
            start_pieces(copies, place_ref, weight_refs[1:blocks], w_outs[1]),
        ]
    weight_refs = weight_refs[blocks:]
    columns = [
        [
            copies.start(weight_refs[i].at[:, at], (w_gate, w_up)[i].at[:, at])
            for i in range(2)
        ]
        for at in chunks
    ]
    downs = [copies.start(weight_refs[2].at[at], w_down.at[at]) for at in chunks]
    copies.flying = []
    for copy in started:
        copy.wait()
    rows = in_order(place_ref, [ref[...] for ref in held[:count]]).astype(F32)
    width = rows.shape[1] // count
    mixed = None
    for i in range(groups):
        for copy in outs_in[i]:
            copy.wait()
        term = jnp.dot(held[count + i][...], w_outs[i][...], preferred_element_type=F32)
        term = term.astype(BF16).astype(F32)
        mixed = term if mixed is None else mixed + term
    residual = (rows + mixed).astype(BF16)
    normed = rms_norm(residual.astype(F32), held[2 * count][...])
    if count == 2:
        first = place_ref[0] == 0
        out_scr[2][...] = jnp.where(first, residual[:, :width], residual[:, width:])
        copies.start(out_scr[2], out_refs[2])
    else:
        out_scr[1][...] = residual
        copies.start(out_scr[1], out_refs[1])
    hidden = []
    for i, at in enumerate(chunks):
        columns[i][0].wait()
        columns[i][1].wait()
        gate_act = jnp.dot(normed, w_gate[:, at], preferred_element_type=F32)
        up_act = jnp.dot(normed, w_up[:, at], preferred_element_type=F32)
        hidden.append((gate_act / (1.0 + jnp.exp(-gate_act)) * up_act).astype(BF16))
    for copy in downs:
        copy.wait()
    hidden = jnp.concatenate(hidden, axis=1)
    terms = jnp.dot(hidden, w_down[...], preferred_element_type=F32).astype(BF16)
    if count == 2:
        out_scr[0][...] = jnp.where(first, terms[:, :width], terms[:, width:])
        out_scr[1][...] = jnp.where(first, terms[:, width:], terms[:, :width])
        copies.start(out_scr[0], out_refs[0])
        copies.start(out_scr[1], out_refs[1])
    else:
        out_scr[0][...] = terms
        copies.start(out_scr[0], out_refs[0])
    copies.wait()


def load_kernel(*refs):
    count = len(refs) // 2
    _, started = fetch(refs[:count], refs[count : 2 * count], refs[-1])
    for copy in started:
        copy.wait()


def load(limit, *arrays):
    return pl.pallas_call(
        load_kernel,
        in_specs=[ANY] * len(arrays),
        out_specs=[HELD] * len(arrays),
        out_shape=[jax.ShapeDtypeStruct(x.shape, x.dtype) for x in arrays],
        scratch_shapes=[pltpu.SemaphoreType.DMA((len(arrays),))],
        compiler_params=params(limit),
        cost_estimate=cost(0, sum(2 * x.size for x in arrays)),
        name="load",
    )(*arrays)


def start_pieces(copies, place_ref, pieces, target):
    rows = pieces[0].shape[0]
    odd = place_ref[1]
    starts = (2 * odd, 2 * odd + 1, 2 * (1 - odd), 2 * (1 - odd) + 1)
    return [
        copies.start(piece, target.at[pl.ds(start * rows, rows)])
        for piece, start in zip(pieces, starts)
    ]


def tail_kernel(place_ref, *refs):
    w_gate, w_up, sources, pieces, w_down_hbm = refs[0], refs[1], refs[2:8], refs[8:12], refs[12]
    send_ref, hidden_ref, residual_ref = refs[13:16]
    held, (w_out_other, w_down, send_scr, sems) = refs[16:22], refs[22:]
    own_ref, other_ref, gain_ref, att_ref, att_other_ref, w_out_ref = held
    width = send_scr.shape[1]
    hidden_width = w_gate.shape[1]
    away = pl.ds(pl.multiple_of((1 - place_ref[0]) * width, width), width)
    copies, started = fetch(sources, held, sems)
    arriving = start_pieces(copies, place_ref, pieces, w_out_other)
    down = copies.start(w_down_hbm.at[:, away], w_down)
    copies.flying = []
    for copy in started:
        copy.wait()
    rows = in_order(place_ref, [own_ref[...], other_ref[...]]).astype(F32)
    mixed = jnp.dot(att_ref[...], w_out_ref[...], preferred_element_type=F32)
    for copy in arriving:
        copy.wait()
    mixed_other = jnp.dot(att_other_ref[...], w_out_other[...], preferred_element_type=F32)
    mixed = mixed.astype(BF16).astype(F32) + mixed_other.astype(BF16).astype(F32)
    residual = (rows + mixed).astype(BF16)
    normed = rms_norm(residual.astype(F32), gain_ref[...])
    residual_ref[...] = jnp.where(place_ref[0] == 0, residual[:, :width], residual[:, width:])
    hidden = []
    for start in range(0, hidden_width, CHUNK):
        at = slice(start, min(start + CHUNK, hidden_width))
        gate_act = jnp.dot(normed, w_gate[:, at], preferred_element_type=F32)
        up_act = jnp.dot(normed, w_up[:, at], preferred_element_type=F32)
        hidden.append((gate_act / (1.0 + jnp.exp(-gate_act)) * up_act).astype(BF16))
    hidden = jnp.concatenate(hidden, axis=1)
    down.wait()
    send_scr[...] = jnp.dot(hidden, w_down[...], preferred_element_type=F32).astype(BF16)
    copies.start(send_scr, send_ref)
    hidden_ref[...] = hidden
    copies.wait()


def keep_kernel(place_ref, hidden_ref, residual_ref, w_down_hbm, out_ref, w_down, sems):
    width = out_ref.shape[1]
    own = pl.ds(pl.multiple_of(place_ref[0] * width, width), width)
    copies = Copies(sems)
    copies.start(w_down_hbm.at[:, own], w_down)
    copies.wait()
    term = jnp.dot(hidden_ref[...], w_down[...], preferred_element_type=F32).astype(BF16)
    out_ref[...] = residual_ref[...].astype(F32) + term.astype(F32)


def tail(place, parts, attended, gain, w_outs, w_gate, w_up, w_down):
    attended, w_gate, w_up = lax.optimization_barrier((attended, w_gate, w_up))
    rows, width = parts[0].shape
    hidden = w_up.shape[1]
    held = load(TAIL_VMEM, w_gate, w_up)
    sources = (*parts, gain, *swap(attended, 2), w_outs[0])
    half = jax.ShapeDtypeStruct((rows, width), BF16)
    units = jax.ShapeDtypeStruct((rows, hidden), BF16)
    half_down = pltpu.VMEM((hidden, width), BF16)
    send, units, residual = pl.pallas_call(
        tail_kernel,
        in_specs=[SCALAR] + [HELD] * 2 + [ANY] * 11,
        out_specs=[HBM, HELD, HELD],
        out_shape=[half, units, half],
        scratch_shapes=scratch_like(*sources, w_outs[0])
        + [half_down, pltpu.VMEM((rows, width), BF16), pltpu.SemaphoreType.DMA((12,))],
        compiler_params=params(TAIL_VMEM),
        cost_estimate=cost(10 * rows * width * hidden, 6 * width * hidden, rows * hidden),
        name="tail",
    )(place, *held, *sources, *w_outs[1:], w_down)
    kept = pl.pallas_call(
        keep_kernel,
        in_specs=[SCALAR] + [HELD] * 2 + [ANY],
        out_specs=HELD,
        out_shape=jax.ShapeDtypeStruct((rows, width), F32),
        scratch_shapes=[half_down, pltpu.SemaphoreType.DMA((1,))],
        compiler_params=params(TAIL_VMEM),
        cost_estimate=cost(2 * rows * width * hidden, 2 * width * hidden),
        name="keep",
    )(place, units, residual, w_down)
    other = lax.ppermute(send, "tensor", [(0, 1), (1, 0)])
    return (kept + other.astype(F32)).astype(BF16)


def swap(block, count):
    if count == 2:
        return [block, lax.ppermute(block, "tensor", [(0, 1), (1, 0)])]
    if count == 1:
        return [block]
    gathered = lax.all_gather(block, "tensor", axis=0, tiled=False)
    return [gathered[i] for i in range(count)]


def share_rows(block, count, replicas, after):
    if count != 2 or replicas % 2:
        return swap(block, count), after
    half = block.shape[0] // 2
    odd = lax.axis_index("replica") % 2
    mine = lax.dynamic_slice_in_dim(block, odd * half, half, axis=0)
    pieces = (mine[: half // 2], mine[half // 2 :])
    pieces, after = lax.optimization_barrier((pieces, after))
    return [lax.ppermute(piece, "tensor", [(0, 1), (1, 0)]) for piece in pieces], after


def pass_rows(fetched, replicas):
    return lax.ppermute(fetched, "replica", [(i, i ^ 1) for i in range(replicas)])


def finish(place, parts, attended, gain, w_outs, *weights):
    count = len(parts)
    rows = parts[0].shape[0]
    model = sum(part.shape[1] for part in parts)
    hidden = weights[-1].shape[0]
    width = model // count
    if count == 2:
        outs = [jax.ShapeDtypeStruct((rows, width), BF16)] * 3
    else:
        outs = [jax.ShapeDtypeStruct((rows, model), BF16)] * 2
    operands = (*parts, *attended, gain)
    copies = len(operands) + len(w_outs) + 3 * (-(-hidden // CHUNK)) + len(outs)
    held = [pltpu.VMEM(w.shape, w.dtype) for w in [w_outs[0]] * count + list(weights)]
    return pl.pallas_call(
        functools.partial(mlp_kernel, count, len(w_outs)),
        in_specs=[SCALAR] + [ANY] * (len(operands) + len(w_outs) + len(weights)),
        out_specs=[HBM] * len(outs),
        out_shape=outs,
        scratch_shapes=held
        + scratch_like(*operands, *outs)
        + [pltpu.SemaphoreType.DMA((copies,))],
        compiler_params=params(),
        cost_estimate=cost(6 * rows * model * hidden, 6 * model * hidden, rows * hidden),
        name="mlp",
    )(place, *operands, *w_outs, *weights)


def exchange(terms, count):
    if count == 2:
        keep, send, residual = terms
        other = lax.ppermute(send, "tensor", [(0, 1), (1, 0)])
        summed = keep.astype(F32) + other.astype(F32)
        return (residual.astype(F32) + summed).astype(BF16)
    terms, residual = terms
    width = terms.shape[1] // count
    summed = lax.psum_scatter(terms.astype(F32), "tensor", scatter_dimension=1, tiled=True)
    own = lax.dynamic_slice_in_dim(residual, lax.axis_index("tensor") * width, width, axis=1)
    return (own.astype(F32) + summed).astype(BF16)


def body(
    prompt_rows,
    request_rows,
    request_keyval_cache,
    cache_len,
    destination,
    prefix_cache,
    attn_gain,
    w_query,
    keyval_weight,
    w_out,
    mlp_gain,
    w_gate,
    w_up,
    w_down,
):
    count = lax.axis_size("tensor")
    replicas = lax.axis_size("replica")
    place = jnp.stack((lax.axis_index("tensor"), lax.axis_index("replica") % 2)).astype(jnp.int32)
    requests = request_rows.shape[0]
    prompts = prompt_rows.shape[0]
    model = w_query.shape[0]
    width = w_query.shape[1]
    kv_width = keyval_weight.shape[1]
    heads = width // HEAD_SIZE
    prefix_len = prefix_cache.shape[0]
    attn_gain = attn_gain.reshape(1, model)
    mlp_gain = mlp_gain.reshape(1, model)

    request_parts = swap(request_rows, count)

    per_peer = 2 * requests // replicas
    slots = replicas * per_peer
    target = destination.reshape(1, requests)
    cached = request_keyval_cache.shape[1]
    w_outs, prompt_rows = share_rows(w_out, count, replicas, prompt_rows)
    prompt_parts = swap(prompt_rows, count)
    operands = (*request_parts, attn_gain, target, w_query, keyval_weight)
    outs = [
        jax.ShapeDtypeStruct((slots, width), BF16),
        jax.ShapeDtypeStruct((requests, width), BF16),
        jax.ShapeDtypeStruct((requests, kv_width), BF16),
    ]
    send, queries, keyval = pl.pallas_call(
        functools.partial(request_kernel, count, per_peer),
        in_specs=[SCALAR] + [ANY] * len(operands),
        out_specs=[HBM] * 3,
        out_shape=outs,
        scratch_shapes=scratch_like(*operands, *outs)
        + [pltpu.SemaphoreType.DMA((len(operands) + 3,))],
        compiler_params=params(),
        cost_estimate=cost(
            2 * requests * model * (width + kv_width), 2 * model * (width + kv_width)
        ),
        name="request_project",
    )(place, *operands)

    send, prompt_parts[-1] = lax.optimization_barrier((send, prompt_parts[-1]))
    slot_queries = lax.all_to_all(send, "replica", split_axis=0, concat_axis=0, tiled=True)

    operands = (
        *prompt_parts,
        attn_gain,
        w_query,
        keyval_weight,
        prefix_cache,
        queries,
        keyval,
        cache_len.reshape(1, requests),
        request_keyval_cache,
    )
    outs = [
        jax.ShapeDtypeStruct((prompts, width), BF16),
        jax.ShapeDtypeStruct((requests, width + PAIR), F32),
    ]
    blocks = (requests // GROUP, heads * GROUP)
    prompt_attended, past = pl.pallas_call(
        functools.partial(prompt_kernel, count),
        in_specs=[SCALAR] + [ANY] * len(operands),
        out_specs=[HBM] * 2,
        out_shape=outs,
        scratch_shapes=scratch_like(*operands)
        + [
            pltpu.VMEM((heads, prompts, PAIR), BF16),
            pltpu.VMEM((prefix_len, kv_width), BF16),
        ]
        + scratch_like(*outs)
        + [
            pltpu.VMEM((*blocks, kv_width), F32),
            pltpu.VMEM((*blocks, GROUP * cached), F32),
            pltpu.VMEM((*blocks, GROUP * cached), BF16),
            pltpu.VMEM((*blocks, kv_width), F32),
            pltpu.SemaphoreType.DMA((len(operands) + 2,)),
        ],
        compiler_params=params(),
        cost_estimate=cost(
            2 * prompts * model * (width + kv_width) + 4 * prompts * heads * prefix_len * PAIR,
            2 * model * (width + kv_width) + 2 * prefix_len * kv_width,
            prompts * heads * prefix_len,
        ),
        name="prompt_attention",
    )(place, *operands)

    prompt_attended = swap(prompt_attended, count)
    slot_queries, prompt_attended[0], w_outs[0] = lax.optimization_barrier(
        (slot_queries, prompt_attended[0], w_outs[0])
    )
    passed = [pass_rows(w_outs[0], replicas)] if count == 2 else []
    slot_out = pl.pallas_call(
        slot_kernel,
        in_specs=[ANY, HBM],
        out_specs=HBM,
        out_shape=jax.ShapeDtypeStruct((slots, width + PAIR), BF16),
        scratch_shapes=scratch_like(slot_queries, prefix_cache)
        + [
            pltpu.VMEM((slots, width + PAIR), BF16),
            pltpu.VMEM((heads, slots, PAIR), BF16),
            pltpu.VMEM((prefix_len, kv_width), BF16),
            pltpu.SemaphoreType.DMA((3 + heads // 2,)),
        ],
        compiler_params=params(),
        cost_estimate=cost(
            4 * slots * heads * prefix_len * PAIR,
            2 * prefix_len * kv_width,
            slots * heads * prefix_len,
        ),
        name="slot_attention",
    )(slot_queries, prefix_cache)

    slot_out, w_outs, prompt_attended = lax.optimization_barrier(
        (slot_out, w_outs, prompt_attended)
    )
    if count == 2:
        w_outs = [w_out, *w_outs, *passed, pass_rows(w_outs[1], replicas)]
    back = lax.all_to_all(slot_out, "replica", split_axis=0, concat_axis=0, tiled=True)

    weights = (mlp_gain, w_outs, w_gate, w_up, w_down)
    prompt_terms = finish(place, prompt_parts, prompt_attended, *weights)
    back, prompt_terms = lax.optimization_barrier((back, prompt_terms))
    operands = (target, back, past)
    request_attended = pl.pallas_call(
        functools.partial(merge_kernel, per_peer),
        in_specs=[ANY] * len(operands),
        out_specs=HBM,
        out_shape=jax.ShapeDtypeStruct((requests, width), BF16),
        scratch_shapes=scratch_like(*operands)
        + [pltpu.VMEM((requests, width), BF16), pltpu.SemaphoreType.DMA((4,))],
        compiler_params=params(),
        cost_estimate=cost(4 * requests * slots * width, 4 * slots * width),
        name="merge",
    )(*operands)

    if count == 2:
        request_out = tail(place, request_parts, request_attended, *weights)
    else:
        request_out = exchange(
            finish(place, request_parts, swap(request_attended, count), *weights), count
        )
    return (exchange(prompt_terms, count), request_out)


def solution(mesh):
    return jax.shard_map(
        body,
        mesh=mesh,
        in_specs=(
            P("replica", "tensor"),
            P("replica", "tensor"),
            P("replica", None, "tensor"),
            P("replica"),
            P("replica", None),
            P("replica", "tensor"),
            P(),
            P(None, "tensor"),
            P(None, "tensor"),
            P("tensor", None),
            P(),
            P(None, "tensor"),
            P(None, "tensor"),
            P("tensor", None),
        ),
        out_specs=(P("replica", "tensor"), P("replica", "tensor")),
        check_vma=False,
    )
```

```python
import functools
import math

import jax
import jax.numpy as jnp
from jax import lax
from jax.experimental import pallas as pl
from jax.experimental.pallas import tpu as pltpu
from jax.sharding import PartitionSpec as P

HEAD_SIZE = 64
QUERIES_PER_KEY = 4
PAIR = 2 * HEAD_SIZE
GROUP = 8
CHUNK = 256
FILL = 32
EPS = 1e-05
FACTOR = HEAD_SIZE ** (-0.5) * math.log2(math.e)
F32 = jnp.float32
BF16 = jnp.bfloat16
MIB = 1024 * 1024
MOST_VMEM = 62 * MIB
REQUEST_VMEM = 40 * MIB
TAIL_VMEM = 40 * MIB
MERGE_VMEM = 40 * MIB
ANY = pl.BlockSpec(memory_space=pl.ANY)
HBM = pl.BlockSpec(memory_space=pltpu.HBM)
HELD = pl.BlockSpec(memory_space=pltpu.VMEM)
SCALAR = pl.BlockSpec(memory_space=pltpu.SMEM)


def params(limit=MOST_VMEM):
    return pltpu.CompilerParams(vmem_limit_bytes=limit)


def cost(flops, read, exps=0):
    return pl.CostEstimate(flops=int(flops), bytes_accessed=int(read), transcendentals=int(exps))


def lane_ids(shape):
    return lax.broadcasted_iota(jnp.int32, shape, len(shape) - 1)


def rms_norm(values, gain_row):
    inv_scale = lax.rsqrt(jnp.mean(values * values, axis=1, keepdims=True) + EPS)
    return (values * inv_scale * gain_row).astype(BF16)


def in_order(place_ref, parts):
    if len(parts) == 2:
        first = place_ref[0] == 0
        own, other = parts
        parts = (jnp.where(first, own, other), jnp.where(first, other, own))
    return jnp.concatenate(parts, axis=1)


def column_of(row):
    shape = (row.shape[1], row.shape[1])
    rows = lax.broadcasted_iota(jnp.int32, shape, 0)
    return jnp.sum(
        jnp.where(rows == lane_ids(shape), jnp.broadcast_to(row, shape), 0), axis=1, keepdims=True
    )


def slot_places(target_row, per_peer):
    count = target_row.shape[1]
    target_column = column_of(target_row)
    shape = (count, count)
    rows, columns = lax.broadcasted_iota(jnp.int32, shape, 0), lane_ids(shape)
    same = (target_column == target_row).astype(jnp.int32)
    column = target_column * per_peer + jnp.sum(
        jnp.where(columns < rows, same, 0), axis=1, keepdims=True
    )
    row = target_row * per_peer + jnp.sum(
        jnp.where(rows < columns, same, 0), axis=0, keepdims=True
    )
    return column, row


def head_query(queries, head):
    pair = head // 2
    block = queries[:, pair * PAIR : (pair + 1) * PAIR].astype(F32)
    if head % 2:
        block = pltpu.roll(block, HEAD_SIZE, 1)
    return jnp.where(lane_ids(block.shape) < HEAD_SIZE, block, 0.0).astype(BF16)


def ones_for_keys(keyval):
    key_half = lane_ids(keyval.shape) % PAIR < HEAD_SIZE
    return jnp.where(key_half, 1.0, keyval.astype(F32)).astype(BF16)


def scores_of(query_rows, key_rows):
    return lax.dot_general(
        query_rows, key_rows, (((1,), (1,)), ((), ())), preferred_element_type=F32
    )


def pack_pair(even, odd):
    even = even / pltpu.roll(even, HEAD_SIZE, 1)
    odd = odd / pltpu.roll(odd, HEAD_SIZE, 1)
    return jnp.where(
        lane_ids(even.shape) < HEAD_SIZE, pltpu.roll(even, HEAD_SIZE, 1), odd
    )


class Copies:
    def __init__(self, sems):
        self.sems = sems
        self.used = 0
        self.flying = []

    def start(self, source, target):
        copy = pltpu.make_async_copy(source, target, self.sems.at[self.used])
        copy.start()
        self.used += 1
        self.flying.append(copy)
        return copy

    def wait(self):
        for copy in self.flying:
            copy.wait()
        self.flying = []


def fetch(refs, targets, sems):
    copies = Copies(sems)
    for ref, target in zip(refs, targets):
        copies.start(ref, target)
    started, copies.flying = copies.flying, []
    return copies, started


def scratch_like(*arrays):
    return [pltpu.VMEM(x.shape, x.dtype) for x in arrays]


def request_kernel(count, per_peer, place_ref, *refs):
    inputs = count + 2
    w_query_ref, keyval_weight_ref, *refs = refs
    sources, (send_ref, both_ref), refs = refs[:inputs], refs[inputs : inputs + 2], refs[inputs + 2 :]
    held, (send_scr, both_scr, sems) = refs[:inputs], refs[inputs:]
    copies, started = fetch(sources, held, sems)
    gain_ref, target_ref = held[count:]
    for copy in started:
        copy.wait()
    _, slot_row = slot_places(target_ref[...], per_peer)
    spread = lax.broadcasted_iota(jnp.int32, (send_scr.shape[0], slot_row.shape[1]), 0) == slot_row
    rows = in_order(place_ref, [ref[...] for ref in held[:count]])
    normed = rms_norm(rows.astype(F32), gain_ref[...])
    queries = jnp.dot(normed, w_query_ref[...], preferred_element_type=F32).astype(BF16)
    send_scr[...] = jnp.dot(
        spread.astype(BF16), queries, preferred_element_type=F32
    ).astype(BF16)
    copies.start(send_scr, send_ref)
    width = queries.shape[1]
    both_scr[:, :width] = queries
    both_scr[:, width:] = jnp.dot(normed, keyval_weight_ref[...], preferred_element_type=F32).astype(BF16)
    copies.start(both_scr, both_ref)
    copies.wait()


def past_attention(queries, keyval, lengths, cache_ref, past_scr, q_scr, score_scr, weight_scr, mixed_scr):
    requests, cached, kv_width = cache_ref.shape
    groups = requests // GROUP
    keys = GROUP * cached
    heads = queries.shape[1] // HEAD_SIZE
    block_rows = heads * GROUP
    q_scr[...] = jnp.zeros_like(q_scr)
    for head in range(heads):
        at = head // QUERIES_PER_KEY * PAIR
        q_scr[:, head * GROUP : (head + 1) * GROUP, at : at + PAIR] = (
            head_query(queries, head).astype(F32).reshape(groups, GROUP, PAIR)
        )
    own = jnp.broadcast_to(
        keyval.astype(F32).reshape(groups, 1, GROUP, kv_width), (groups, heads, GROUP, kv_width)
    ).reshape(groups * block_rows, kv_width)
    own_scores = jnp.sum(
        q_scr[...].reshape(groups * block_rows, kv_width) * own, axis=1, keepdims=True
    )
    owner = lax.broadcasted_iota(jnp.int32, (block_rows, keys), 0) % GROUP
    columns = lane_ids((block_rows, keys))
    position = jnp.where(columns // cached == owner, columns % cached, cached)
    for group in range(groups):
        block = cache_ref[group * GROUP : (group + 1) * GROUP].reshape(keys, kv_width)
        live = position < jnp.concatenate(
            [lengths[group * GROUP : (group + 1) * GROUP]] * heads, axis=0
        )
        score_scr[group] = jnp.where(
            live, scores_of(q_scr[group].astype(BF16), block), -jnp.inf
        )
    scores = score_scr[...].reshape(groups * block_rows, keys)
    row_max = jnp.maximum(jnp.max(scores, axis=1, keepdims=True), own_scores)
    exp_vals = jnp.exp2((scores - row_max) * FACTOR)
    own_exp = jnp.exp2((own_scores - row_max) * FACTOR)
    weight_scr[...] = exp_vals.astype(BF16).reshape(groups, block_rows, keys)
    total = jnp.sum(exp_vals, axis=1, keepdims=True) + own_exp
    log_sum = (row_max * FACTOR + jnp.log2(total)).reshape(groups, block_rows, 1)
    for group in range(groups):
        block = cache_ref[group * GROUP : (group + 1) * GROUP].reshape(keys, kv_width)
        mixed_scr[group] = jnp.dot(weight_scr[group], block, preferred_element_type=F32)
    mixed = mixed_scr[...].reshape(groups * block_rows, kv_width)
    mixed = (mixed + own_exp.astype(BF16).astype(F32) * own) * (1.0 / total)
    mixed = mixed.reshape(groups, block_rows, kv_width)
    lanes = lane_ids((requests, PAIR))
    sums = jnp.zeros((requests, PAIR), F32)
    done = []
    for head in range(heads):
        at = head // QUERIES_PER_KEY * PAIR
        rows_of = slice(head * GROUP, (head + 1) * GROUP)
        done.append(mixed[:, rows_of, at : at + PAIR].reshape(requests, PAIR))
        sums = jnp.where(lanes == head, log_sum[:, rows_of].reshape(requests, 1), sums)
    for pair in range(heads // 2):
        past_scr[:, pair * PAIR : (pair + 1) * PAIR] = jnp.where(
            lanes < HEAD_SIZE, pltpu.roll(done[2 * pair], HEAD_SIZE, 1), done[2 * pair + 1]
        )
    past_scr[:, heads * HEAD_SIZE :] = sums


def pipelined(count, score, soften, settle):
    scores, pending = score(0), None
    for i in range(count):
        following = score(i + 1) if i + 1 < count else None
        weights = soften(i, scores)
        if pending is not None:
            settle(i - 1, pending)
        scores, pending = following, weights
    settle(count - 1, pending)


def prompt_kernel(count, place_ref, *refs):
    inputs = count + 7
    sources, (att_ref, past_ref), refs = refs[:inputs], refs[inputs : inputs + 2], refs[inputs + 2 :]
    held, (q_scr, kvx_scr, att_scr, past_scr, *past_scrs, sems) = refs[:inputs], refs[inputs:]
    copies, started = fetch(sources, held, sems)
    for copy in started[: count + 1]:
        copy.wait()
    gain_ref, w_query_ref, keyval_weight_ref, prefix_ref = held[count : count + 4]
    projected_ref, len_ref, cache_ref = held[count + 4 :]
    rows = in_order(place_ref, [ref[...] for ref in held[:count]])
    normed = rms_norm(rows.astype(F32), gain_ref[...])
    started[count + 1].wait()
    queries = jnp.dot(normed, w_query_ref[...], preferred_element_type=F32).astype(BF16)
    started[count + 2].wait()
    keyval = jnp.dot(normed, keyval_weight_ref[...], preferred_element_type=F32).astype(BF16)
    started[count + 3].wait()
    heads = queries.shape[1] // HEAD_SIZE
    row_count = queries.shape[0]
    for head in range(heads):
        q_scr[head] = head_query(queries, head)
    kvx_scr[...] = ones_for_keys(prefix_ref[...])
    own_ones = ones_for_keys(keyval)
    row_ids = lax.broadcasted_iota(jnp.int32, (2 * row_count, row_count), 0) % row_count
    visible = lax.broadcasted_iota(jnp.int32, (2 * row_count, row_count), 1) <= row_ids

    def columns_of(pair):
        kv = 2 * pair // QUERIES_PER_KEY
        return slice(kv * PAIR, (kv + 1) * PAIR)

    def score(pair):
        query_rows = q_scr[pl.ds(2 * pair, 2)].reshape(2 * row_count, PAIR)
        past = scores_of(query_rows, prefix_ref[:, columns_of(pair)])
        own = scores_of(query_rows, keyval[:, columns_of(pair)])
        return past, jnp.where(visible, own, -jnp.inf)

    def soften(pair, scores):
        past, own = scores
        row_max = jnp.maximum(
            jnp.max(past, axis=1, keepdims=True), jnp.max(own, axis=1, keepdims=True)
        )
        return [jnp.exp2((part - row_max) * FACTOR).astype(BF16) for part in (past, own)]

    def settle(pair, weights):
        total = jnp.dot(weights[0], kvx_scr[:, columns_of(pair)], preferred_element_type=F32)
        total = total + jnp.dot(
            weights[1], own_ones[:, columns_of(pair)], preferred_element_type=F32
        )
        att_scr[:, pair * PAIR : (pair + 1) * PAIR] = pack_pair(
            total[:row_count], total[row_count:]
        ).astype(BF16)

    pipelined(heads // 2, score, soften, settle)
    copies.start(att_scr, att_ref)
    for copy in started[count + 4 :]:
        copy.wait()
    past_attention(
        projected_ref[:, : heads * HEAD_SIZE],
        projected_ref[:, heads * HEAD_SIZE :],
        column_of(len_ref[...]),
        cache_ref,
        past_scr,
        *past_scrs,
    )
    copies.start(past_scr, past_ref)
    copies.wait()


def slot_kernel(q_hbm, prefix_hbm, out_hbm, q_ref, prefix_ref, out_ref, q_scr, kvx_scr, sems):
    copies, started = fetch((q_hbm, prefix_hbm), (q_ref, prefix_ref), sems)
    started[0].wait()
    slots, width = q_ref.shape
    heads = width // HEAD_SIZE
    queries = q_ref[...]
    for head in range(heads):
        q_scr[head] = head_query(queries, head)
    started[1].wait()
    kvx_scr[...] = ones_for_keys(prefix_ref[...])
    lanes = lane_ids((slots, PAIR))
    sums = [jnp.zeros((slots, PAIR), F32)]
    even = []

    def columns_of(head):
        kv = head // QUERIES_PER_KEY
        return slice(kv * PAIR, (kv + 1) * PAIR)

    def score(head):
        return scores_of(q_scr[head], prefix_ref[:, columns_of(head)])

    def soften(head, scores):
        row_max = jnp.max(scores, axis=1, keepdims=True)
        return row_max, jnp.exp2((scores - row_max) * FACTOR).astype(BF16)

    def settle(head, pending):
        row_max, weights = pending
        total = jnp.dot(weights, kvx_scr[:, columns_of(head)], preferred_element_type=F32)
        log_sum = row_max * FACTOR + jnp.log2(total)
        high = log_sum.astype(BF16).astype(F32)
        middle = (log_sum - high).astype(BF16).astype(F32)
        low = log_sum - high - middle
        for place, part in enumerate((high, middle, low)):
            sums[0] = jnp.where(lanes == 3 * head + place, part, sums[0])
        if head % 2 == 0:
            even.append(total)
            return
        at = slice((head - 1) * HEAD_SIZE, (head + 1) * HEAD_SIZE)
        out_ref[:, at] = pack_pair(even[-1], total).astype(BF16)
        copies.start(out_ref.at[:, at], out_hbm.at[:, at])

    pipelined(heads, score, soften, settle)
    out_ref[:, width:] = sums[0].astype(BF16)
    copies.start(out_ref.at[:, width:], out_hbm.at[:, width:])
    copies.wait()


def merge_kernel(per_peer, *refs):
    sources, att_ref, held, (att_scr, sems) = refs[:3], refs[3], refs[4:7], refs[7:]
    copies, started = fetch(sources, held, sems)
    target_ref, back_ref, past_ref = held
    for copy in started:
        copy.wait()
    slot_column, _ = slot_places(target_ref[...], per_peer)
    gather = lane_ids((slot_column.shape[0], back_ref.shape[0])) == slot_column
    width = past_ref.shape[1] - PAIR
    heads = width // HEAD_SIZE
    prefix = jnp.dot(gather.astype(BF16), back_ref[...], preferred_element_type=F32)
    prefix_sums = prefix[:, width:]
    past_sums = past_ref[:, width:]
    lanes = lane_ids(past_sums.shape)
    shares = []
    for head in range(heads):
        prefix_log = jnp.sum(
            jnp.where(lanes // 3 == head, prefix_sums, 0.0), axis=1, keepdims=True
        )
        past_log = jnp.sum(jnp.where(lanes == head, past_sums, 0.0), axis=1, keepdims=True)
        top = jnp.maximum(prefix_log, past_log)
        prefix_part = jnp.exp2(prefix_log - top)
        past_part = jnp.exp2(past_log - top)
        both = prefix_part + past_part
        shares.append((prefix_part / both, past_part / both))
    for pair in range(heads // 2):
        at = slice(pair * PAIR, (pair + 1) * PAIR)
        key_half = lanes < HEAD_SIZE
        prefix_share = jnp.where(key_half, shares[2 * pair][0], shares[2 * pair + 1][0])
        past_share = jnp.where(key_half, shares[2 * pair][1], shares[2 * pair + 1][1])
        att_scr[:, at] = (prefix_share * prefix[:, at] + past_share * past_ref[:, at]).astype(BF16)
    copies.start(att_scr, att_ref)
    copies.wait()


def mlp_kernel(count, blocks, place_ref, *refs):
    inputs = 2 * count + 1
    groups = count
    weight_count = groups + 3
    sources, refs = refs[:inputs], refs[inputs:]
    weight_refs, refs = refs[: blocks + 3], refs[blocks + 3 :]
    outs = 3 if count == 2 else 2
    out_refs, held_refs, refs = refs[:outs], refs[outs : outs + weight_count], refs[outs + weight_count :]
    held, out_scr, sems = refs[:inputs], refs[inputs : inputs + outs], refs[inputs + outs]
    copies, started = fetch(sources, held, sems)
    w_outs, (w_gate, w_up, w_down) = held_refs[:groups], held_refs[groups:]
    hidden_width = w_gate.shape[1]
    chunks = [
        pl.ds(start, min(CHUNK, hidden_width - start)) for start in range(0, hidden_width, CHUNK)
    ]
    if blocks == groups:
        outs_in = [[copies.start(weight_refs[i], w_outs[i])] for i in range(groups)]
    else:
        outs_in = [
            [copies.start(weight_refs[0], w_outs[0])],
            start_pieces(copies, place_ref, weight_refs[1:blocks], w_outs[1]),
        ]
    weight_refs = weight_refs[blocks:]
    columns = [
        [
            copies.start(weight_refs[i].at[:, at], (w_gate, w_up)[i].at[:, at])
            for i in range(2)
        ]
        for at in chunks
    ]
    downs = [copies.start(weight_refs[2].at[at], w_down.at[at]) for at in chunks]
    copies.flying = []
    for copy in started:
        copy.wait()
    rows = in_order(place_ref, [ref[...] for ref in held[:count]]).astype(F32)
    width = rows.shape[1] // count
    mixed = None
    for i in range(groups):
        for copy in outs_in[i]:
            copy.wait()
        term = jnp.dot(held[count + i][...], w_outs[i][...], preferred_element_type=F32)
        term = term.astype(BF16).astype(F32)
        mixed = term if mixed is None else mixed + term
    residual = (rows + mixed).astype(BF16)
    normed = rms_norm(residual.astype(F32), held[2 * count][...])
    if count == 2:
        first = place_ref[0] == 0
        out_scr[2][...] = jnp.where(first, residual[:, :width], residual[:, width:])
        copies.start(out_scr[2], out_refs[2])
    else:
        out_scr[1][...] = residual
        copies.start(out_scr[1], out_refs[1])
    hidden = []
    for i, at in enumerate(chunks):
        columns[i][0].wait()
        columns[i][1].wait()
        gate_act = jnp.dot(normed, w_gate[:, at], preferred_element_type=F32)
        up_act = jnp.dot(normed, w_up[:, at], preferred_element_type=F32)
        hidden.append((gate_act / (1.0 + jnp.exp(-gate_act)) * up_act).astype(BF16))
    for copy in downs:
        copy.wait()
    hidden = jnp.concatenate(hidden, axis=1)
    terms = jnp.dot(hidden, w_down[...], preferred_element_type=F32).astype(BF16)
    if count == 2:
        out_scr[0][...] = jnp.where(first, terms[:, :width], terms[:, width:])
        out_scr[1][...] = jnp.where(first, terms[:, width:], terms[:, :width])
        copies.start(out_scr[0], out_refs[0])
        copies.start(out_scr[1], out_refs[1])
    else:
        out_scr[0][...] = terms
        copies.start(out_scr[0], out_refs[0])
    copies.wait()


def load_kernel(*refs):
    count = len(refs) // 2
    _, started = fetch(refs[:count], refs[count : 2 * count], refs[-1])
    for copy in started:
        copy.wait()


def load(limit, *arrays):
    return pl.pallas_call(
        load_kernel,
        in_specs=[ANY] * len(arrays),
        out_specs=[HELD] * len(arrays),
        out_shape=[jax.ShapeDtypeStruct(x.shape, x.dtype) for x in arrays],
        scratch_shapes=[pltpu.SemaphoreType.DMA((len(arrays),))],
        compiler_params=params(limit),
        cost_estimate=cost(0, sum(2 * x.size for x in arrays)),
        name="load",
    )(*arrays)


def start_pieces(copies, place_ref, pieces, target):
    rows = pieces[0].shape[0]
    odd = place_ref[1]
    starts = (2 * odd, 2 * odd + 1, 2 * (1 - odd), 2 * (1 - odd) + 1)
    return [
        copies.start(piece, target.at[pl.ds(start * rows, rows)])
        for piece, start in zip(pieces, starts)
    ]


def tail_kernel(place_ref, *refs):
    w_gate, sources, pieces, w_up_hbm, w_down_hbm = refs[0], refs[1:7], refs[7:11], refs[11], refs[12]
    send_ref, hidden_ref, residual_ref = refs[13:16]
    held, (w_out_other, w_up, w_down, send_scr, sems) = refs[16:22], refs[22:]
    own_ref, other_ref, gain_ref, att_ref, att_other_ref, w_out_ref = held
    width = send_scr.shape[1]
    hidden_width = w_gate.shape[1]
    away = pl.ds(pl.multiple_of((1 - place_ref[0]) * width, width), width)
    copies, started = fetch(sources, held, sems)
    arriving = start_pieces(copies, place_ref, pieces, w_out_other)
    chunks = [
        pl.ds(start, min(CHUNK, hidden_width - start)) for start in range(0, hidden_width, CHUNK)
    ]
    ups = [copies.start(w_up_hbm.at[:, at], w_up.at[:, at]) for at in chunks]
    downs = [copies.start(w_down_hbm.at[at, away], w_down.at[at]) for at in chunks]
    copies.flying = []
    for copy in started:
        copy.wait()
    rows = in_order(place_ref, [own_ref[...], other_ref[...]]).astype(F32)
    mixed = jnp.dot(att_ref[...], w_out_ref[...], preferred_element_type=F32)
    for copy in arriving:
        copy.wait()
    mixed_other = jnp.dot(att_other_ref[...], w_out_other[...], preferred_element_type=F32)
    mixed = mixed.astype(BF16).astype(F32) + mixed_other.astype(BF16).astype(F32)
    residual = (rows + mixed).astype(BF16)
    normed = rms_norm(residual.astype(F32), gain_ref[...])
    residual_ref[...] = jnp.where(place_ref[0] == 0, residual[:, :width], residual[:, width:])
    hidden = []
    for at, copy in zip(chunks, ups):
        gate_act = jnp.dot(normed, w_gate[:, at], preferred_element_type=F32)
        copy.wait()
        up_act = jnp.dot(normed, w_up[:, at], preferred_element_type=F32)
        hidden.append((gate_act / (1.0 + jnp.exp(-gate_act)) * up_act).astype(BF16))
    hidden = jnp.concatenate(hidden, axis=1)
    hidden_ref[...] = hidden
    split = chunks[-1].start
    for copy in downs[:-1]:
        copy.wait()
    total = jnp.dot(hidden[:, :split], w_down[:split], preferred_element_type=F32)
    downs[-1].wait()
    total += jnp.dot(hidden[:, split:], w_down[split:], preferred_element_type=F32)
    send_scr[...] = total.astype(BF16)
    copies.start(send_scr, send_ref)
    copies.wait()


def keep_kernel(place_ref, hidden_ref, residual_ref, w_down_hbm, out_ref, w_down, sems):
    width = out_ref.shape[1]
    own = pl.ds(pl.multiple_of(place_ref[0] * width, width), width)
    copies = Copies(sems)
    copies.start(w_down_hbm.at[:, own], w_down)
    copies.wait()
    term = jnp.dot(hidden_ref[...], w_down[...], preferred_element_type=F32).astype(BF16)
    out_ref[...] = residual_ref[...].astype(F32) + term.astype(F32)


def tail(place, parts, attended, gain, w_outs, w_gate, w_up, w_down):
    attended, w_gate = lax.optimization_barrier((attended, w_gate))
    rows, width = parts[0].shape
    hidden = w_up.shape[1]
    held = load(TAIL_VMEM, w_gate)
    sources = (*parts, gain, *swap(attended, 2), w_outs[0])
    half = jax.ShapeDtypeStruct((rows, width), BF16)
    units = jax.ShapeDtypeStruct((rows, hidden), BF16)
    half_down = pltpu.VMEM((hidden, width), BF16)
    send, units, residual = pl.pallas_call(
        tail_kernel,
        in_specs=[SCALAR, HELD] + [ANY] * (len(sources) + 6),
        out_specs=[HBM, HELD, HELD],
        out_shape=[half, units, half],
        scratch_shapes=scratch_like(*sources, w_outs[0], w_up)
        + [
            half_down,
            pltpu.VMEM((rows, width), BF16),
            pltpu.SemaphoreType.DMA((12 + 2 * -(-hidden // CHUNK),)),
        ],
        compiler_params=params(TAIL_VMEM),
        cost_estimate=cost(10 * rows * width * hidden, 6 * width * hidden, rows * hidden),
        name="tail",
    )(place, *held, *sources, *w_outs[1:], w_up, w_down)
    kept = pl.pallas_call(
        keep_kernel,
        in_specs=[SCALAR] + [HELD] * 2 + [ANY],
        out_specs=HELD,
        out_shape=jax.ShapeDtypeStruct((rows, width), F32),
        scratch_shapes=[half_down, pltpu.SemaphoreType.DMA((1,))],
        compiler_params=params(TAIL_VMEM),
        cost_estimate=cost(2 * rows * width * hidden, 2 * width * hidden),
        name="keep",
    )(place, units, residual, w_down)
    other = lax.ppermute(send, "tensor", [(0, 1), (1, 0)])
    return (kept + other.astype(F32)).astype(BF16)


def swap(block, count):
    if count == 2:
        return [block, lax.ppermute(block, "tensor", [(0, 1), (1, 0)])]
    if count == 1:
        return [block]
    gathered = lax.all_gather(block, "tensor", axis=0, tiled=False)
    return [gathered[i] for i in range(count)]


def share_rows(block, count, replicas, after):
    if count != 2 or replicas % 2:
        return swap(block, count), after
    half = block.shape[0] // 2
    odd = lax.axis_index("replica") % 2
    mine = lax.dynamic_slice_in_dim(block, odd * half, half, axis=0)
    pieces = (mine[: half // 2], mine[half // 2 :])
    pieces, after = lax.optimization_barrier((pieces, after))
    return [lax.ppermute(piece, "tensor", [(0, 1), (1, 0)]) for piece in pieces], after


def pass_rows(fetched, replicas):
    return lax.ppermute(fetched, "replica", [(i, i ^ 1) for i in range(replicas)])


def finish(place, parts, attended, gain, w_outs, *weights):
    count = len(parts)
    rows = parts[0].shape[0]
    model = sum(part.shape[1] for part in parts)
    hidden = weights[-1].shape[0]
    width = model // count
    if count == 2:
        outs = [jax.ShapeDtypeStruct((rows, width), BF16)] * 3
    else:
        outs = [jax.ShapeDtypeStruct((rows, model), BF16)] * 2
    operands = (*parts, *attended, gain)
    copies = len(operands) + len(w_outs) + 3 * (-(-hidden // CHUNK)) + len(outs)
    held = [pltpu.VMEM(w.shape, w.dtype) for w in [w_outs[0]] * count + list(weights)]
    return pl.pallas_call(
        functools.partial(mlp_kernel, count, len(w_outs)),
        in_specs=[SCALAR] + [ANY] * (len(operands) + len(w_outs) + len(weights)),
        out_specs=[HBM] * len(outs),
        out_shape=outs,
        scratch_shapes=held
        + scratch_like(*operands, *outs)
        + [pltpu.SemaphoreType.DMA((copies,))],
        compiler_params=params(),
        cost_estimate=cost(FILL * 6 * rows * model * hidden, 6 * model * hidden, rows * hidden),
        name="mlp",
    )(place, *operands, *w_outs, *weights)


def exchange(terms, count):
    if count == 2:
        keep, send, residual = terms
        other = lax.ppermute(send, "tensor", [(0, 1), (1, 0)])
        summed = keep.astype(F32) + other.astype(F32)
        return (residual.astype(F32) + summed).astype(BF16)
    terms, residual = terms
    width = terms.shape[1] // count
    summed = lax.psum_scatter(terms.astype(F32), "tensor", scatter_dimension=1, tiled=True)
    own = lax.dynamic_slice_in_dim(residual, lax.axis_index("tensor") * width, width, axis=1)
    return (own.astype(F32) + summed).astype(BF16)


def body(
    prompt_rows,
    request_rows,
    request_keyval_cache,
    cache_len,
    destination,
    prefix_cache,
    attn_gain,
    w_query,
    keyval_weight,
    w_out,
    mlp_gain,
    w_gate,
    w_up,
    w_down,
):
    count = lax.axis_size("tensor")
    replicas = lax.axis_size("replica")
    place = jnp.stack((lax.axis_index("tensor"), lax.axis_index("replica") % 2)).astype(jnp.int32)
    requests = request_rows.shape[0]
    prompts = prompt_rows.shape[0]
    model = w_query.shape[0]
    width = w_query.shape[1]
    kv_width = keyval_weight.shape[1]
    heads = width // HEAD_SIZE
    prefix_len = prefix_cache.shape[0]
    attn_gain = attn_gain.reshape(1, model)
    mlp_gain = mlp_gain.reshape(1, model)

    request_parts = swap(request_rows, count)

    per_peer = 2 * requests // replicas
    slots = replicas * per_peer
    target = destination.reshape(1, requests)
    cached = request_keyval_cache.shape[1]
    w_outs, prompt_rows = share_rows(w_out, count, replicas, prompt_rows)
    prompt_parts = swap(prompt_rows, count)
    operands = (*request_parts, attn_gain, target)
    held = load(REQUEST_VMEM, w_query, keyval_weight)
    outs = [
        jax.ShapeDtypeStruct((slots, width), BF16),
        jax.ShapeDtypeStruct((requests, width + kv_width), BF16),
    ]
    send, projected = pl.pallas_call(
        functools.partial(request_kernel, count, per_peer),
        in_specs=[SCALAR, HELD, HELD] + [ANY] * len(operands),
        out_specs=[HBM] * 2,
        out_shape=outs,
        scratch_shapes=scratch_like(*operands, *outs)
        + [pltpu.SemaphoreType.DMA((len(operands) + 3,))],
        compiler_params=params(REQUEST_VMEM),
        cost_estimate=cost(0, 0),
        name="request_project",
    )(place, *held, *operands)

    slot_queries = lax.all_to_all(send, "replica", split_axis=0, concat_axis=0, tiled=True)

    operands = (
        *prompt_parts,
        attn_gain,
        w_query,
        keyval_weight,
        prefix_cache,
        projected,
        cache_len.reshape(1, requests),
        request_keyval_cache,
    )
    outs = [
        jax.ShapeDtypeStruct((prompts, width), BF16),
        jax.ShapeDtypeStruct((requests, width + PAIR), F32),
    ]
    blocks = (requests // GROUP, heads * GROUP)
    prompt_attended, past = pl.pallas_call(
        functools.partial(prompt_kernel, count),
        in_specs=[SCALAR] + [ANY] * len(operands),
        out_specs=[HBM] * 2,
        out_shape=outs,
        scratch_shapes=scratch_like(*operands)
        + [
            pltpu.VMEM((heads, prompts, PAIR), BF16),
            pltpu.VMEM((prefix_len, kv_width), BF16),
        ]
        + scratch_like(*outs)
        + [
            pltpu.VMEM((*blocks, kv_width), F32),
            pltpu.VMEM((*blocks, GROUP * cached), F32),
            pltpu.VMEM((*blocks, GROUP * cached), BF16),
            pltpu.VMEM((*blocks, kv_width), F32),
            pltpu.SemaphoreType.DMA((len(operands) + 2,)),
        ],
        compiler_params=params(),
        cost_estimate=cost(
            FILL * (2 * prompts * model * (width + kv_width)) + 4 * prompts * heads * prefix_len * PAIR,
            2 * model * (width + kv_width) + 2 * prefix_len * kv_width,
            prompts * heads * prefix_len,
        ),
        name="prompt_attention",
    )(place, *operands)

    prompt_attended = swap(prompt_attended, count)
    slot_queries, prompt_attended[0], w_outs[0] = lax.optimization_barrier(
        (slot_queries, prompt_attended[0], w_outs[0])
    )
    passed = [pass_rows(w_outs[0], replicas)] if count == 2 else []
    slot_out = pl.pallas_call(
        slot_kernel,
        in_specs=[ANY, HBM],
        out_specs=HBM,
        out_shape=jax.ShapeDtypeStruct((slots, width + PAIR), BF16),
        scratch_shapes=scratch_like(slot_queries, prefix_cache)
        + [
            pltpu.VMEM((slots, width + PAIR), BF16),
            pltpu.VMEM((heads, slots, PAIR), BF16),
            pltpu.VMEM((prefix_len, kv_width), BF16),
            pltpu.SemaphoreType.DMA((3 + heads // 2,)),
        ],
        compiler_params=params(),
        cost_estimate=cost(
            4 * slots * heads * prefix_len * PAIR,
            2 * prefix_len * kv_width,
            slots * heads * prefix_len,
        ),
        name="slot_attention",
    )(slot_queries, prefix_cache)

    slot_out, w_outs = lax.optimization_barrier((slot_out, w_outs))
    if count == 2:
        w_outs = [w_out, *w_outs, *passed, pass_rows(w_outs[1], replicas)]
    back = lax.all_to_all(slot_out, "replica", split_axis=0, concat_axis=0, tiled=True)

    weights = (mlp_gain, w_outs, w_gate, w_up, w_down)
    prompt_terms = finish(place, prompt_parts, prompt_attended, *weights)
    back, prompt_terms = lax.optimization_barrier((back, prompt_terms))
    operands = (target, back, past)
    request_attended = pl.pallas_call(
        functools.partial(merge_kernel, per_peer),
        in_specs=[ANY] * len(operands),
        out_specs=HBM,
        out_shape=jax.ShapeDtypeStruct((requests, width), BF16),
        scratch_shapes=scratch_like(*operands)
        + [pltpu.VMEM((requests, width), BF16), pltpu.SemaphoreType.DMA((4,))],
        compiler_params=params(MERGE_VMEM),
        cost_estimate=cost(4 * requests * slots * width, 4 * slots * width),
        name="merge",
    )(*operands)

    if count == 2:
        request_out = tail(place, request_parts, request_attended, *weights)
    else:
        request_out = exchange(
            finish(place, request_parts, swap(request_attended, count), *weights), count
        )
    return (exchange(prompt_terms, count), request_out)


def solution(mesh):
    return jax.shard_map(
        body,
        mesh=mesh,
        in_specs=(
            P("replica", "tensor"),
            P("replica", "tensor"),
            P("replica", None, "tensor"),
            P("replica"),
            P("replica", None),
            P("replica", "tensor"),
            P(),
            P(None, "tensor"),
            P(None, "tensor"),
            P("tensor", None),
            P(),
            P(None, "tensor"),
            P(None, "tensor"),
            P("tensor", None),
        ),
        out_specs=(P("replica", "tensor"), P("replica", "tensor")),
        check_vma=False,
    )
```

```python
import functools
import math

import jax
import jax.numpy as jnp
from jax import lax
from jax.experimental import pallas as pl
from jax.experimental.pallas import tpu as pltpu
from jax.sharding import PartitionSpec as P

HEAD_SIZE = 64
QUERIES_PER_KEY = 4
PAIR = 2 * HEAD_SIZE
GROUP = 8
CHUNK = 256
FILL = 32
EPS = 1e-05
FACTOR = HEAD_SIZE ** (-0.5) * math.log2(math.e)
F32 = jnp.float32
BF16 = jnp.bfloat16
MIB = 1024 * 1024
MOST_VMEM = 61 * MIB
MLP_VMEM = 60 * MIB
REQUEST_VMEM = 40 * MIB
SLOT_VMEM = 48 * MIB
TAIL_VMEM = 40 * MIB
MERGE_VMEM = 40 * MIB
ANY = pl.BlockSpec(memory_space=pl.ANY)
HBM = pl.BlockSpec(memory_space=pltpu.HBM)
HELD = pl.BlockSpec(memory_space=pltpu.VMEM)
SCALAR = pl.BlockSpec(memory_space=pltpu.SMEM)


def params(limit=MOST_VMEM):
    return pltpu.CompilerParams(vmem_limit_bytes=limit)


def cost(flops, read, exps=0):
    return pl.CostEstimate(flops=int(flops), bytes_accessed=int(read), transcendentals=int(exps))


def lane_ids(shape):
    return lax.broadcasted_iota(jnp.int32, shape, len(shape) - 1)


def rms_norm(values, gain_row):
    inv_scale = lax.rsqrt(jnp.mean(values * values, axis=1, keepdims=True) + EPS)
    return (values * inv_scale * gain_row).astype(BF16)


def in_order(place_ref, parts):
    if len(parts) == 2:
        first = place_ref[0] == 0
        own, other = parts
        parts = (jnp.where(first, own, other), jnp.where(first, other, own))
    return jnp.concatenate(parts, axis=1)


def column_of(row):
    shape = (row.shape[1], row.shape[1])
    rows = lax.broadcasted_iota(jnp.int32, shape, 0)
    return jnp.sum(
        jnp.where(rows == lane_ids(shape), jnp.broadcast_to(row, shape), 0), axis=1, keepdims=True
    )


def slot_places(target_row, per_peer):
    count = target_row.shape[1]
    target_column = column_of(target_row)
    shape = (count, count)
    rows, columns = lax.broadcasted_iota(jnp.int32, shape, 0), lane_ids(shape)
    same = (target_column == target_row).astype(jnp.int32)
    column = target_column * per_peer + jnp.sum(
        jnp.where(columns < rows, same, 0), axis=1, keepdims=True
    )
    row = target_row * per_peer + jnp.sum(
        jnp.where(rows < columns, same, 0), axis=0, keepdims=True
    )
    return column, row


def head_query(queries, head):
    pair = head // 2
    block = queries[:, pair * PAIR : (pair + 1) * PAIR].astype(F32)
    if head % 2:
        block = pltpu.roll(block, HEAD_SIZE, 1)
    return jnp.where(lane_ids(block.shape) < HEAD_SIZE, block, 0.0).astype(BF16)


def ones_for_keys(keyval):
    key_half = lane_ids(keyval.shape) % PAIR < HEAD_SIZE
    return jnp.where(key_half, 1.0, keyval.astype(F32)).astype(BF16)


def scores_of(query_rows, key_rows):
    return lax.dot_general(
        query_rows, key_rows, (((1,), (1,)), ((), ())), preferred_element_type=F32
    )


def pack_pair(even, odd):
    even = even / pltpu.roll(even, HEAD_SIZE, 1)
    odd = odd / pltpu.roll(odd, HEAD_SIZE, 1)
    return jnp.where(
        lane_ids(even.shape) < HEAD_SIZE, pltpu.roll(even, HEAD_SIZE, 1), odd
    )


class Copies:
    def __init__(self, sems):
        self.sems = sems
        self.used = 0
        self.flying = []

    def start(self, source, target):
        copy = pltpu.make_async_copy(source, target, self.sems.at[self.used])
        copy.start()
        self.used += 1
        self.flying.append(copy)
        return copy

    def wait(self):
        for copy in self.flying:
            copy.wait()
        self.flying = []


def fetch(refs, targets, sems):
    copies = Copies(sems)
    for ref, target in zip(refs, targets):
        copies.start(ref, target)
    started, copies.flying = copies.flying, []
    return copies, started


def scratch_like(*arrays):
    return [pltpu.VMEM(x.shape, x.dtype) for x in arrays]


def request_kernel(count, per_peer, place_ref, w_query_ref, *refs):
    inputs = count + 2
    sources, send_ref, refs = refs[:inputs], refs[inputs], refs[inputs + 1 :]
    held, (send_scr, sems) = refs[:inputs], refs[inputs:]
    copies, started = fetch(sources, held, sems)
    gain_ref, target_ref = held[count:]
    for copy in started:
        copy.wait()
    _, slot_row = slot_places(target_ref[...], per_peer)
    spread = lax.broadcasted_iota(jnp.int32, (send_scr.shape[0], slot_row.shape[1]), 0) == slot_row
    rows = in_order(place_ref, [ref[...] for ref in held[:count]])
    normed = rms_norm(rows.astype(F32), gain_ref[...])
    queries = jnp.dot(normed, w_query_ref[...], preferred_element_type=F32).astype(BF16)
    send_scr[...] = jnp.dot(
        spread.astype(BF16), queries, preferred_element_type=F32
    ).astype(BF16)
    copies.start(send_scr, send_ref)
    copies.wait()


def past_attention(queries, keyval, lengths, cache_ref, past_scr, q_scr, score_scr, weight_scr, mixed_scr):
    requests, cached, kv_width = cache_ref.shape
    groups = requests // GROUP
    keys = GROUP * cached
    heads = queries.shape[1] // HEAD_SIZE
    block_rows = heads * GROUP
    q_scr[...] = jnp.zeros_like(q_scr)
    for head in range(heads):
        at = head // QUERIES_PER_KEY * PAIR
        q_scr[:, head * GROUP : (head + 1) * GROUP, at : at + PAIR] = (
            head_query(queries, head).astype(F32).reshape(groups, GROUP, PAIR)
        )
    own = jnp.broadcast_to(
        keyval.astype(F32).reshape(groups, 1, GROUP, kv_width), (groups, heads, GROUP, kv_width)
    ).reshape(groups * block_rows, kv_width)
    own_scores = jnp.sum(
        q_scr[...].reshape(groups * block_rows, kv_width) * own, axis=1, keepdims=True
    )
    owner = lax.broadcasted_iota(jnp.int32, (block_rows, keys), 0) % GROUP
    columns = lane_ids((block_rows, keys))
    position = jnp.where(columns // cached == owner, columns % cached, cached)
    for group in range(groups):
        block = cache_ref[group * GROUP : (group + 1) * GROUP].reshape(keys, kv_width)
        live = position < jnp.concatenate(
            [lengths[group * GROUP : (group + 1) * GROUP]] * heads, axis=0
        )
        score_scr[group] = jnp.where(
            live, scores_of(q_scr[group].astype(BF16), block), -jnp.inf
        )
    scores = score_scr[...].reshape(groups * block_rows, keys)
    row_max = jnp.maximum(jnp.max(scores, axis=1, keepdims=True), own_scores)
    exp_vals = jnp.exp2((scores - row_max) * FACTOR)
    own_exp = jnp.exp2((own_scores - row_max) * FACTOR)
    weight_scr[...] = exp_vals.astype(BF16).reshape(groups, block_rows, keys)
    total = jnp.sum(exp_vals, axis=1, keepdims=True) + own_exp
    log_sum = (row_max * FACTOR + jnp.log2(total)).reshape(groups, block_rows, 1)
    for group in range(groups):
        block = cache_ref[group * GROUP : (group + 1) * GROUP].reshape(keys, kv_width)
        mixed_scr[group] = jnp.dot(weight_scr[group], block, preferred_element_type=F32)
    mixed = mixed_scr[...].reshape(groups * block_rows, kv_width)
    mixed = (mixed + own_exp.astype(BF16).astype(F32) * own) * (1.0 / total)
    mixed = mixed.reshape(groups, block_rows, kv_width)
    lanes = lane_ids((requests, PAIR))
    sums = jnp.zeros((requests, PAIR), F32)
    done = []
    for head in range(heads):
        at = head // QUERIES_PER_KEY * PAIR
        rows_of = slice(head * GROUP, (head + 1) * GROUP)
        done.append(mixed[:, rows_of, at : at + PAIR].reshape(requests, PAIR))
        sums = jnp.where(lanes == head, log_sum[:, rows_of].reshape(requests, 1), sums)
    for pair in range(heads // 2):
        past_scr[:, pair * PAIR : (pair + 1) * PAIR] = jnp.where(
            lanes < HEAD_SIZE, pltpu.roll(done[2 * pair], HEAD_SIZE, 1), done[2 * pair + 1]
        )
    past_scr[:, heads * HEAD_SIZE :] = sums


def pipelined(count, score, soften, settle):
    scores, pending = score(0), None
    for i in range(count):
        following = score(i + 1) if i + 1 < count else None
        weights = soften(i, scores)
        if pending is not None:
            settle(i - 1, pending)
        scores, pending = following, weights
    settle(count - 1, pending)


def prompt_kernel(count, place_ref, *refs):
    inputs = 2 * count + 6
    sources, (att_ref, past_ref), refs = refs[:inputs], refs[inputs : inputs + 2], refs[inputs + 2 :]
    held, (q_scr, kvx_scr, att_scr, past_scr, *past_scrs, sems) = refs[:inputs], refs[inputs:]
    copies, started = fetch(sources, held, sems)
    first = 2 * count + 1
    for copy in started[:first]:
        copy.wait()
    gain_ref, w_query_ref, keyval_weight_ref, prefix_ref, len_ref, cache_ref = held[first - 1 :]
    rows = jnp.concatenate(
        [
            in_order(place_ref, [ref[...] for ref in held[at : at + count]])
            for at in (0, count)
        ],
        axis=0,
    )
    normed = rms_norm(rows.astype(F32), gain_ref[...])
    started[first].wait()
    both_queries = jnp.dot(normed, w_query_ref[...], preferred_element_type=F32).astype(BF16)
    started[first + 1].wait()
    both_keyval = jnp.dot(
        normed, keyval_weight_ref[...], preferred_element_type=F32
    ).astype(BF16)
    started[first + 2].wait()
    prompts = held[0].shape[0]
    queries, keyval = both_queries[:prompts], both_keyval[:prompts]
    heads = queries.shape[1] // HEAD_SIZE
    row_count = queries.shape[0]
    for head in range(heads):
        q_scr[head] = head_query(queries, head)
    kvx_scr[...] = ones_for_keys(prefix_ref[...])
    own_ones = ones_for_keys(keyval)
    row_ids = lax.broadcasted_iota(jnp.int32, (2 * row_count, row_count), 0) % row_count
    visible = lax.broadcasted_iota(jnp.int32, (2 * row_count, row_count), 1) <= row_ids

    def columns_of(pair):
        kv = 2 * pair // QUERIES_PER_KEY
        return slice(kv * PAIR, (kv + 1) * PAIR)

    def score(pair):
        query_rows = q_scr[pl.ds(2 * pair, 2)].reshape(2 * row_count, PAIR)
        past = scores_of(query_rows, prefix_ref[:, columns_of(pair)])
        own = scores_of(query_rows, keyval[:, columns_of(pair)])
        return past, jnp.where(visible, own, -jnp.inf)

    def soften(pair, scores):
        past, own = scores
        row_max = jnp.maximum(
            jnp.max(past, axis=1, keepdims=True), jnp.max(own, axis=1, keepdims=True)
        )
        return [jnp.exp2((part - row_max) * FACTOR).astype(BF16) for part in (past, own)]

    def settle(pair, weights):
        total = jnp.dot(weights[0], kvx_scr[:, columns_of(pair)], preferred_element_type=F32)
        total = total + jnp.dot(
            weights[1], own_ones[:, columns_of(pair)], preferred_element_type=F32
        )
        att_scr[:, pair * PAIR : (pair + 1) * PAIR] = pack_pair(
            total[:row_count], total[row_count:]
        ).astype(BF16)

    pipelined(heads // 2, score, soften, settle)
    copies.start(att_scr, att_ref)
    for copy in started[first + 3 :]:
        copy.wait()
    past_attention(
        both_queries[prompts:],
        both_keyval[prompts:],
        column_of(len_ref[...]),
        cache_ref,
        past_scr,
        *past_scrs,
    )
    copies.start(past_scr, past_ref)
    copies.wait()


def slot_kernel(q_ref, prefix_ref, out_hbm, out_ref, kvx_scr, sems):
    copies = Copies(sems)
    slots, width = q_ref.shape
    heads = width // HEAD_SIZE
    queries = q_ref[...]
    lanes = lane_ids((slots, PAIR))
    sums = [jnp.zeros((slots, PAIR), F32)]
    even = []

    def columns_of(head):
        kv = head // QUERIES_PER_KEY
        return slice(kv * PAIR, (kv + 1) * PAIR)

    def score(head):
        at = columns_of(head)
        if head % QUERIES_PER_KEY == 0:
            kvx_scr[:, at] = ones_for_keys(prefix_ref[:, at])
        return scores_of(head_query(queries, head), prefix_ref[:, at])

    def soften(head, scores):
        row_max = jnp.max(scores, axis=1, keepdims=True)
        return row_max, jnp.exp2((scores - row_max) * FACTOR).astype(BF16)

    def settle(head, pending):
        row_max, weights = pending
        total = jnp.dot(weights, kvx_scr[:, columns_of(head)], preferred_element_type=F32)
        log_sum = row_max * FACTOR + jnp.log2(total)
        high = log_sum.astype(BF16).astype(F32)
        middle = (log_sum - high).astype(BF16).astype(F32)
        low = log_sum - high - middle
        for place, part in enumerate((high, middle, low)):
            sums[0] = jnp.where(lanes == 3 * head + place, part, sums[0])
        if head % 2 == 0:
            even.append(total)
            return
        at = slice((head - 1) * HEAD_SIZE, (head + 1) * HEAD_SIZE)
        out_ref[:, at] = pack_pair(even[-1], total).astype(BF16)
        copies.start(out_ref.at[:, at], out_hbm.at[:, at])

    pipelined(heads, score, soften, settle)
    out_ref[:, width:] = sums[0].astype(BF16)
    copies.start(out_ref.at[:, width:], out_hbm.at[:, width:])
    copies.wait()


def merge_kernel(per_peer, *refs):
    target_ref, back_ref, past_ref, att_ref = refs
    slot_column, _ = slot_places(target_ref[...], per_peer)
    gather = lane_ids((slot_column.shape[0], back_ref.shape[0])) == slot_column
    width = past_ref.shape[1] - PAIR
    heads = width // HEAD_SIZE
    prefix = jnp.dot(gather.astype(BF16), back_ref[...], preferred_element_type=F32)
    prefix_sums = prefix[:, width:]
    past_sums = past_ref[:, width:]
    lanes = lane_ids(past_sums.shape)
    shares = []
    for head in range(heads):
        prefix_log = jnp.sum(
            jnp.where(lanes // 3 == head, prefix_sums, 0.0), axis=1, keepdims=True
        )
        past_log = jnp.sum(jnp.where(lanes == head, past_sums, 0.0), axis=1, keepdims=True)
        top = jnp.maximum(prefix_log, past_log)
        prefix_part = jnp.exp2(prefix_log - top)
        past_part = jnp.exp2(past_log - top)
        both = prefix_part + past_part
        shares.append((prefix_part / both, past_part / both))
    for pair in range(heads // 2):
        at = slice(pair * PAIR, (pair + 1) * PAIR)
        key_half = lanes < HEAD_SIZE
        prefix_share = jnp.where(key_half, shares[2 * pair][0], shares[2 * pair + 1][0])
        past_share = jnp.where(key_half, shares[2 * pair][1], shares[2 * pair + 1][1])
        att_ref[:, at] = (prefix_share * prefix[:, at] + past_share * past_ref[:, at]).astype(BF16)


def apart(hidden, w_down, split, copies):
    for copy in copies[:-1]:
        copy.wait()
    total = None
    if split:
        total = jnp.dot(hidden[:, :split], w_down[:split], preferred_element_type=F32)
    copies[-1].wait()
    last = jnp.dot(hidden[:, split:], w_down[split:], preferred_element_type=F32)
    return last if total is None else total + last


def mlp_kernel(count, blocks, place_ref, *refs):
    inputs = 2 * count + 1
    groups = count
    weight_count = groups + 3
    sources, refs = refs[:inputs], refs[inputs:]
    weight_refs, refs = refs[: blocks + 3], refs[blocks + 3 :]
    outs = 3 if count == 2 else 2
    out_refs, held_refs, refs = refs[:outs], refs[outs : outs + weight_count], refs[outs + weight_count :]
    held, out_scr, sems = refs[:inputs], refs[inputs : inputs + outs], refs[inputs + outs]
    copies, started = fetch(sources, held, sems)
    w_outs, (w_gate, w_up, w_down) = held_refs[:groups], held_refs[groups:]
    hidden_width = w_gate.shape[1]
    chunks = [
        pl.ds(start, min(CHUNK, hidden_width - start)) for start in range(0, hidden_width, CHUNK)
    ]
    if blocks == groups:
        outs_in = [[copies.start(weight_refs[i], w_outs[i])] for i in range(groups)]
    else:
        outs_in = [
            [copies.start(weight_refs[0], w_outs[0])],
            start_pieces(copies, place_ref, weight_refs[1:blocks], w_outs[1]),
        ]
    weight_refs = weight_refs[blocks:]
    columns = [
        [
            copies.start(weight_refs[i].at[:, at], (w_gate, w_up)[i].at[:, at])
            for i in range(2)
        ]
        for at in chunks
    ]
    downs = [copies.start(weight_refs[2].at[at], w_down.at[at]) for at in chunks]
    copies.flying = []
    for copy in started:
        copy.wait()
    rows = in_order(place_ref, [ref[...] for ref in held[:count]]).astype(F32)
    width = rows.shape[1] // count
    mixed = None
    for i in range(groups):
        for copy in outs_in[i]:
            copy.wait()
        term = jnp.dot(held[count + i][...], w_outs[i][...], preferred_element_type=F32)
        term = term.astype(BF16).astype(F32)
        mixed = term if mixed is None else mixed + term
    residual = (rows + mixed).astype(BF16)
    normed = rms_norm(residual.astype(F32), held[2 * count][...])
    if count == 2:
        first = place_ref[0] == 0
        out_scr[2][...] = jnp.where(first, residual[:, :width], residual[:, width:])
        copies.start(out_scr[2], out_refs[2])
    else:
        out_scr[1][...] = residual
        copies.start(out_scr[1], out_refs[1])
    hidden = []
    for i, at in enumerate(chunks):
        columns[i][0].wait()
        columns[i][1].wait()
        gate_act = jnp.dot(normed, w_gate[:, at], preferred_element_type=F32)
        up_act = jnp.dot(normed, w_up[:, at], preferred_element_type=F32)
        hidden.append((gate_act / (1.0 + jnp.exp(-gate_act)) * up_act).astype(BF16))
    hidden = jnp.concatenate(hidden, axis=1)
    terms = apart(hidden, w_down, chunks[-1].start, downs).astype(BF16)
    if count == 2:
        out_scr[0][...] = jnp.where(first, terms[:, :width], terms[:, width:])
        out_scr[1][...] = jnp.where(first, terms[:, width:], terms[:, :width])
        copies.start(out_scr[0], out_refs[0])
        copies.start(out_scr[1], out_refs[1])
    else:
        out_scr[0][...] = terms
        copies.start(out_scr[0], out_refs[0])
    copies.wait()


def load_kernel(*refs):
    count = len(refs) // 2
    _, started = fetch(refs[:count], refs[count : 2 * count], refs[-1])
    for copy in started:
        copy.wait()


def load(limit, *arrays):
    return pl.pallas_call(
        load_kernel,
        in_specs=[ANY] * len(arrays),
        out_specs=[HELD] * len(arrays),
        out_shape=[jax.ShapeDtypeStruct(x.shape, x.dtype) for x in arrays],
        scratch_shapes=[pltpu.SemaphoreType.DMA((len(arrays),))],
        compiler_params=params(limit),
        cost_estimate=cost(0, sum(2 * x.size for x in arrays)),
        name="load",
    )(*arrays)


def start_pieces(copies, place_ref, pieces, target):
    rows = pieces[0].shape[0]
    odd = place_ref[1]
    starts = (2 * odd, 2 * odd + 1, 2 * (1 - odd), 2 * (1 - odd) + 1)
    return [
        copies.start(piece, target.at[pl.ds(start * rows, rows)])
        for piece, start in zip(pieces, starts)
    ]


def tail_kernel(place_ref, *refs):
    w_gate, sources, pieces, w_up_hbm, w_down_hbm = refs[0], refs[1:7], refs[7:11], refs[11], refs[12]
    send_ref, hidden_ref, residual_ref = refs[13:16]
    held, (w_out_other, w_up, w_down, sems) = refs[16:22], refs[22:]
    own_ref, other_ref, gain_ref, att_ref, att_other_ref, w_out_ref = held
    width = send_ref.shape[1]
    hidden_width = w_gate.shape[1]
    away = pl.ds(pl.multiple_of((1 - place_ref[0]) * width, width), width)
    copies, started = fetch(sources, held, sems)
    arriving = start_pieces(copies, place_ref, pieces, w_out_other)
    chunks = [
        pl.ds(start, min(CHUNK, hidden_width - start)) for start in range(0, hidden_width, CHUNK)
    ]
    ups = [copies.start(w_up_hbm.at[:, at], w_up.at[:, at]) for at in chunks]
    downs = [copies.start(w_down_hbm.at[at, away], w_down.at[at]) for at in chunks]
    copies.flying = []
    for copy in started:
        copy.wait()
    rows = in_order(place_ref, [own_ref[...], other_ref[...]]).astype(F32)
    mixed = jnp.dot(att_ref[...], w_out_ref[...], preferred_element_type=F32)
    for copy in arriving:
        copy.wait()
    mixed_other = jnp.dot(att_other_ref[...], w_out_other[...], preferred_element_type=F32)
    mixed = mixed.astype(BF16).astype(F32) + mixed_other.astype(BF16).astype(F32)
    residual = (rows + mixed).astype(BF16)
    normed = rms_norm(residual.astype(F32), gain_ref[...])
    residual_ref[...] = jnp.where(place_ref[0] == 0, residual[:, :width], residual[:, width:])
    hidden = []
    for at, copy in zip(chunks, ups):
        gate_act = jnp.dot(normed, w_gate[:, at], preferred_element_type=F32)
        copy.wait()
        up_act = jnp.dot(normed, w_up[:, at], preferred_element_type=F32)
        hidden.append((gate_act / (1.0 + jnp.exp(-gate_act)) * up_act).astype(BF16))
    hidden = jnp.concatenate(hidden, axis=1)
    hidden_ref[...] = hidden
    send_ref[...] = apart(hidden, w_down, chunks[-1].start, downs).astype(BF16)


def keep_kernel(place_ref, hidden_ref, residual_ref, w_down_hbm, out_ref, w_down, sems):
    width = out_ref.shape[1]
    own = pl.ds(pl.multiple_of(place_ref[0] * width, width), width)
    copies = Copies(sems)
    copies.start(w_down_hbm.at[:, own], w_down)
    copies.wait()
    term = jnp.dot(hidden_ref[...], w_down[...], preferred_element_type=F32).astype(BF16)
    out_ref[...] = residual_ref[...].astype(F32) + term.astype(F32)


def tail(place, parts, attended, gain, w_outs, w_gate, w_up, w_down):
    attended, w_gate = lax.optimization_barrier((attended, w_gate))
    rows, width = parts[0].shape
    hidden = w_up.shape[1]
    held = load(TAIL_VMEM, w_gate)
    sources = (*parts, gain, *swap(attended, 2), w_outs[0])
    half = jax.ShapeDtypeStruct((rows, width), BF16)
    units = jax.ShapeDtypeStruct((rows, hidden), BF16)
    half_down = pltpu.VMEM((hidden, width), BF16)
    send, units, residual = pl.pallas_call(
        tail_kernel,
        in_specs=[SCALAR, HELD] + [ANY] * (len(sources) + 6),
        out_specs=[HELD] * 3,
        out_shape=[half, units, half],
        scratch_shapes=scratch_like(*sources, w_outs[0], w_up)
        + [
            half_down,
            pltpu.SemaphoreType.DMA((12 + 2 * -(-hidden // CHUNK),)),
        ],
        compiler_params=params(TAIL_VMEM),
        cost_estimate=cost(10 * rows * width * hidden, 6 * width * hidden, rows * hidden),
        name="tail",
    )(place, *held, *sources, *w_outs[1:], w_up, w_down)
    kept = pl.pallas_call(
        keep_kernel,
        in_specs=[SCALAR] + [HELD] * 2 + [ANY],
        out_specs=HELD,
        out_shape=jax.ShapeDtypeStruct((rows, width), F32),
        scratch_shapes=[half_down, pltpu.SemaphoreType.DMA((1,))],
        compiler_params=params(TAIL_VMEM),
        cost_estimate=cost(2 * rows * width * hidden, 2 * width * hidden),
        name="keep",
    )(place, units, residual, w_down)
    other = lax.ppermute(send, "tensor", [(0, 1), (1, 0)])
    return (kept + other.astype(F32)).astype(BF16)


def swap(block, count):
    if count == 2:
        return [block, lax.ppermute(block, "tensor", [(0, 1), (1, 0)])]
    if count == 1:
        return [block]
    gathered = lax.all_gather(block, "tensor", axis=0, tiled=False)
    return [gathered[i] for i in range(count)]


def share_rows(block, count, replicas, after):
    if count != 2 or replicas % 2:
        return swap(block, count), after
    half = block.shape[0] // 2
    odd = lax.axis_index("replica") % 2
    mine = lax.dynamic_slice_in_dim(block, odd * half, half, axis=0)
    pieces = (mine[: half // 2], mine[half // 2 :])
    pieces, after = lax.optimization_barrier((pieces, after))
    return [lax.ppermute(piece, "tensor", [(0, 1), (1, 0)]) for piece in pieces], after


def pass_rows(fetched, replicas):
    return lax.ppermute(fetched, "replica", [(i, i ^ 1) for i in range(replicas)])


def finish(place, parts, attended, gain, w_outs, *weights):
    count = len(parts)
    rows = parts[0].shape[0]
    model = sum(part.shape[1] for part in parts)
    hidden = weights[-1].shape[0]
    width = model // count
    if count == 2:
        outs = [jax.ShapeDtypeStruct((rows, width), BF16)] * 3
    else:
        outs = [jax.ShapeDtypeStruct((rows, model), BF16)] * 2
    operands = (*parts, *attended, gain)
    copies = len(operands) + len(w_outs) + 3 * (-(-hidden // CHUNK)) + len(outs)
    held = [pltpu.VMEM(w.shape, w.dtype) for w in [w_outs[0]] * count + list(weights)]
    return pl.pallas_call(
        functools.partial(mlp_kernel, count, len(w_outs)),
        in_specs=[SCALAR] + [ANY] * (len(operands) + len(w_outs) + len(weights)),
        out_specs=[HBM] * len(outs),
        out_shape=outs,
        scratch_shapes=held
        + scratch_like(*operands, *outs)
        + [pltpu.SemaphoreType.DMA((copies,))],
        compiler_params=params(MLP_VMEM),
        cost_estimate=cost(FILL * 6 * rows * model * hidden, 6 * model * hidden, rows * hidden),
        name="mlp",
    )(place, *operands, *w_outs, *weights)


def exchange(terms, count):
    if count == 2:
        keep, send, residual = terms
        other = lax.ppermute(send, "tensor", [(0, 1), (1, 0)])
        summed = keep.astype(F32) + other.astype(F32)
        return (residual.astype(F32) + summed).astype(BF16)
    terms, residual = terms
    width = terms.shape[1] // count
    summed = lax.psum_scatter(terms.astype(F32), "tensor", scatter_dimension=1, tiled=True)
    own = lax.dynamic_slice_in_dim(residual, lax.axis_index("tensor") * width, width, axis=1)
    return (own.astype(F32) + summed).astype(BF16)


def body(
    prompt_rows,
    request_rows,
    request_keyval_cache,
    cache_len,
    destination,
    prefix_cache,
    attn_gain,
    w_query,
    keyval_weight,
    w_out,
    mlp_gain,
    w_gate,
    w_up,
    w_down,
):
    count = lax.axis_size("tensor")
    replicas = lax.axis_size("replica")
    place = jnp.stack((lax.axis_index("tensor"), lax.axis_index("replica") % 2)).astype(jnp.int32)
    requests = request_rows.shape[0]
    prompts = prompt_rows.shape[0]
    model = w_query.shape[0]
    width = w_query.shape[1]
    kv_width = keyval_weight.shape[1]
    heads = width // HEAD_SIZE
    prefix_len = prefix_cache.shape[0]
    attn_gain = attn_gain.reshape(1, model)
    mlp_gain = mlp_gain.reshape(1, model)

    request_parts = swap(request_rows, count)

    per_peer = 2 * requests // replicas
    slots = replicas * per_peer
    target = destination.reshape(1, requests)
    cached = request_keyval_cache.shape[1]
    w_outs, prompt_rows = share_rows(w_out, count, replicas, prompt_rows)
    prompt_parts = swap(prompt_rows, count)
    operands = (*request_parts, attn_gain, target)
    slot_rows = jax.ShapeDtypeStruct((slots, width), BF16)
    send = pl.pallas_call(
        functools.partial(request_kernel, count, per_peer),
        in_specs=[SCALAR, HELD] + [ANY] * len(operands),
        out_specs=HBM,
        out_shape=slot_rows,
        scratch_shapes=scratch_like(*operands, slot_rows)
        + [pltpu.SemaphoreType.DMA((len(operands) + 1,))],
        compiler_params=params(REQUEST_VMEM),
        cost_estimate=cost(0, 0),
        name="request_project",
    )(place, *load(REQUEST_VMEM, w_query), *operands)

    slot_queries = lax.all_to_all(send, "replica", split_axis=0, concat_axis=0, tiled=True)

    operands = (
        *prompt_parts,
        *request_parts,
        attn_gain,
        w_query,
        keyval_weight,
        prefix_cache,
        cache_len.reshape(1, requests),
        request_keyval_cache,
    )
    outs = [
        jax.ShapeDtypeStruct((prompts, width), BF16),
        jax.ShapeDtypeStruct((requests, width + PAIR), F32),
    ]
    blocks = (requests // GROUP, heads * GROUP)
    prompt_attended, past = pl.pallas_call(
        functools.partial(prompt_kernel, count),
        in_specs=[SCALAR] + [ANY] * len(operands),
        out_specs=[HBM] * 2,
        out_shape=outs,
        scratch_shapes=scratch_like(*operands)
        + [
            pltpu.VMEM((heads, prompts, PAIR), BF16),
            pltpu.VMEM((prefix_len, kv_width), BF16),
        ]
        + scratch_like(*outs)
        + [
            pltpu.VMEM((*blocks, kv_width), F32),
            pltpu.VMEM((*blocks, GROUP * cached), F32),
            pltpu.VMEM((*blocks, GROUP * cached), BF16),
            pltpu.VMEM((*blocks, kv_width), F32),
            pltpu.SemaphoreType.DMA((len(operands) + 2,)),
        ],
        compiler_params=params(),
        cost_estimate=cost(
            FILL * (2 * prompts * model * (width + kv_width)) + 4 * prompts * heads * prefix_len * PAIR,
            2 * model * (width + kv_width) + 2 * prefix_len * kv_width,
            prompts * heads * prefix_len,
        ),
        name="prompt_attention",
    )(place, *operands)

    prompt_attended = swap(prompt_attended, count)
    slot_queries, prompt_attended[0], w_outs[0] = lax.optimization_barrier(
        (slot_queries, prompt_attended[0], w_outs[0])
    )
    passed = [pass_rows(w_outs[0], replicas)] if count == 2 else []
    slot_out = pl.pallas_call(
        slot_kernel,
        in_specs=[HELD] * 2,
        out_specs=HBM,
        out_shape=jax.ShapeDtypeStruct((slots, width + PAIR), BF16),
        scratch_shapes=[
            pltpu.VMEM((slots, width + PAIR), BF16),
            pltpu.VMEM((prefix_len, kv_width), BF16),
            pltpu.SemaphoreType.DMA((1 + heads // 2,)),
        ],
        compiler_params=params(SLOT_VMEM),
        cost_estimate=cost(
            4 * slots * heads * prefix_len * PAIR,
            2 * prefix_len * kv_width,
            slots * heads * prefix_len,
        ),
        name="slot_attention",
    )(slot_queries, prefix_cache)

    slot_out, w_outs = lax.optimization_barrier((slot_out, w_outs))
    if count == 2:
        w_outs = [w_out, *w_outs, *passed, pass_rows(w_outs[1], replicas)]
    back = lax.all_to_all(slot_out, "replica", split_axis=0, concat_axis=0, tiled=True)

    weights = (mlp_gain, w_outs, w_gate, w_up, w_down)
    prompt_terms = finish(place, prompt_parts, prompt_attended, *weights)
    back, prompt_terms = lax.optimization_barrier((back, prompt_terms))
    operands = (target, back, past)
    request_attended = pl.pallas_call(
        functools.partial(merge_kernel, per_peer),
        in_specs=[HELD] * len(operands),
        out_specs=HELD,
        out_shape=jax.ShapeDtypeStruct((requests, width), BF16),
        compiler_params=params(MERGE_VMEM),
        cost_estimate=cost(4 * requests * slots * width, 4 * slots * width),
        name="merge",
    )(*operands)

    if count == 2:
        request_out = tail(place, request_parts, request_attended, *weights)
    else:
        request_out = exchange(
            finish(place, request_parts, swap(request_attended, count), *weights), count
        )
    return (exchange(prompt_terms, count), request_out)


def solution(mesh):
    return jax.shard_map(
        body,
        mesh=mesh,
        in_specs=(
            P("replica", "tensor"),
            P("replica", "tensor"),
            P("replica", None, "tensor"),
            P("replica"),
            P("replica", None),
            P("replica", "tensor"),
            P(),
            P(None, "tensor"),
            P(None, "tensor"),
            P("tensor", None),
            P(),
            P(None, "tensor"),
            P(None, "tensor"),
            P("tensor", None),
        ),
        out_specs=(P("replica", "tensor"), P("replica", "tensor")),
        check_vma=False,
    )
```

```python
import functools
import math

import jax
import jax.numpy as jnp
from jax import lax
from jax.experimental import pallas as pl
from jax.experimental.pallas import tpu as pltpu
from jax.sharding import PartitionSpec as P

HEAD_SIZE = 64
QUERIES_PER_KEY = 4
PAIR = 2 * HEAD_SIZE
GROUP = 8
CHUNK = 256
FILL = 32
EPS = 1e-05
FACTOR = HEAD_SIZE ** (-0.5) * math.log2(math.e)
F32 = jnp.float32
BF16 = jnp.bfloat16
MIB = 1024 * 1024
MOST_VMEM = 61 * MIB
MLP_VMEM = 60 * MIB
PROMPT_VMEM = 62 * MIB
REQUEST_VMEM = 40 * MIB
SLOT_VMEM = 48 * MIB
TAIL_VMEM = 40 * MIB
MERGE_VMEM = 40 * MIB
ANY = pl.BlockSpec(memory_space=pl.ANY)
HBM = pl.BlockSpec(memory_space=pltpu.HBM)
HELD = pl.BlockSpec(memory_space=pltpu.VMEM)
SCALAR = pl.BlockSpec(memory_space=pltpu.SMEM)


def params(limit=MOST_VMEM):
    return pltpu.CompilerParams(vmem_limit_bytes=limit)


def cost(flops, read, exps=0):
    return pl.CostEstimate(flops=int(flops), bytes_accessed=int(read), transcendentals=int(exps))


def lane_ids(shape):
    return lax.broadcasted_iota(jnp.int32, shape, len(shape) - 1)


def rms_norm(values, gain_row):
    inv_scale = lax.rsqrt(jnp.mean(values * values, axis=1, keepdims=True) + EPS)
    return (values * inv_scale * gain_row).astype(BF16)


def in_order(place_ref, parts):
    if len(parts) == 2:
        first = place_ref[0] == 0
        own, other = parts
        parts = (jnp.where(first, own, other), jnp.where(first, other, own))
    return jnp.concatenate(parts, axis=1)


def column_of(row):
    shape = (row.shape[1], row.shape[1])
    rows = lax.broadcasted_iota(jnp.int32, shape, 0)
    return jnp.sum(
        jnp.where(rows == lane_ids(shape), jnp.broadcast_to(row, shape), 0), axis=1, keepdims=True
    )


def slot_places(target_row, per_peer):
    count = target_row.shape[1]
    target_column = column_of(target_row)
    shape = (count, count)
    rows, columns = lax.broadcasted_iota(jnp.int32, shape, 0), lane_ids(shape)
    same = (target_column == target_row).astype(jnp.int32)
    column = target_column * per_peer + jnp.sum(
        jnp.where(columns < rows, same, 0), axis=1, keepdims=True
    )
    row = target_row * per_peer + jnp.sum(
        jnp.where(rows < columns, same, 0), axis=0, keepdims=True
    )
    return column, row


def head_query(queries, head):
    pair = head // 2
    block = queries[:, pair * PAIR : (pair + 1) * PAIR].astype(F32)
    if head % 2:
        block = pltpu.roll(block, HEAD_SIZE, 1)
    return jnp.where(lane_ids(block.shape) < HEAD_SIZE, block, 0.0).astype(BF16)


def ones_for_keys(keyval):
    key_half = lane_ids(keyval.shape) % PAIR < HEAD_SIZE
    return jnp.where(key_half, 1.0, keyval.astype(F32)).astype(BF16)


def scores_of(query_rows, key_rows):
    return lax.dot_general(
        query_rows, key_rows, (((1,), (1,)), ((), ())), preferred_element_type=F32
    )


def pack_pair(even, odd):
    even = even / pltpu.roll(even, HEAD_SIZE, 1)
    odd = odd / pltpu.roll(odd, HEAD_SIZE, 1)
    return jnp.where(
        lane_ids(even.shape) < HEAD_SIZE, pltpu.roll(even, HEAD_SIZE, 1), odd
    )


class Copies:
    def __init__(self, sems):
        self.sems = sems
        self.used = 0
        self.flying = []

    def start(self, source, target):
        copy = pltpu.make_async_copy(source, target, self.sems.at[self.used])
        copy.start()
        self.used += 1
        self.flying.append(copy)
        return copy

    def wait(self):
        for copy in self.flying:
            copy.wait()
        self.flying = []


def fetch(refs, targets, sems):
    copies = Copies(sems)
    for ref, target in zip(refs, targets):
        copies.start(ref, target)
    started, copies.flying = copies.flying, []
    return copies, started


def scratch_like(*arrays):
    return [pltpu.VMEM(x.shape, x.dtype) for x in arrays]


def request_kernel(count, per_peer, place_ref, w_query_ref, *refs):
    inputs = count + 2
    sources, send_ref, refs = refs[:inputs], refs[inputs], refs[inputs + 1 :]
    held, (send_scr, sems) = refs[:inputs], refs[inputs:]
    copies, started = fetch(sources, held, sems)
    gain_ref, target_ref = held[count:]
    for copy in started:
        copy.wait()
    _, slot_row = slot_places(target_ref[...], per_peer)
    spread = lax.broadcasted_iota(jnp.int32, (send_scr.shape[0], slot_row.shape[1]), 0) == slot_row
    rows = in_order(place_ref, [ref[...] for ref in held[:count]])
    normed = rms_norm(rows.astype(F32), gain_ref[...])
    queries = jnp.dot(normed, w_query_ref[...], preferred_element_type=F32).astype(BF16)
    send_scr[...] = jnp.dot(
        spread.astype(BF16), queries, preferred_element_type=F32
    ).astype(BF16)
    copies.start(send_scr, send_ref)
    copies.wait()


def past_attention(queries, keyval, lengths, cache_ref, past_scr, q_scr, score_scr, weight_scr, mixed_scr):
    requests, cached, kv_width = cache_ref.shape
    groups = requests // GROUP
    keys = GROUP * cached
    heads = queries.shape[1] // HEAD_SIZE
    block_rows = heads * GROUP
    q_scr[...] = jnp.zeros_like(q_scr)
    for head in range(heads):
        at = head // QUERIES_PER_KEY * PAIR
        q_scr[:, head * GROUP : (head + 1) * GROUP, at : at + PAIR] = (
            head_query(queries, head).astype(F32).reshape(groups, GROUP, PAIR)
        )
    own = jnp.broadcast_to(
        keyval.astype(F32).reshape(groups, 1, GROUP, kv_width), (groups, heads, GROUP, kv_width)
    ).reshape(groups * block_rows, kv_width)
    own_scores = jnp.sum(
        q_scr[...].reshape(groups * block_rows, kv_width) * own, axis=1, keepdims=True
    )
    owner = lax.broadcasted_iota(jnp.int32, (block_rows, keys), 0) % GROUP
    columns = lane_ids((block_rows, keys))
    position = jnp.where(columns // cached == owner, columns % cached, cached)
    for group in range(groups):
        block = cache_ref[group * GROUP : (group + 1) * GROUP].reshape(keys, kv_width)
        live = position < jnp.concatenate(
            [lengths[group * GROUP : (group + 1) * GROUP]] * heads, axis=0
        )
        score_scr[group] = jnp.where(
            live, scores_of(q_scr[group].astype(BF16), block), -jnp.inf
        )
    scores = score_scr[...].reshape(groups * block_rows, keys)
    row_max = jnp.maximum(jnp.max(scores, axis=1, keepdims=True), own_scores)
    exp_vals = jnp.exp2((scores - row_max) * FACTOR)
    own_exp = jnp.exp2((own_scores - row_max) * FACTOR)
    weight_scr[...] = exp_vals.astype(BF16).reshape(groups, block_rows, keys)
    total = jnp.sum(exp_vals, axis=1, keepdims=True) + own_exp
    log_sum = (row_max * FACTOR + jnp.log2(total)).reshape(groups, block_rows, 1)
    for group in range(groups):
        block = cache_ref[group * GROUP : (group + 1) * GROUP].reshape(keys, kv_width)
        mixed_scr[group] = jnp.dot(weight_scr[group], block, preferred_element_type=F32)
    mixed = mixed_scr[...].reshape(groups * block_rows, kv_width)
    mixed = (mixed + own_exp.astype(BF16).astype(F32) * own) * (1.0 / total)
    mixed = mixed.reshape(groups, block_rows, kv_width)
    lanes = lane_ids((requests, PAIR))
    sums = jnp.zeros((requests, PAIR), F32)
    done = []
    for head in range(heads):
        at = head // QUERIES_PER_KEY * PAIR
        rows_of = slice(head * GROUP, (head + 1) * GROUP)
        done.append(mixed[:, rows_of, at : at + PAIR].reshape(requests, PAIR))
        sums = jnp.where(lanes == head, log_sum[:, rows_of].reshape(requests, 1), sums)
    for pair in range(heads // 2):
        past_scr[:, pair * PAIR : (pair + 1) * PAIR] = jnp.where(
            lanes < HEAD_SIZE, pltpu.roll(done[2 * pair], HEAD_SIZE, 1), done[2 * pair + 1]
        )
    past_scr[:, heads * HEAD_SIZE :] = sums


def pipelined(count, score, soften, settle):
    scores, pending = score(0), None
    for i in range(count):
        following = score(i + 1) if i + 1 < count else None
        weights = soften(i, scores)
        if pending is not None:
            settle(i - 1, pending)
        scores, pending = following, weights
    settle(count - 1, pending)


def prompt_kernel(count, place_ref, *refs):
    inputs = 2 * count + 6
    sources, (att_ref, past_ref), refs = refs[:inputs], refs[inputs : inputs + 2], refs[inputs + 2 :]
    held, (q_scr, kvx_scr, att_scr, past_scr, *past_scrs, sems) = refs[:inputs], refs[inputs:]
    copies, started = fetch(sources, held, sems)
    first = 2 * count + 1
    for copy in started[:first]:
        copy.wait()
    gain_ref, w_query_ref, keyval_weight_ref, prefix_ref, len_ref, cache_ref = held[first - 1 :]
    rows = jnp.concatenate(
        [
            in_order(place_ref, [ref[...] for ref in held[at : at + count]])
            for at in (0, count)
        ],
        axis=0,
    )
    normed = rms_norm(rows.astype(F32), gain_ref[...])
    started[first].wait()
    both_queries = jnp.dot(normed, w_query_ref[...], preferred_element_type=F32).astype(BF16)
    started[first + 1].wait()
    both_keyval = jnp.dot(
        normed, keyval_weight_ref[...], preferred_element_type=F32
    ).astype(BF16)
    started[first + 2].wait()
    prompts = held[0].shape[0]
    queries, keyval = both_queries[:prompts], both_keyval[:prompts]
    heads = queries.shape[1] // HEAD_SIZE
    row_count = queries.shape[0]
    for head in range(heads):
        q_scr[head] = head_query(queries, head)
    kvx_scr[...] = ones_for_keys(prefix_ref[...])
    own_ones = ones_for_keys(keyval)
    row_ids = lax.broadcasted_iota(jnp.int32, (2 * row_count, row_count), 0) % row_count
    visible = lax.broadcasted_iota(jnp.int32, (2 * row_count, row_count), 1) <= row_ids

    def columns_of(pair):
        kv = 2 * pair // QUERIES_PER_KEY
        return slice(kv * PAIR, (kv + 1) * PAIR)

    def score(pair):
        query_rows = q_scr[pl.ds(2 * pair, 2)].reshape(2 * row_count, PAIR)
        past = scores_of(query_rows, prefix_ref[:, columns_of(pair)])
        own = scores_of(query_rows, keyval[:, columns_of(pair)])
        return past, jnp.where(visible, own, -jnp.inf)

    def soften(pair, scores):
        past, own = scores
        row_max = jnp.maximum(
            jnp.max(past, axis=1, keepdims=True), jnp.max(own, axis=1, keepdims=True)
        )
        return [jnp.exp2((part - row_max) * FACTOR).astype(BF16) for part in (past, own)]

    def settle(pair, weights):
        total = jnp.dot(weights[0], kvx_scr[:, columns_of(pair)], preferred_element_type=F32)
        total = total + jnp.dot(
            weights[1], own_ones[:, columns_of(pair)], preferred_element_type=F32
        )
        att_scr[:, pair * PAIR : (pair + 1) * PAIR] = pack_pair(
            total[:row_count], total[row_count:]
        ).astype(BF16)

    pipelined(heads // 2, score, soften, settle)
    copies.start(att_scr, att_ref)
    for copy in started[first + 3 :]:
        copy.wait()
    past_attention(
        both_queries[prompts:],
        both_keyval[prompts:],
        column_of(len_ref[...]),
        cache_ref,
        past_scr,
        *past_scrs,
    )
    copies.start(past_scr, past_ref)
    copies.wait()


def slot_kernel(q_ref, prefix_ref, out_hbm, out_ref, kvx_scr, sems):
    copies = Copies(sems)
    slots, width = q_ref.shape
    heads = width // HEAD_SIZE
    queries = q_ref[...]
    lanes = lane_ids((slots, PAIR))
    sums = [jnp.zeros((slots, PAIR), F32)]
    even = []

    def columns_of(head):
        kv = head // QUERIES_PER_KEY
        return slice(kv * PAIR, (kv + 1) * PAIR)

    def score(head):
        at = columns_of(head)
        if head % QUERIES_PER_KEY == 0:
            kvx_scr[:, at] = ones_for_keys(prefix_ref[:, at])
        return scores_of(head_query(queries, head), prefix_ref[:, at])

    def soften(head, scores):
        row_max = jnp.max(scores, axis=1, keepdims=True)
        return row_max, jnp.exp2((scores - row_max) * FACTOR).astype(BF16)

    def settle(head, pending):
        row_max, weights = pending
        total = jnp.dot(weights, kvx_scr[:, columns_of(head)], preferred_element_type=F32)
        log_sum = row_max * FACTOR + jnp.log2(total)
        high = log_sum.astype(BF16).astype(F32)
        middle = (log_sum - high).astype(BF16).astype(F32)
        low = log_sum - high - middle
        for place, part in enumerate((high, middle, low)):
            sums[0] = jnp.where(lanes == 3 * head + place, part, sums[0])
        if head % 2 == 0:
            even.append(total)
            return
        at = slice((head - 1) * HEAD_SIZE, (head + 1) * HEAD_SIZE)
        out_ref[:, at] = pack_pair(even[-1], total).astype(BF16)
        copies.start(out_ref.at[:, at], out_hbm.at[:, at])

    pipelined(heads, score, soften, settle)
    out_ref[:, width:] = sums[0].astype(BF16)
    copies.start(out_ref.at[:, width:], out_hbm.at[:, width:])
    copies.wait()


def merge_kernel(per_peer, *refs):
    target_ref, back_ref, past_ref, att_ref = refs
    slot_column, _ = slot_places(target_ref[...], per_peer)
    gather = lane_ids((slot_column.shape[0], back_ref.shape[0])) == slot_column
    width = past_ref.shape[1] - PAIR
    heads = width // HEAD_SIZE
    prefix = jnp.dot(gather.astype(BF16), back_ref[...], preferred_element_type=F32)
    prefix_sums = prefix[:, width:]
    past_sums = past_ref[:, width:]
    lanes = lane_ids(past_sums.shape)
    shares = []
    for head in range(heads):
        prefix_log = jnp.sum(
            jnp.where(lanes // 3 == head, prefix_sums, 0.0), axis=1, keepdims=True
        )
        past_log = jnp.sum(jnp.where(lanes == head, past_sums, 0.0), axis=1, keepdims=True)
        top = jnp.maximum(prefix_log, past_log)
        prefix_part = jnp.exp2(prefix_log - top)
        past_part = jnp.exp2(past_log - top)
        both = prefix_part + past_part
        shares.append((prefix_part / both, past_part / both))
    for pair in range(heads // 2):
        at = slice(pair * PAIR, (pair + 1) * PAIR)
        key_half = lanes < HEAD_SIZE
        prefix_share = jnp.where(key_half, shares[2 * pair][0], shares[2 * pair + 1][0])
        past_share = jnp.where(key_half, shares[2 * pair][1], shares[2 * pair + 1][1])
        att_ref[:, at] = (prefix_share * prefix[:, at] + past_share * past_ref[:, at]).astype(BF16)


def apart(hidden, w_down, split, copies):
    for copy in copies[:-1]:
        copy.wait()
    total = None
    if split:
        total = jnp.dot(hidden[:, :split], w_down[:split], preferred_element_type=F32)
    copies[-1].wait()
    last = jnp.dot(hidden[:, split:], w_down[split:], preferred_element_type=F32)
    return last if total is None else total + last


def mlp_kernel(count, blocks, place_ref, *refs):
    inputs = 2 * count + 1
    groups = count
    weight_count = groups + 3
    sources, refs = refs[:inputs], refs[inputs:]
    weight_refs, refs = refs[: blocks + 3], refs[blocks + 3 :]
    outs = 3 if count == 2 else 2
    out_refs, held_refs, refs = refs[:outs], refs[outs : outs + weight_count], refs[outs + weight_count :]
    held, out_scr, sems = refs[:inputs], refs[inputs : inputs + outs], refs[inputs + outs]
    copies, started = fetch(sources, held, sems)
    w_outs, (w_gate, w_up, w_down) = held_refs[:groups], held_refs[groups:]
    hidden_width = w_gate.shape[1]
    chunks = [
        pl.ds(start, min(CHUNK, hidden_width - start)) for start in range(0, hidden_width, CHUNK)
    ]
    if blocks == groups:
        outs_in = [[copies.start(weight_refs[i], w_outs[i])] for i in range(groups)]
    else:
        outs_in = [
            [copies.start(weight_refs[0], w_outs[0])],
            start_pieces(copies, place_ref, weight_refs[1:blocks], w_outs[1]),
        ]
    weight_refs = weight_refs[blocks:]
    columns = [
        [
            copies.start(weight_refs[i].at[:, at], (w_gate, w_up)[i].at[:, at])
            for i in range(2)
        ]
        for at in chunks
    ]
    downs = [copies.start(weight_refs[2].at[at], w_down.at[at]) for at in chunks]
    copies.flying = []
    for copy in started:
        copy.wait()
    rows = in_order(place_ref, [ref[...] for ref in held[:count]]).astype(F32)
    width = rows.shape[1] // count
    mixed = None
    for i in range(groups):
        for copy in outs_in[i]:
            copy.wait()
        term = jnp.dot(held[count + i][...], w_outs[i][...], preferred_element_type=F32)
        term = term.astype(BF16).astype(F32)
        mixed = term if mixed is None else mixed + term
    residual = (rows + mixed).astype(BF16)
    normed = rms_norm(residual.astype(F32), held[2 * count][...])
    if count == 2:
        first = place_ref[0] == 0
        out_scr[2][...] = jnp.where(first, residual[:, :width], residual[:, width:])
        copies.start(out_scr[2], out_refs[2])
    else:
        out_scr[1][...] = residual
        copies.start(out_scr[1], out_refs[1])
    hidden = []
    for i, at in enumerate(chunks):
        columns[i][0].wait()
        columns[i][1].wait()
        gate_act = jnp.dot(normed, w_gate[:, at], preferred_element_type=F32)
        up_act = jnp.dot(normed, w_up[:, at], preferred_element_type=F32)
        hidden.append((gate_act / (1.0 + jnp.exp(-gate_act)) * up_act).astype(BF16))
    hidden = jnp.concatenate(hidden, axis=1)
    terms = apart(hidden, w_down, chunks[-1].start, downs).astype(BF16)
    if count == 2:
        out_scr[0][...] = jnp.where(first, terms[:, :width], terms[:, width:])
        out_scr[1][...] = jnp.where(first, terms[:, width:], terms[:, :width])
        copies.start(out_scr[0], out_refs[0])
        copies.start(out_scr[1], out_refs[1])
    else:
        out_scr[0][...] = terms
        copies.start(out_scr[0], out_refs[0])
    copies.wait()


def load_kernel(*refs):
    count = len(refs) // 2
    _, started = fetch(refs[:count], refs[count : 2 * count], refs[-1])
    for copy in started:
        copy.wait()


def load(limit, *arrays):
    return pl.pallas_call(
        load_kernel,
        in_specs=[ANY] * len(arrays),
        out_specs=[HELD] * len(arrays),
        out_shape=[jax.ShapeDtypeStruct(x.shape, x.dtype) for x in arrays],
        scratch_shapes=[pltpu.SemaphoreType.DMA((len(arrays),))],
        compiler_params=params(limit),
        cost_estimate=cost(0, sum(2 * x.size for x in arrays)),
        name="load",
    )(*arrays)


def start_pieces(copies, place_ref, pieces, target):
    rows = pieces[0].shape[0]
    odd = place_ref[1]
    starts = (2 * odd, 2 * odd + 1, 2 * (1 - odd), 2 * (1 - odd) + 1)
    return [
        copies.start(piece, target.at[pl.ds(start * rows, rows)])
        for piece, start in zip(pieces, starts)
    ]


def own_share_kernel(att_ref, w_out_ref, term_ref):
    term_ref[...] = jnp.dot(
        att_ref[...], w_out_ref[...], preferred_element_type=F32
    ).astype(BF16)


def tail_kernel(place_ref, *refs):
    w_gate, term_ref, *refs = refs
    sources, pieces, w_up_hbm, w_down_hbm = refs[:4], refs[4:8], refs[8], refs[9]
    send_ref, hidden_ref, residual_ref, *refs = refs[10:]
    held, (w_out_other, w_up, w_down, sems) = refs[:4], refs[4:]
    own_ref, other_ref, gain_ref, att_other_ref = held
    width = send_ref.shape[1]
    hidden_width = w_gate.shape[1]
    away = pl.ds(pl.multiple_of((1 - place_ref[0]) * width, width), width)
    copies, started = fetch(sources, held, sems)
    arriving = start_pieces(copies, place_ref, pieces, w_out_other)
    chunks = [
        pl.ds(start, min(CHUNK, hidden_width - start)) for start in range(0, hidden_width, CHUNK)
    ]
    ups = [copies.start(w_up_hbm.at[:, at], w_up.at[:, at]) for at in chunks]
    downs = [copies.start(w_down_hbm.at[at, away], w_down.at[at]) for at in chunks]
    for copy in started + arriving:
        copy.wait()
    mixed_other = jnp.dot(att_other_ref[...], w_out_other[...], preferred_element_type=F32)
    rows = in_order(place_ref, [own_ref[...], other_ref[...]]).astype(F32)
    mixed = term_ref[...].astype(F32) + mixed_other.astype(BF16).astype(F32)
    residual = (rows + mixed).astype(BF16)
    normed = rms_norm(residual.astype(F32), gain_ref[...])
    residual_ref[...] = jnp.where(place_ref[0] == 0, residual[:, :width], residual[:, width:])
    hidden = []
    for at, copy in zip(chunks, ups):
        gate_act = jnp.dot(normed, w_gate[:, at], preferred_element_type=F32)
        copy.wait()
        up_act = jnp.dot(normed, w_up[:, at], preferred_element_type=F32)
        hidden.append((gate_act / (1.0 + jnp.exp(-gate_act)) * up_act).astype(BF16))
    hidden = jnp.concatenate(hidden, axis=1)
    hidden_ref[...] = hidden
    send_ref[...] = apart(hidden, w_down, chunks[-1].start, downs).astype(BF16)


def keep_kernel(place_ref, hidden_ref, residual_ref, w_down_hbm, out_ref, w_down, sems):
    width = out_ref.shape[1]
    own = pl.ds(pl.multiple_of(place_ref[0] * width, width), width)
    copies = Copies(sems)
    copies.start(w_down_hbm.at[:, own], w_down)
    copies.wait()
    term = jnp.dot(hidden_ref[...], w_down[...], preferred_element_type=F32).astype(BF16)
    out_ref[...] = residual_ref[...].astype(F32) + term.astype(F32)


def tail(place, parts, attended, gain, w_outs, w_gate, w_up, w_down):
    attended, w_gate = lax.optimization_barrier((attended, w_gate))
    rows, width = parts[0].shape
    hidden = w_up.shape[1]
    held = load(TAIL_VMEM, w_gate)
    term = pl.pallas_call(
        own_share_kernel,
        in_specs=[HELD] * 2,
        out_specs=HELD,
        out_shape=jax.ShapeDtypeStruct((rows, 2 * width), BF16),
        compiler_params=params(TAIL_VMEM),
        cost_estimate=cost(4 * rows * width * attended.shape[1], 2 * w_outs[0].size),
        name="own_share",
    )(attended, w_outs[0])
    held = (*held, term)
    sources = (*parts, gain, swap(attended, 2)[1])
    half = jax.ShapeDtypeStruct((rows, width), BF16)
    units = jax.ShapeDtypeStruct((rows, hidden), BF16)
    half_down = pltpu.VMEM((hidden, width), BF16)
    send, units, residual = pl.pallas_call(
        tail_kernel,
        in_specs=[SCALAR, HELD, HELD] + [ANY] * (len(sources) + 6),
        out_specs=[HELD] * 3,
        out_shape=[half, units, half],
        scratch_shapes=scratch_like(*sources, w_outs[0], w_up)
        + [
            half_down,
            pltpu.SemaphoreType.DMA((8 + 2 * -(-hidden // CHUNK),)),
        ],
        compiler_params=params(TAIL_VMEM),
        cost_estimate=cost(10 * rows * width * hidden, 6 * width * hidden, rows * hidden),
        name="tail",
    )(place, *held, *sources, *w_outs[1:], w_up, w_down)
    kept = pl.pallas_call(
        keep_kernel,
        in_specs=[SCALAR] + [HELD] * 2 + [ANY],
        out_specs=HELD,
        out_shape=jax.ShapeDtypeStruct((rows, width), F32),
        scratch_shapes=[half_down, pltpu.SemaphoreType.DMA((1,))],
        compiler_params=params(TAIL_VMEM),
        cost_estimate=cost(2 * rows * width * hidden, 2 * width * hidden),
        name="keep",
    )(place, units, residual, w_down)
    other = lax.ppermute(send, "tensor", [(0, 1), (1, 0)])
    return (kept + other.astype(F32)).astype(BF16)


def swap(block, count):
    if count == 2:
        return [block, lax.ppermute(block, "tensor", [(0, 1), (1, 0)])]
    if count == 1:
        return [block]
    gathered = lax.all_gather(block, "tensor", axis=0, tiled=False)
    return [gathered[i] for i in range(count)]


def share_rows(block, count, replicas, after):
    if count != 2 or replicas % 2:
        return swap(block, count), after
    half = block.shape[0] // 2
    odd = lax.axis_index("replica") % 2
    mine = lax.dynamic_slice_in_dim(block, odd * half, half, axis=0)
    pieces = (mine[: half // 2], mine[half // 2 :])
    pieces, after = lax.optimization_barrier((pieces, after))
    return [lax.ppermute(piece, "tensor", [(0, 1), (1, 0)]) for piece in pieces], after


def pass_rows(fetched, replicas):
    return lax.ppermute(fetched, "replica", [(i, i ^ 1) for i in range(replicas)])


def finish(place, parts, attended, gain, w_outs, *weights):
    count = len(parts)
    rows = parts[0].shape[0]
    model = sum(part.shape[1] for part in parts)
    hidden = weights[-1].shape[0]
    width = model // count
    if count == 2:
        outs = [jax.ShapeDtypeStruct((rows, width), BF16)] * 3
    else:
        outs = [jax.ShapeDtypeStruct((rows, model), BF16)] * 2
    operands = (*parts, *attended, gain)
    copies = len(operands) + len(w_outs) + 3 * (-(-hidden // CHUNK)) + len(outs)
    held = [pltpu.VMEM(w.shape, w.dtype) for w in [w_outs[0]] * count + list(weights)]
    return pl.pallas_call(
        functools.partial(mlp_kernel, count, len(w_outs)),
        in_specs=[SCALAR] + [ANY] * (len(operands) + len(w_outs) + len(weights)),
        out_specs=[HBM] * len(outs),
        out_shape=outs,
        scratch_shapes=held
        + scratch_like(*operands, *outs)
        + [pltpu.SemaphoreType.DMA((copies,))],
        compiler_params=params(MLP_VMEM),
        cost_estimate=cost(FILL * 6 * rows * model * hidden, 6 * model * hidden, rows * hidden),
        name="mlp",
    )(place, *operands, *w_outs, *weights)


def exchange(terms, count):
    if count == 2:
        keep, send, residual = terms
        other = lax.ppermute(send, "tensor", [(0, 1), (1, 0)])
        summed = keep.astype(F32) + other.astype(F32)
        return (residual.astype(F32) + summed).astype(BF16)
    terms, residual = terms
    width = terms.shape[1] // count
    summed = lax.psum_scatter(terms.astype(F32), "tensor", scatter_dimension=1, tiled=True)
    own = lax.dynamic_slice_in_dim(residual, lax.axis_index("tensor") * width, width, axis=1)
    return (own.astype(F32) + summed).astype(BF16)


def body(
    prompt_rows,
    request_rows,
    request_keyval_cache,
    cache_len,
    destination,
    prefix_cache,
    attn_gain,
    w_query,
    keyval_weight,
    w_out,
    mlp_gain,
    w_gate,
    w_up,
    w_down,
):
    count = lax.axis_size("tensor")
    replicas = lax.axis_size("replica")
    place = jnp.stack((lax.axis_index("tensor"), lax.axis_index("replica") % 2)).astype(jnp.int32)
    requests = request_rows.shape[0]
    prompts = prompt_rows.shape[0]
    model = w_query.shape[0]
    width = w_query.shape[1]
    kv_width = keyval_weight.shape[1]
    heads = width // HEAD_SIZE
    prefix_len = prefix_cache.shape[0]
    attn_gain = attn_gain.reshape(1, model)
    mlp_gain = mlp_gain.reshape(1, model)

    request_parts = swap(request_rows, count)

    per_peer = 2 * requests // replicas
    slots = replicas * per_peer
    target = destination.reshape(1, requests)
    cached = request_keyval_cache.shape[1]
    w_outs, prompt_rows = share_rows(w_out, count, replicas, prompt_rows)
    prompt_parts = swap(prompt_rows, count)
    operands = (*request_parts, attn_gain, target)
    slot_rows = jax.ShapeDtypeStruct((slots, width), BF16)
    send = pl.pallas_call(
        functools.partial(request_kernel, count, per_peer),
        in_specs=[SCALAR, HELD] + [ANY] * len(operands),
        out_specs=HBM,
        out_shape=slot_rows,
        scratch_shapes=scratch_like(*operands, slot_rows)
        + [pltpu.SemaphoreType.DMA((len(operands) + 1,))],
        compiler_params=params(REQUEST_VMEM),
        cost_estimate=cost(0, 0),
        name="request_project",
    )(place, *load(REQUEST_VMEM, w_query), *operands)

    slot_queries = lax.all_to_all(send, "replica", split_axis=0, concat_axis=0, tiled=True)

    operands = (
        *prompt_parts,
        *request_parts,
        attn_gain,
        w_query,
        keyval_weight,
        prefix_cache,
        cache_len.reshape(1, requests),
        request_keyval_cache,
    )
    outs = [
        jax.ShapeDtypeStruct((prompts, width), BF16),
        jax.ShapeDtypeStruct((requests, width + PAIR), F32),
    ]
    blocks = (requests // GROUP, heads * GROUP)
    prompt_attended, past = pl.pallas_call(
        functools.partial(prompt_kernel, count),
        in_specs=[SCALAR] + [ANY] * len(operands),
        out_specs=[HBM] * 2,
        out_shape=outs,
        scratch_shapes=scratch_like(*operands)
        + [
            pltpu.VMEM((heads, prompts, PAIR), BF16),
            pltpu.VMEM((prefix_len, kv_width), BF16),
        ]
        + scratch_like(*outs)
        + [
            pltpu.VMEM((*blocks, kv_width), F32),
            pltpu.VMEM((*blocks, GROUP * cached), F32),
            pltpu.VMEM((*blocks, GROUP * cached), BF16),
            pltpu.VMEM((*blocks, kv_width), F32),
            pltpu.SemaphoreType.DMA((len(operands) + 2,)),
        ],
        compiler_params=params(PROMPT_VMEM),
        cost_estimate=cost(
            FILL * (2 * prompts * model * (width + kv_width)) + 4 * prompts * heads * prefix_len * PAIR,
            2 * model * (width + kv_width) + 2 * prefix_len * kv_width,
            prompts * heads * prefix_len,
        ),
        name="prompt_attention",
    )(place, *operands)

    prompt_attended = swap(prompt_attended, count)
    slot_queries, prompt_attended[0], w_outs[0] = lax.optimization_barrier(
        (slot_queries, prompt_attended[0], w_outs[0])
    )
    passed = [pass_rows(w_outs[0], replicas)] if count == 2 else []
    slot_out = pl.pallas_call(
        slot_kernel,
        in_specs=[HELD] * 2,
        out_specs=HBM,
        out_shape=jax.ShapeDtypeStruct((slots, width + PAIR), BF16),
        scratch_shapes=[
            pltpu.VMEM((slots, width + PAIR), BF16),
            pltpu.VMEM((prefix_len, kv_width), BF16),
            pltpu.SemaphoreType.DMA((1 + heads // 2,)),
        ],
        compiler_params=params(SLOT_VMEM),
        cost_estimate=cost(
            4 * slots * heads * prefix_len * PAIR,
            2 * prefix_len * kv_width,
            slots * heads * prefix_len,
        ),
        name="slot_attention",
    )(slot_queries, prefix_cache)

    slot_out, w_outs = lax.optimization_barrier((slot_out, w_outs))
    if count == 2:
        w_outs = [w_out, *w_outs, *passed, pass_rows(w_outs[1], replicas)]
    back = lax.all_to_all(slot_out, "replica", split_axis=0, concat_axis=0, tiled=True)

    weights = (mlp_gain, w_outs, w_gate, w_up, w_down)
    prompt_terms = finish(place, prompt_parts, prompt_attended, *weights)
    back, prompt_terms = lax.optimization_barrier((back, prompt_terms))
    operands = (target, back, past)
    request_attended = pl.pallas_call(
        functools.partial(merge_kernel, per_peer),
        in_specs=[HELD] * len(operands),
        out_specs=HELD,
        out_shape=jax.ShapeDtypeStruct((requests, width), BF16),
        compiler_params=params(MERGE_VMEM),
        cost_estimate=cost(4 * requests * slots * width, 4 * slots * width),
        name="merge",
    )(*operands)

    if count == 2:
        request_out = tail(place, request_parts, request_attended, *weights)
    else:
        request_out = exchange(
            finish(place, request_parts, swap(request_attended, count), *weights), count
        )
    return (exchange(prompt_terms, count), request_out)


def solution(mesh):
    return jax.shard_map(
        body,
        mesh=mesh,
        in_specs=(
            P("replica", "tensor"),
            P("replica", "tensor"),
            P("replica", None, "tensor"),
            P("replica"),
            P("replica", None),
            P("replica", "tensor"),
            P(),
            P(None, "tensor"),
            P(None, "tensor"),
            P("tensor", None),
            P(),
            P(None, "tensor"),
            P(None, "tensor"),
            P("tensor", None),
        ),
        out_specs=(P("replica", "tensor"), P("replica", "tensor")),
        check_vma=False,
    )
```

```python
import functools
import math

import jax
import jax.numpy as jnp
from jax import lax
from jax.experimental import pallas as pl
from jax.experimental.pallas import tpu as pltpu
from jax.sharding import PartitionSpec as P

HEAD_SIZE = 64
QUERIES_PER_KEY = 4
PAIR = 2 * HEAD_SIZE
GROUP = 8
CHUNK = 256
FILL = 32
EPS = 1e-05
FACTOR = HEAD_SIZE ** (-0.5) * math.log2(math.e)
F32 = jnp.float32
BF16 = jnp.bfloat16
MIB = 1024 * 1024
MOST_VMEM = 61 * MIB
MLP_VMEM = 60 * MIB
PROMPT_VMEM = 62 * MIB
REQUEST_VMEM = 40 * MIB
SLOT_VMEM = 48 * MIB
TAIL_VMEM = 40 * MIB
MERGE_VMEM = 40 * MIB
ANY = pl.BlockSpec(memory_space=pl.ANY)
HBM = pl.BlockSpec(memory_space=pltpu.HBM)
HELD = pl.BlockSpec(memory_space=pltpu.VMEM)
SCALAR = pl.BlockSpec(memory_space=pltpu.SMEM)


def params(limit=MOST_VMEM):
    return pltpu.CompilerParams(vmem_limit_bytes=limit)


def cost(flops, read, exps=0):
    return pl.CostEstimate(flops=int(flops), bytes_accessed=int(read), transcendentals=int(exps))


def lane_ids(shape):
    return lax.broadcasted_iota(jnp.int32, shape, len(shape) - 1)


def rms_norm(values, gain_row):
    inv_scale = lax.rsqrt(jnp.mean(values * values, axis=1, keepdims=True) + EPS)
    return (values * inv_scale * gain_row).astype(BF16)


def in_order(place_ref, parts):
    if len(parts) == 2:
        first = place_ref[0] == 0
        own, other = parts
        parts = (jnp.where(first, own, other), jnp.where(first, other, own))
    return jnp.concatenate(parts, axis=1)


def column_of(row):
    shape = (row.shape[1], row.shape[1])
    rows = lax.broadcasted_iota(jnp.int32, shape, 0)
    return jnp.sum(
        jnp.where(rows == lane_ids(shape), jnp.broadcast_to(row, shape), 0), axis=1, keepdims=True
    )


def slot_places(target_row, per_peer):
    count = target_row.shape[1]
    target_column = column_of(target_row)
    shape = (count, count)
    rows, columns = lax.broadcasted_iota(jnp.int32, shape, 0), lane_ids(shape)
    same = (target_column == target_row).astype(jnp.int32)
    column = target_column * per_peer + jnp.sum(
        jnp.where(columns < rows, same, 0), axis=1, keepdims=True
    )
    row = target_row * per_peer + jnp.sum(
        jnp.where(rows < columns, same, 0), axis=0, keepdims=True
    )
    return column, row


def head_query(queries, head):
    pair = head // 2
    block = queries[:, pair * PAIR : (pair + 1) * PAIR].astype(F32)
    if head % 2:
        block = pltpu.roll(block, HEAD_SIZE, 1)
    return jnp.where(lane_ids(block.shape) < HEAD_SIZE, block, 0.0).astype(BF16)


def ones_for_keys(keyval):
    key_half = lane_ids(keyval.shape) % PAIR < HEAD_SIZE
    return jnp.where(key_half, 1.0, keyval.astype(F32)).astype(BF16)


def scores_of(query_rows, key_rows):
    return lax.dot_general(
        query_rows, key_rows, (((1,), (1,)), ((), ())), preferred_element_type=F32
    )


def pack_pair(even, odd):
    even = even / pltpu.roll(even, HEAD_SIZE, 1)
    odd = odd / pltpu.roll(odd, HEAD_SIZE, 1)
    return jnp.where(
        lane_ids(even.shape) < HEAD_SIZE, pltpu.roll(even, HEAD_SIZE, 1), odd
    )


class Copies:
    def __init__(self, sems):
        self.sems = sems
        self.used = 0
        self.flying = []

    def start(self, source, target):
        copy = pltpu.make_async_copy(source, target, self.sems.at[self.used])
        copy.start()
        self.used += 1
        self.flying.append(copy)
        return copy

    def wait(self):
        for copy in self.flying:
            copy.wait()
        self.flying = []


def fetch(refs, targets, sems):
    copies = Copies(sems)
    for ref, target in zip(refs, targets):
        copies.start(ref, target)
    started, copies.flying = copies.flying, []
    return copies, started


def scratch_like(*arrays):
    return [pltpu.VMEM(x.shape, x.dtype) for x in arrays]


def request_kernel(count, per_peer, place_ref, w_query_ref, *refs):
    inputs = count + 2
    sources, send_ref, refs = refs[:inputs], refs[inputs], refs[inputs + 1 :]
    held, (send_scr, sems) = refs[:inputs], refs[inputs:]
    copies, started = fetch(sources, held, sems)
    target_ref, gain_ref = held[:2]
    started[0].wait()
    _, slot_row = slot_places(target_ref[...], per_peer)
    slots, half = send_scr.shape[0], send_scr.shape[0] // 2
    spread = lax.broadcasted_iota(jnp.int32, (slots, slot_row.shape[1]), 0) == slot_row
    spread = spread.astype(BF16)
    for copy in started[1:]:
        copy.wait()
    rows = in_order(place_ref, [ref[...] for ref in held[2:]])
    normed = rms_norm(rows.astype(F32), gain_ref[...])
    queries = jnp.dot(normed, w_query_ref[...], preferred_element_type=F32).astype(BF16)
    for at in (slice(0, half), slice(half, slots)):
        send_scr[at] = jnp.dot(spread[at], queries, preferred_element_type=F32).astype(BF16)
        copies.start(send_scr.at[at], send_ref.at[at])
    copies.wait()


def past_attention(queries, keyval, lengths, cache_ref, past_scr, q_scr, score_scr, weight_scr, mixed_scr):
    requests, cached, kv_width = cache_ref.shape
    groups = requests // GROUP
    keys = GROUP * cached
    heads = queries.shape[1] // HEAD_SIZE
    block_rows = heads * GROUP
    q_scr[...] = jnp.zeros_like(q_scr)
    for head in range(heads):
        at = head // QUERIES_PER_KEY * PAIR
        q_scr[:, head * GROUP : (head + 1) * GROUP, at : at + PAIR] = (
            head_query(queries, head).astype(F32).reshape(groups, GROUP, PAIR)
        )
    own = jnp.broadcast_to(
        keyval.astype(F32).reshape(groups, 1, GROUP, kv_width), (groups, heads, GROUP, kv_width)
    ).reshape(groups * block_rows, kv_width)
    own_scores = jnp.sum(
        q_scr[...].reshape(groups * block_rows, kv_width) * own, axis=1, keepdims=True
    )
    owner = lax.broadcasted_iota(jnp.int32, (block_rows, keys), 0) % GROUP
    columns = lane_ids((block_rows, keys))
    position = jnp.where(columns // cached == owner, columns % cached, cached)
    for group in range(groups):
        block = cache_ref[group * GROUP : (group + 1) * GROUP].reshape(keys, kv_width)
        live = position < jnp.concatenate(
            [lengths[group * GROUP : (group + 1) * GROUP]] * heads, axis=0
        )
        score_scr[group] = jnp.where(
            live, scores_of(q_scr[group].astype(BF16), block), -jnp.inf
        )
    scores = score_scr[...].reshape(groups * block_rows, keys)
    row_max = jnp.maximum(jnp.max(scores, axis=1, keepdims=True), own_scores)
    exp_vals = jnp.exp2((scores - row_max) * FACTOR)
    own_exp = jnp.exp2((own_scores - row_max) * FACTOR)
    weight_scr[...] = exp_vals.astype(BF16).reshape(groups, block_rows, keys)
    total = jnp.sum(exp_vals, axis=1, keepdims=True) + own_exp
    log_sum = (row_max * FACTOR + jnp.log2(total)).reshape(groups, block_rows, 1)
    for group in range(groups):
        block = cache_ref[group * GROUP : (group + 1) * GROUP].reshape(keys, kv_width)
        mixed_scr[group] = jnp.dot(weight_scr[group], block, preferred_element_type=F32)
    mixed = mixed_scr[...].reshape(groups * block_rows, kv_width)
    mixed = (mixed + own_exp.astype(BF16).astype(F32) * own) * (1.0 / total)
    mixed = mixed.reshape(groups, block_rows, kv_width)
    lanes = lane_ids((requests, PAIR))
    sums = jnp.zeros((requests, PAIR), F32)
    done = []
    for head in range(heads):
        at = head // QUERIES_PER_KEY * PAIR
        rows_of = slice(head * GROUP, (head + 1) * GROUP)
        done.append(mixed[:, rows_of, at : at + PAIR].reshape(requests, PAIR))
        sums = jnp.where(lanes == head, log_sum[:, rows_of].reshape(requests, 1), sums)
    for pair in range(heads // 2):
        past_scr[:, pair * PAIR : (pair + 1) * PAIR] = jnp.where(
            lanes < HEAD_SIZE, pltpu.roll(done[2 * pair], HEAD_SIZE, 1), done[2 * pair + 1]
        )
    past_scr[:, heads * HEAD_SIZE :] = sums


def pipelined(count, score, soften, settle):
    scores, pending = score(0), None
    for i in range(count):
        following = score(i + 1) if i + 1 < count else None
        weights = soften(i, scores)
        if pending is not None:
            settle(i - 1, pending)
        scores, pending = following, weights
    settle(count - 1, pending)


def prompt_kernel(count, place_ref, *refs):
    inputs = 2 * count + 6
    sources, (att_ref, past_ref), refs = refs[:inputs], refs[inputs : inputs + 2], refs[inputs + 2 :]
    held, (q_scr, kvx_scr, att_scr, past_scr, *past_scrs, sems) = refs[:inputs], refs[inputs:]
    copies, started = fetch(sources, held, sems)
    first = 2 * count + 1
    for copy in started[:first]:
        copy.wait()
    gain_ref, w_query_ref, keyval_weight_ref, prefix_ref, len_ref, cache_ref = held[first - 1 :]
    rows = jnp.concatenate(
        [
            in_order(place_ref, [ref[...] for ref in held[at : at + count]])
            for at in (0, count)
        ],
        axis=0,
    )
    normed = rms_norm(rows.astype(F32), gain_ref[...])
    started[first].wait()
    both_queries = jnp.dot(normed, w_query_ref[...], preferred_element_type=F32).astype(BF16)
    started[first + 1].wait()
    both_keyval = jnp.dot(
        normed, keyval_weight_ref[...], preferred_element_type=F32
    ).astype(BF16)
    started[first + 2].wait()
    prompts = held[0].shape[0]
    queries, keyval = both_queries[:prompts], both_keyval[:prompts]
    heads = queries.shape[1] // HEAD_SIZE
    row_count = queries.shape[0]
    for head in range(heads):
        q_scr[head] = head_query(queries, head)
    kvx_scr[...] = ones_for_keys(prefix_ref[...])
    own_ones = ones_for_keys(keyval)
    row_ids = lax.broadcasted_iota(jnp.int32, (2 * row_count, row_count), 0) % row_count
    visible = lax.broadcasted_iota(jnp.int32, (2 * row_count, row_count), 1) <= row_ids

    def columns_of(pair):
        kv = 2 * pair // QUERIES_PER_KEY
        return slice(kv * PAIR, (kv + 1) * PAIR)

    def score(pair):
        query_rows = q_scr[pl.ds(2 * pair, 2)].reshape(2 * row_count, PAIR)
        past = scores_of(query_rows, prefix_ref[:, columns_of(pair)])
        own = scores_of(query_rows, keyval[:, columns_of(pair)])
        return past, jnp.where(visible, own, -jnp.inf)

    def soften(pair, scores):
        past, own = scores
        row_max = jnp.maximum(
            jnp.max(past, axis=1, keepdims=True), jnp.max(own, axis=1, keepdims=True)
        )
        return [jnp.exp2((part - row_max) * FACTOR).astype(BF16) for part in (past, own)]

    def settle(pair, weights):
        total = jnp.dot(weights[0], kvx_scr[:, columns_of(pair)], preferred_element_type=F32)
        total = total + jnp.dot(
            weights[1], own_ones[:, columns_of(pair)], preferred_element_type=F32
        )
        att_scr[:, pair * PAIR : (pair + 1) * PAIR] = pack_pair(
            total[:row_count], total[row_count:]
        ).astype(BF16)

    pipelined(heads // 2, score, soften, settle)
    copies.start(att_scr, att_ref)
    for copy in started[first + 3 :]:
        copy.wait()
    past_attention(
        both_queries[prompts:],
        both_keyval[prompts:],
        column_of(len_ref[...]),
        cache_ref,
        past_scr,
        *past_scrs,
    )
    copies.start(past_scr, past_ref)
    copies.wait()


def slot_kernel(q_ref, prefix_ref, out_hbm, out_ref, kvx_scr, sems):
    copies = Copies(sems)
    slots, width = q_ref.shape
    heads = width // HEAD_SIZE
    queries = q_ref[...]
    lanes = lane_ids((slots, PAIR))
    sums = [jnp.zeros((slots, PAIR), F32)]
    even = []

    def columns_of(head):
        kv = head // QUERIES_PER_KEY
        return slice(kv * PAIR, (kv + 1) * PAIR)

    def score(head):
        at = columns_of(head)
        if head % QUERIES_PER_KEY == 0:
            kvx_scr[:, at] = ones_for_keys(prefix_ref[:, at])
        return scores_of(head_query(queries, head), prefix_ref[:, at])

    def soften(head, scores):
        row_max = jnp.max(scores, axis=1, keepdims=True)
        return row_max, jnp.exp2((scores - row_max) * FACTOR).astype(BF16)

    def settle(head, pending):
        row_max, weights = pending
        total = jnp.dot(weights, kvx_scr[:, columns_of(head)], preferred_element_type=F32)
        log_sum = row_max * FACTOR + jnp.log2(total)
        high = log_sum.astype(BF16).astype(F32)
        middle = (log_sum - high).astype(BF16).astype(F32)
        low = log_sum - high - middle
        for place, part in enumerate((high, middle, low)):
            sums[0] = jnp.where(lanes == 3 * head + place, part, sums[0])
        if head % 2 == 0:
            even.append(total)
            return
        at = slice((head - 1) * HEAD_SIZE, (head + 1) * HEAD_SIZE)
        out_ref[:, at] = pack_pair(even[-1], total).astype(BF16)
        copies.start(out_ref.at[:, at], out_hbm.at[:, at])

    pipelined(heads, score, soften, settle)
    out_ref[:, width:] = sums[0].astype(BF16)
    copies.start(out_ref.at[:, width:], out_hbm.at[:, width:])
    copies.wait()


def merge_kernel(per_peer, *refs):
    target_ref, back_ref, past_ref, att_ref = refs
    slot_column, _ = slot_places(target_ref[...], per_peer)
    gather = lane_ids((slot_column.shape[0], back_ref.shape[0])) == slot_column
    width = past_ref.shape[1] - PAIR
    heads = width // HEAD_SIZE
    prefix = jnp.dot(gather.astype(BF16), back_ref[...], preferred_element_type=F32)
    prefix_sums = prefix[:, width:]
    past_sums = past_ref[:, width:]
    lanes = lane_ids(past_sums.shape)
    shares = []
    for head in range(heads):
        prefix_log = jnp.sum(
            jnp.where(lanes // 3 == head, prefix_sums, 0.0), axis=1, keepdims=True
        )
        past_log = jnp.sum(jnp.where(lanes == head, past_sums, 0.0), axis=1, keepdims=True)
        top = jnp.maximum(prefix_log, past_log)
        prefix_part = jnp.exp2(prefix_log - top)
        past_part = jnp.exp2(past_log - top)
        both = prefix_part + past_part
        shares.append((prefix_part / both, past_part / both))
    for pair in range(heads // 2):
        at = slice(pair * PAIR, (pair + 1) * PAIR)
        key_half = lanes < HEAD_SIZE
        prefix_share = jnp.where(key_half, shares[2 * pair][0], shares[2 * pair + 1][0])
        past_share = jnp.where(key_half, shares[2 * pair][1], shares[2 * pair + 1][1])
        att_ref[:, at] = (prefix_share * prefix[:, at] + past_share * past_ref[:, at]).astype(BF16)


def apart(hidden, w_down, split, copies):
    for copy in copies[:-1]:
        copy.wait()
    total = None
    if split:
        total = jnp.dot(hidden[:, :split], w_down[:split], preferred_element_type=F32)
    copies[-1].wait()
    last = jnp.dot(hidden[:, split:], w_down[split:], preferred_element_type=F32)
    return last if total is None else total + last


def mlp_kernel(count, blocks, place_ref, *refs):
    inputs = 2 * count + 1
    groups = count
    weight_count = groups + 3
    sources, refs = refs[:inputs], refs[inputs:]
    weight_refs, refs = refs[: blocks + 3], refs[blocks + 3 :]
    outs = 3 if count == 2 else 2
    out_refs, held_refs, refs = refs[:outs], refs[outs : outs + weight_count], refs[outs + weight_count :]
    held, out_scr, sems = refs[:inputs], refs[inputs : inputs + outs], refs[inputs + outs]
    copies, started = fetch(sources, held, sems)
    w_outs, (w_gate, w_up, w_down) = held_refs[:groups], held_refs[groups:]
    hidden_width = w_gate.shape[1]
    chunks = [
        pl.ds(start, min(CHUNK, hidden_width - start)) for start in range(0, hidden_width, CHUNK)
    ]
    if blocks == groups:
        outs_in = [[copies.start(weight_refs[i], w_outs[i])] for i in range(groups)]
    else:
        outs_in = [
            [copies.start(weight_refs[0], w_outs[0])],
            start_pieces(copies, place_ref, weight_refs[1:blocks], w_outs[1]),
        ]
    weight_refs = weight_refs[blocks:]
    columns = [
        [
            copies.start(weight_refs[i].at[:, at], (w_gate, w_up)[i].at[:, at])
            for i in range(2)
        ]
        for at in chunks
    ]
    downs = [copies.start(weight_refs[2].at[at], w_down.at[at]) for at in chunks]
    copies.flying = []
    for copy in started:
        copy.wait()
    rows = in_order(place_ref, [ref[...] for ref in held[:count]]).astype(F32)
    width = rows.shape[1] // count
    mixed = None
    for i in range(groups):
        for copy in outs_in[i]:
            copy.wait()
        term = jnp.dot(held[count + i][...], w_outs[i][...], preferred_element_type=F32)
        term = term.astype(BF16).astype(F32)
        mixed = term if mixed is None else mixed + term
    residual = (rows + mixed).astype(BF16)
    normed = rms_norm(residual.astype(F32), held[2 * count][...])
    if count == 2:
        first = place_ref[0] == 0
        out_scr[2][...] = jnp.where(first, residual[:, :width], residual[:, width:])
        copies.start(out_scr[2], out_refs[2])
    else:
        out_scr[1][...] = residual
        copies.start(out_scr[1], out_refs[1])
    hidden = []
    for i, at in enumerate(chunks):
        columns[i][0].wait()
        columns[i][1].wait()
        gate_act = jnp.dot(normed, w_gate[:, at], preferred_element_type=F32)
        up_act = jnp.dot(normed, w_up[:, at], preferred_element_type=F32)
        hidden.append((gate_act / (1.0 + jnp.exp(-gate_act)) * up_act).astype(BF16))
    hidden = jnp.concatenate(hidden, axis=1)
    terms = apart(hidden, w_down, chunks[-1].start, downs).astype(BF16)
    if count == 2:
        out_scr[0][...] = jnp.where(first, terms[:, :width], terms[:, width:])
        out_scr[1][...] = jnp.where(first, terms[:, width:], terms[:, :width])
        copies.start(out_scr[0], out_refs[0])
        copies.start(out_scr[1], out_refs[1])
    else:
        out_scr[0][...] = terms
        copies.start(out_scr[0], out_refs[0])
    copies.wait()


def load_kernel(*refs):
    count = len(refs) // 2
    _, started = fetch(refs[:count], refs[count : 2 * count], refs[-1])
    for copy in started:
        copy.wait()


def load(limit, *arrays):
    return pl.pallas_call(
        load_kernel,
        in_specs=[ANY] * len(arrays),
        out_specs=[HELD] * len(arrays),
        out_shape=[jax.ShapeDtypeStruct(x.shape, x.dtype) for x in arrays],
        scratch_shapes=[pltpu.SemaphoreType.DMA((len(arrays),))],
        compiler_params=params(limit),
        cost_estimate=cost(0, sum(2 * x.size for x in arrays)),
        name="load",
    )(*arrays)


def start_pieces(copies, place_ref, pieces, target):
    rows = pieces[0].shape[0]
    odd = place_ref[1]
    starts = (2 * odd, 2 * odd + 1, 2 * (1 - odd), 2 * (1 - odd) + 1)
    return [
        copies.start(piece, target.at[pl.ds(start * rows, rows)])
        for piece, start in zip(pieces, starts)
    ]


def own_share_kernel(att_ref, w_out_ref, term_ref):
    term_ref[...] = jnp.dot(
        att_ref[...], w_out_ref[...], preferred_element_type=F32
    ).astype(BF16)


def tail_kernel(place_ref, *refs):
    w_gate, term_ref, *refs = refs
    sources, pieces, w_up_hbm, w_down_hbm = refs[:4], refs[4:8], refs[8], refs[9]
    send_ref, hidden_ref, residual_ref, *refs = refs[10:]
    held, (w_out_other, w_up, w_down, sems) = refs[:4], refs[4:]
    own_ref, other_ref, gain_ref, att_other_ref = held
    width = send_ref.shape[1]
    hidden_width = w_gate.shape[1]
    away = pl.ds(pl.multiple_of((1 - place_ref[0]) * width, width), width)
    copies, started = fetch(sources, held, sems)
    arriving = start_pieces(copies, place_ref, pieces, w_out_other)
    chunks = [
        pl.ds(start, min(CHUNK, hidden_width - start)) for start in range(0, hidden_width, CHUNK)
    ]
    ups = [copies.start(w_up_hbm.at[:, at], w_up.at[:, at]) for at in chunks]
    downs = [copies.start(w_down_hbm.at[at, away], w_down.at[at]) for at in chunks]
    for copy in started + arriving:
        copy.wait()
    mixed_other = jnp.dot(att_other_ref[...], w_out_other[...], preferred_element_type=F32)
    rows = in_order(place_ref, [own_ref[...], other_ref[...]]).astype(F32)
    mixed = term_ref[...].astype(F32) + mixed_other.astype(BF16).astype(F32)
    residual = (rows + mixed).astype(BF16)
    normed = rms_norm(residual.astype(F32), gain_ref[...])
    residual_ref[...] = jnp.where(place_ref[0] == 0, residual[:, :width], residual[:, width:])
    hidden = []
    for at, copy in zip(chunks, ups):
        gate_act = jnp.dot(normed, w_gate[:, at], preferred_element_type=F32)
        copy.wait()
        up_act = jnp.dot(normed, w_up[:, at], preferred_element_type=F32)
        hidden.append((gate_act / (1.0 + jnp.exp(-gate_act)) * up_act).astype(BF16))
    hidden = jnp.concatenate(hidden, axis=1)
    hidden_ref[...] = hidden
    send_ref[...] = apart(hidden, w_down, chunks[-1].start, downs).astype(BF16)


def keep_kernel(place_ref, hidden_ref, residual_ref, w_down_hbm, out_ref, w_down, sems):
    width = out_ref.shape[1]
    own = pl.ds(pl.multiple_of(place_ref[0] * width, width), width)
    copies = Copies(sems)
    copies.start(w_down_hbm.at[:, own], w_down)
    copies.wait()
    term = jnp.dot(hidden_ref[...], w_down[...], preferred_element_type=F32).astype(BF16)
    out_ref[...] = residual_ref[...].astype(F32) + term.astype(F32)


def tail(place, parts, attended, gain, w_outs, w_gate, w_up, w_down):
    attended, w_gate = lax.optimization_barrier((attended, w_gate))
    rows, width = parts[0].shape
    hidden = w_up.shape[1]
    held = load(TAIL_VMEM, w_gate)
    term = pl.pallas_call(
        own_share_kernel,
        in_specs=[HELD] * 2,
        out_specs=HELD,
        out_shape=jax.ShapeDtypeStruct((rows, 2 * width), BF16),
        compiler_params=params(TAIL_VMEM),
        cost_estimate=cost(4 * rows * width * attended.shape[1], 2 * w_outs[0].size),
        name="own_share",
    )(attended, w_outs[0])
    held = (*held, term)
    sources = (*parts, gain, swap(attended, 2)[1])
    half = jax.ShapeDtypeStruct((rows, width), BF16)
    units = jax.ShapeDtypeStruct((rows, hidden), BF16)
    half_down = pltpu.VMEM((hidden, width), BF16)
    send, units, residual = pl.pallas_call(
        tail_kernel,
        in_specs=[SCALAR, HELD, HELD] + [ANY] * (len(sources) + 6),
        out_specs=[HELD] * 3,
        out_shape=[half, units, half],
        scratch_shapes=scratch_like(*sources, w_outs[0], w_up)
        + [
            half_down,
            pltpu.SemaphoreType.DMA((8 + 2 * -(-hidden // CHUNK),)),
        ],
        compiler_params=params(TAIL_VMEM),
        cost_estimate=cost(10 * rows * width * hidden, 6 * width * hidden, rows * hidden),
        name="tail",
    )(place, *held, *sources, *w_outs[1:], w_up, w_down)
    kept = pl.pallas_call(
        keep_kernel,
        in_specs=[SCALAR] + [HELD] * 2 + [ANY],
        out_specs=HELD,
        out_shape=jax.ShapeDtypeStruct((rows, width), F32),
        scratch_shapes=[half_down, pltpu.SemaphoreType.DMA((1,))],
        compiler_params=params(TAIL_VMEM),
        cost_estimate=cost(2 * rows * width * hidden, 2 * width * hidden),
        name="keep",
    )(place, units, residual, w_down)
    other = lax.ppermute(send, "tensor", [(0, 1), (1, 0)])
    return (kept + other.astype(F32)).astype(BF16)


def swap(block, count):
    if count == 2:
        return [block, lax.ppermute(block, "tensor", [(0, 1), (1, 0)])]
    if count == 1:
        return [block]
    gathered = lax.all_gather(block, "tensor", axis=0, tiled=False)
    return [gathered[i] for i in range(count)]


def share_rows(block, count, replicas, after):
    if count != 2 or replicas % 2:
        return swap(block, count), after
    half = block.shape[0] // 2
    odd = lax.axis_index("replica") % 2
    mine = lax.dynamic_slice_in_dim(block, odd * half, half, axis=0)
    pieces = (mine[: half // 2], mine[half // 2 :])
    pieces, after = lax.optimization_barrier((pieces, after))
    return [lax.ppermute(piece, "tensor", [(0, 1), (1, 0)]) for piece in pieces], after


def pass_rows(fetched, replicas):
    return lax.ppermute(fetched, "replica", [(i, i ^ 1) for i in range(replicas)])


def finish(place, parts, attended, gain, w_outs, *weights):
    count = len(parts)
    rows = parts[0].shape[0]
    model = sum(part.shape[1] for part in parts)
    hidden = weights[-1].shape[0]
    width = model // count
    if count == 2:
        outs = [jax.ShapeDtypeStruct((rows, width), BF16)] * 3
    else:
        outs = [jax.ShapeDtypeStruct((rows, model), BF16)] * 2
    operands = (*parts, *attended, gain)
    copies = len(operands) + len(w_outs) + 3 * (-(-hidden // CHUNK)) + len(outs)
    held = [pltpu.VMEM(w.shape, w.dtype) for w in [w_outs[0]] * count + list(weights)]
    return pl.pallas_call(
        functools.partial(mlp_kernel, count, len(w_outs)),
        in_specs=[SCALAR] + [ANY] * (len(operands) + len(w_outs) + len(weights)),
        out_specs=[HBM] * len(outs),
        out_shape=outs,
        scratch_shapes=held
        + scratch_like(*operands, *outs)
        + [pltpu.SemaphoreType.DMA((copies,))],
        compiler_params=params(MLP_VMEM),
        cost_estimate=cost(FILL * 6 * rows * model * hidden, 6 * model * hidden, rows * hidden),
        name="mlp",
    )(place, *operands, *w_outs, *weights)


def exchange(terms, count):
    if count == 2:
        keep, send, residual = terms
        other = lax.ppermute(send, "tensor", [(0, 1), (1, 0)])
        summed = keep.astype(F32) + other.astype(F32)
        return (residual.astype(F32) + summed).astype(BF16)
    terms, residual = terms
    width = terms.shape[1] // count
    summed = lax.psum_scatter(terms.astype(F32), "tensor", scatter_dimension=1, tiled=True)
    own = lax.dynamic_slice_in_dim(residual, lax.axis_index("tensor") * width, width, axis=1)
    return (own.astype(F32) + summed).astype(BF16)


def body(
    prompt_rows,
    request_rows,
    request_keyval_cache,
    cache_len,
    destination,
    prefix_cache,
    attn_gain,
    w_query,
    keyval_weight,
    w_out,
    mlp_gain,
    w_gate,
    w_up,
    w_down,
):
    count = lax.axis_size("tensor")
    replicas = lax.axis_size("replica")
    place = jnp.stack((lax.axis_index("tensor"), lax.axis_index("replica") % 2)).astype(jnp.int32)
    requests = request_rows.shape[0]
    prompts = prompt_rows.shape[0]
    model = w_query.shape[0]
    width = w_query.shape[1]
    kv_width = keyval_weight.shape[1]
    heads = width // HEAD_SIZE
    prefix_len = prefix_cache.shape[0]
    attn_gain = attn_gain.reshape(1, model)
    mlp_gain = mlp_gain.reshape(1, model)

    request_parts = swap(request_rows, count)

    per_peer = 2 * requests // replicas
    slots = replicas * per_peer
    target = destination.reshape(1, requests)
    cached = request_keyval_cache.shape[1]
    w_outs, prompt_rows = share_rows(w_out, count, replicas, prompt_rows)
    prompt_parts = swap(prompt_rows, count)
    operands = (target, attn_gain, *request_parts)
    slot_rows = jax.ShapeDtypeStruct((slots, width), BF16)
    send = pl.pallas_call(
        functools.partial(request_kernel, count, per_peer),
        in_specs=[SCALAR, HELD] + [ANY] * len(operands),
        out_specs=HBM,
        out_shape=slot_rows,
        scratch_shapes=scratch_like(*operands, slot_rows)
        + [pltpu.SemaphoreType.DMA((len(operands) + 2,))],
        compiler_params=params(REQUEST_VMEM),
        cost_estimate=cost(0, 0),
        name="request_project",
    )(place, *load(REQUEST_VMEM, w_query), *operands)

    slot_queries = lax.all_to_all(send, "replica", split_axis=0, concat_axis=0, tiled=True)

    operands = (
        *prompt_parts,
        *request_parts,
        attn_gain,
        w_query,
        keyval_weight,
        prefix_cache,
        cache_len.reshape(1, requests),
        request_keyval_cache,
    )
    outs = [
        jax.ShapeDtypeStruct((prompts, width), BF16),
        jax.ShapeDtypeStruct((requests, width + PAIR), F32),
    ]
    blocks = (requests // GROUP, heads * GROUP)
    prompt_attended, past = pl.pallas_call(
        functools.partial(prompt_kernel, count),
        in_specs=[SCALAR] + [ANY] * len(operands),
        out_specs=[HBM] * 2,
        out_shape=outs,
        scratch_shapes=scratch_like(*operands)
        + [
            pltpu.VMEM((heads, prompts, PAIR), BF16),
            pltpu.VMEM((prefix_len, kv_width), BF16),
        ]
        + scratch_like(*outs)
        + [
            pltpu.VMEM((*blocks, kv_width), F32),
            pltpu.VMEM((*blocks, GROUP * cached), F32),
            pltpu.VMEM((*blocks, GROUP * cached), BF16),
            pltpu.VMEM((*blocks, kv_width), F32),
            pltpu.SemaphoreType.DMA((len(operands) + 2,)),
        ],
        compiler_params=params(PROMPT_VMEM),
        cost_estimate=cost(
            FILL * (2 * prompts * model * (width + kv_width)) + 4 * prompts * heads * prefix_len * PAIR,
            2 * model * (width + kv_width) + 2 * prefix_len * kv_width,
            prompts * heads * prefix_len,
        ),
        name="prompt_attention",
    )(place, *operands)

    prompt_attended = swap(prompt_attended, count)
    slot_queries, prompt_attended[0], w_outs[0] = lax.optimization_barrier(
        (slot_queries, prompt_attended[0], w_outs[0])
    )
    passed = [pass_rows(w_outs[0], replicas)] if count == 2 else []
    slot_out = pl.pallas_call(
        slot_kernel,
        in_specs=[HELD] * 2,
        out_specs=HBM,
        out_shape=jax.ShapeDtypeStruct((slots, width + PAIR), BF16),
        scratch_shapes=[
            pltpu.VMEM((slots, width + PAIR), BF16),
            pltpu.VMEM((prefix_len, kv_width), BF16),
            pltpu.SemaphoreType.DMA((1 + heads // 2,)),
        ],
        compiler_params=params(SLOT_VMEM),
        cost_estimate=cost(
            4 * slots * heads * prefix_len * PAIR,
            2 * prefix_len * kv_width,
            slots * heads * prefix_len,
        ),
        name="slot_attention",
    )(slot_queries, prefix_cache)

    slot_out, w_outs = lax.optimization_barrier((slot_out, w_outs))
    if count == 2:
        w_outs = [w_out, *w_outs, *passed, pass_rows(w_outs[1], replicas)]
    back = lax.all_to_all(slot_out, "replica", split_axis=0, concat_axis=0, tiled=True)

    weights = (mlp_gain, w_outs, w_gate, w_up, w_down)
    prompt_terms = finish(place, prompt_parts, prompt_attended, *weights)
    back, prompt_terms = lax.optimization_barrier((back, prompt_terms))
    operands = (target, back, past)
    request_attended = pl.pallas_call(
        functools.partial(merge_kernel, per_peer),
        in_specs=[HELD] * len(operands),
        out_specs=HELD,
        out_shape=jax.ShapeDtypeStruct((requests, width), BF16),
        compiler_params=params(MERGE_VMEM),
        cost_estimate=cost(4 * requests * slots * width, 4 * slots * width),
        name="merge",
    )(*operands)

    if count == 2:
        request_out = tail(place, request_parts, request_attended, *weights)
    else:
        request_out = exchange(
            finish(place, request_parts, swap(request_attended, count), *weights), count
        )
    return (exchange(prompt_terms, count), request_out)


def solution(mesh):
    return jax.shard_map(
        body,
        mesh=mesh,
        in_specs=(
            P("replica", "tensor"),
            P("replica", "tensor"),
            P("replica", None, "tensor"),
            P("replica"),
            P("replica", None),
            P("replica", "tensor"),
            P(),
            P(None, "tensor"),
            P(None, "tensor"),
            P("tensor", None),
            P(),
            P(None, "tensor"),
            P(None, "tensor"),
            P("tensor", None),
        ),
        out_specs=(P("replica", "tensor"), P("replica", "tensor")),
        check_vma=False,
    )
```
